128 devices in a mesh: dp: 64 (over z, x, y), tensor: 2 (over core).
Axes of the slice: x: 4, y: 4, z: 4, core: 2. Of those that a mesh axis runs over, the one named last changes fastest.
Arguments:
- tokens: bfloat16 [32768, 1536], P('dp'), may hold values from -6 to 6
- seq_lengths: int32 [64, 4], P('dp'), may hold values from 0 to 512, as said below
- norm_in: float32 [1536], replicated, may hold values from 0.5 to 1.5
- proj_gate: bfloat16 [1536, 3072], P(None, 'tensor'), may hold values from -0.15625 to 0.15625
- proj_inner: bfloat16 [1536, 3072], P(None, 'tensor'), may hold values from -0.15625 to 0.15625
- proj_state: bfloat16 [1536, 256], replicated, may hold values from -0.15625 to 0.15625
- proj_step: bfloat16 [1536, 48], P(None, 'tensor'), may hold values from -0.15625 to 0.15625
- conv_inner: float32 [4, 3072], P(None, 'tensor'), may hold values from -3 to 3
- bias_inner: float32 [3072], P('tensor'), may hold values from -3 to 3
- conv_state: float32 [4, 256], replicated, may hold values from -3 to 3
- bias_state: float32 [256], replicated, may hold values from -3 to 3
- step_bias: float32 [48], P('tensor'), may hold values from -3 to -1.5
- decay_log: float32 [48], P('tensor'), may hold values from -3.9 to 0
- skip_gain: float32 [48], P('tensor'), may hold values from 0.5 to 2
- norm_out: float32 [3072], P('tensor'), may hold values from 0.5 to 1.5
- proj_out: bfloat16 [3072, 1536], P('tensor'), may hold values from -0.109375 to 0.109375
- cotangent: bfloat16 [32768, 1536], P('dp'), may hold values from -6 to 6
Outputs:
- block_out: bfloat16 [32768, 1536], P('dp')
- grad_tokens: bfloat16 [32768, 1536], P('dp')
- grad_norm_in: float32 [1536], replicated
- grad_proj_gate: float32 [1536, 3072], P('dp', 'tensor')
- grad_proj_inner: float32 [1536, 3072], P('dp', 'tensor')
- grad_proj_state: float32 [1536, 256], P('dp', 'tensor')
- grad_proj_step: float32 [1536, 48], P('dp', 'tensor')
- grad_conv_inner: float32 [4, 3072], P(None, 'tensor')
- grad_bias_inner: float32 [3072], P('tensor')
- grad_conv_state: float32 [4, 256], P(None, 'tensor')
- grad_bias_state: float32 [256], P('tensor')
- grad_step_bias: float32 [48], P('tensor')
- grad_decay_log: float32 [48], P('tensor')
- grad_skip_gain: float32 [48], P('tensor')
- grad_norm_out: float32 [3072], P('tensor')
- grad_proj_out: float32 [3072, 1536], P('tensor', 'dp')
The draws below stay inside these ranges and needn't reach their ends.
Inputs may be any that keep to these rules, and one draw needn't show every extreme that they name: `seq_lengths`: row d lists the lengths of the sequences packed in order, from the first row, into the 512 rows of data index d; a row sums to at most 512, a zero is an empty slot, rows past the sum are padding; in every draw one data index holds a single sequence of 512 rows.
All inputs are finite; a program needn't handle non-finite values.
Results may differ from the reference program's by a relative error of at most 0.012.
The reference program's roundings to bfloat16 on the way count: a program that leaves them out, or rounds other values in their place, can miss the bound.
Values sent between devices are 32-bit elements; how exact they have to be, the bound alone decides.
No kernel may reach another device: no remote copies, remote signals or barrier semaphores. Data moves between devices by JAX's collectives and lax.ppermute only.
A program may use at most 128 MiB of HBM per device.

```python
import jax
import jax.numpy as jnp
from jax import lax

WIDTH = 1536
HEADS = 48
HEAD_DIM = 64
STATE = 128
KERNEL = 4
ROWS = 512
SLOTS = 4
INNER = 3072
TOKENS = 32768
N_DP = 64


def draw_seq_lengths(key, part):
    key = jax.random.fold_in(key, 17)
    key_used, key_cuts, key_full = jax.random.split(key, 3)
    devices = jnp.arange(N_DP, dtype=jnp.int32)
    full_device = jax.random.randint(key_full, (), 0, N_DP)
    used_rows = jax.random.randint(key_used, (N_DP,), ROWS // 4, ROWS + 1)
    cut_points = jnp.sort(jax.random.randint(key_cuts, (N_DP, SLOTS - 1), 0, ROWS + 1), axis=1)
    scaled = cut_points * used_rows[:, None] // ROWS
    edge_rows = jnp.concatenate([jnp.zeros((N_DP, 1), jnp.int32), scaled.astype(jnp.int32), used_rows[:, None].astype(jnp.int32)], axis=1)
    lengths = edge_rows[:, 1:] - edge_rows[:, :-1]
    single = jnp.zeros((SLOTS,), jnp.int32).at[0].set(ROWS)
    lengths = jnp.where((devices == full_device)[:, None], single[None, :], lengths)
    return lengths.astype(jnp.int32)


def shard_levels(rng, shape, cuts, low, top_value):
    gain, own = 1.0, jax.random.fold_in(rng, 6)
    for dim, parts in cuts:
        steps = jnp.exp(jax.random.uniform(jax.random.fold_in(own, dim), (parts,), jnp.float32, low / len(cuts), top_value / len(cuts)))
        gain = gain * jnp.repeat(steps, shape[dim] // parts).reshape([-1 if axis == dim else 1 for axis in range(len(shape))])
    return gain


def centred(stream_key, shape, deviation, most, cuts=(), kind=jnp.bfloat16):
    level = shard_levels(stream_key, shape, cuts, -0.22, 0.18) if cuts else 1.0
    values = jax.random.normal(stream_key, shape, jnp.float32) * deviation * level
    return jnp.minimum(jnp.maximum(values, -most), most).astype(kind)


def setup_inputs(seed: int = 0) -> dict:
    streams_of = jax.random.split(jax.random.key(seed), 18)
    tokens = centred(streams_of[0], (TOKENS, WIDTH), 1.0, 6.0, ((0, 64),))
    seq_lengths = draw_seq_lengths(jax.random.fold_in(streams_of[17], 71), 0)
    norm_in = jnp.clip(1.0 + 0.1 * jax.random.normal(streams_of[2], (WIDTH,), jnp.float32), 0.5, 1.5)
    proj_gate = centred(streams_of[3], (WIDTH, INNER), WIDTH ** -0.5, 0.15625, ((1, 2),))
    proj_inner = centred(streams_of[4], (WIDTH, INNER), WIDTH ** -0.5, 0.15625, ((1, 2),))
    proj_state = centred(streams_of[5], (WIDTH, 2 * STATE), WIDTH ** -0.5, 0.15625)
    proj_step = centred(streams_of[6], (WIDTH, HEADS), WIDTH ** -0.5, 0.15625, ((1, 2),))
    conv_inner = centred(streams_of[7], (KERNEL, INNER), KERNEL ** -0.5, 3.0, ((1, 2),), jnp.float32)
    bias_inner = centred(streams_of[8], (INNER,), 0.5, 3.0, ((0, 2),), jnp.float32)
    conv_state = centred(streams_of[9], (KERNEL, 2 * STATE), KERNEL ** -0.5, 3.0, (), jnp.float32)
    bias_state = centred(streams_of[10], (2 * STATE,), 0.5, 3.0, (), jnp.float32)
    step_bias = jnp.clip(-3.0 + 1.5 * jax.random.uniform(streams_of[11], (HEADS,), jnp.float32) ** shard_levels(streams_of[11], (HEADS,), ((0, 2),), -0.2, 0.2), -3.0, -1.5)
    decay_log = jnp.clip(-3.9 + 3.9 * jax.random.uniform(streams_of[12], (HEADS,), jnp.float32) ** shard_levels(streams_of[12], (HEADS,), ((0, 2),), -0.2, 0.2), -3.9, 0.0)
    skip_gain = jnp.clip(0.5 + 1.5 * jax.random.uniform(streams_of[13], (HEADS,), jnp.float32) ** shard_levels(streams_of[13], (HEADS,), ((0, 2),), -0.2, 0.2), 0.5, 2.0)
    norm_out = jnp.clip(1.0 + 0.1 * jax.random.normal(streams_of[14], (INNER,), jnp.float32), 0.5, 1.5)
    proj_out = centred(streams_of[15], (INNER, WIDTH), INNER ** -0.5, 0.109375, ((0, 2),))
    cotangent = centred(streams_of[16], (TOKENS, WIDTH), 1.0, 6.0, ((0, 64),))
    return dict(tokens=tokens, seq_lengths=seq_lengths, norm_in=norm_in, proj_gate=proj_gate, proj_inner=proj_inner, proj_state=proj_state, proj_step=proj_step, conv_inner=conv_inner, bias_inner=bias_inner, conv_state=conv_state, bias_state=bias_state, step_bias=step_bias, decay_log=decay_log, skip_gain=skip_gain, norm_out=norm_out, proj_out=proj_out, cotangent=cotangent)


@jax.custom_vjp
def low(v):
    return lax.optimization_barrier(v.astype(jnp.bfloat16)).astype(jnp.float32)

@jax.custom_vjp
def low_back(v):
    return v

def low_keep(v):
    return (low(v), None)

def low_pass(kept, grad):
    return (grad,)

def back_keep(v):
    return (v, None)

def back_low(kept, grad):
    return (low(grad),)
low.defvjp(low_keep, low_pass)
low_back.defvjp(back_keep, back_low)
EPS = 1e-05
HIGH = lax.Precision.HIGHEST

def matmul_high(left, right):
    return jnp.dot(left, right, precision=HIGH, preferred_element_type=jnp.float32)

def segment_rows(lengths, row_count):
    seq_ends = jnp.cumsum(lengths).astype(jnp.int32)
    positions = jnp.arange(row_count, dtype=jnp.int32)
    segment = lax.optimization_barrier(jnp.sum((positions[:, None] >= seq_ends[None, :]).astype(jnp.int32), axis=1)).astype(jnp.int32)
    valid_rows = (positions < seq_ends[-1]).astype(jnp.float32)
    return (segment, valid_rows)

def lag_mask(segment, offset):
    same_seq = (segment[offset:] == segment[:-offset]).astype(jnp.float32)
    return jnp.concatenate([jnp.zeros((offset,), jnp.float32), same_seq])

def shift_down(values, offset):
    return jnp.concatenate([jnp.zeros((offset, values.shape[1]), values.dtype), values[:-offset]], axis=0)

def causal_conv(values, weight, bias, segment):
    total = bias[None, :] + weight[0][None, :] * values
    for offset in range(1, weight.shape[0]):
        keep = lag_mask(segment, offset)
        total = total + weight[offset][None, :] * shift_down(values, offset) * keep[:, None]
    return total

def state_mix(values, step_size, decay_rate, input_map, output_map, segment):
    row_count = values.shape[0]
    positions = jnp.arange(row_count, dtype=jnp.int32)
    causal = ((positions[:, None] >= positions[None, :]) & (segment[:, None] == segment[None, :])).astype(jnp.float32)
    cumulative = jnp.cumsum(step_size * decay_rate[None, :], axis=0)
    log_gap = cumulative[:, None, :] - cumulative[None, :, :]
    kernel = jnp.exp(jnp.where(causal[:, :, None] > 0, log_gap, 0.0)) * causal[:, :, None]
    scores = matmul_high(low(output_map), low(input_map).T)
    weights = low(scores[:, :, None] * kernel * step_size[None, :, :])
    return low_back(jnp.einsum('ijh,jhp->ihp', weights, low(values), precision=HIGH))

def layer_block(tokens, lengths, norm_in, proj_gate, proj_inner, proj_state, proj_step, conv_inner, bias_inner, conv_state, bias_state, step_bias, decay_log, skip_gain, norm_out, proj_out):
    row_count = tokens.shape[0]
    segment, valid_rows = segment_rows(lengths, row_count)
    rstd_in = lax.rsqrt(lax.optimization_barrier(jnp.mean(tokens * tokens, axis=1, keepdims=True)) + EPS)
    normed = low(tokens * rstd_in * norm_in[None, :])
    gate_raw = low_back(matmul_high(normed, proj_gate))
    inner_raw = low_back(matmul_high(normed, proj_inner))
    state_raw = low_back(matmul_high(normed, proj_state))
    step_raw = low_back(matmul_high(normed, proj_step))
    xconv = jax.nn.silu(causal_conv(inner_raw, conv_inner, bias_inner, segment))
    stateconv = jax.nn.silu(causal_conv(state_raw, conv_state, bias_state, segment))
    step_size = jax.nn.softplus(step_raw + step_bias[None, :])
    decay_rate = -jnp.exp(decay_log)
    head_values = xconv.reshape(row_count, HEADS, HEAD_DIM)
    mixed = state_mix(head_values, step_size, decay_rate, stateconv[:, :STATE], stateconv[:, STATE:], segment)
    mixed = mixed + skip_gain[None, :, None] * head_values
    gated = mixed.reshape(row_count, INNER) * jax.nn.silu(gate_raw)
    rstd_out = lax.rsqrt(lax.optimization_barrier(jnp.mean(gated * gated, axis=1, keepdims=True)) + EPS)
    projected = low_back(matmul_high(low(gated * norm_out[None, :]), proj_out))
    return tokens + valid_rows[:, None] * rstd_out * projected

def reference(tokens, seq_lengths, norm_in, proj_gate, proj_inner, proj_state, proj_step, conv_inner, bias_inner, conv_state, bias_state, step_bias, decay_log, skip_gain, norm_out, proj_out, cotangent):
    weights = tuple((argument.astype(jnp.float32) for argument in (norm_in, proj_gate, proj_inner, proj_state, proj_step, conv_inner, bias_inner, conv_state, bias_state, step_bias, decay_log, skip_gain, norm_out, proj_out)))
    blocks = tokens.astype(jnp.float32).reshape(N_DP, ROWS, WIDTH)

    def forward(blocks, *weights):

        def one_block(block_pair):
            return layer_block(block_pair[0], block_pair[1], *weights)
        return lax.map(jax.checkpoint(one_block), (blocks, seq_lengths))
    result, pullback = jax.vjp(forward, blocks, *weights)
    gradients = pullback(cotangent.astype(jnp.float32).reshape(N_DP, ROWS, WIDTH))
    block_out = result.reshape(N_DP * ROWS, WIDTH).astype(jnp.bfloat16)
    grad_tokens = gradients[0].reshape(N_DP * ROWS, WIDTH).astype(jnp.bfloat16)
    return (block_out, grad_tokens, gradients[1], gradients[2], gradients[3], gradients[4], gradients[5], gradients[6], gradients[7], gradients[8], gradients[9], gradients[10], gradients[11], gradients[12], gradients[13], gradients[14])
```

```python
import functools

import jax
import jax.numpy as jnp
from jax import lax
from jax.experimental import pallas as pl
from jax.experimental.pallas import tpu as pltpu
from jax.sharding import PartitionSpec as P

EPS = 1e-05
HIGH = lax.Precision.HIGHEST


FLOWS = 3
DIMS = 6
BLOCKS = 64


def chip_bits(index):
    bits = []
    for place in (4, 2, 0):
        coord = (index >> place) & 3
        bits += [(coord ^ (coord >> 1)) & 1, coord >> 1]
    return bits


def partner(index, dim):
    place = (4, 2, 0)[dim // 2]
    return index ^ ((3 if dim % 2 else 1) << place)


def flow_dim(core, flow, step):
    return (core * FLOWS + flow + step) % DIMS


def flow_pairs(flow, step):
    return [
        (2 * index + core, 2 * partner(index, flow_dim(core, flow, step)) + core)
        for index in range(BLOCKS)
        for core in range(2)
    ]


def swap_tensor(values):
    return lax.ppermute(values, "tensor", [(0, 1), (1, 0)])


def block_places():
    mine = chip_bits(lax.axis_index("dp"))
    core = lax.axis_index("tensor")
    every = chip_bits(jnp.arange(BLOCKS, dtype=jnp.int32))
    differ = [one ^ other for one, other in zip(mine, every)]
    places = []
    for flow in range(FLOWS):
        by_core = []
        for which in range(2):
            place = jnp.zeros((BLOCKS,), jnp.int32)
            for step in range(DIMS):
                place = place * 2 + differ[flow_dim(which, flow, step)]
            by_core.append(place)
        places.append(jnp.where(core == 0, by_core[0], by_core[1]))
    return jnp.stack(places)


def weight_grad_kernel(places, left, right, keep, send, held, sems):
    flow = pl.program_id(0)
    slot = lax.rem(flow, 2)
    rows = left.shape[0]
    per = rows // BLOCKS
    half = rows // 2

    def copies(which, at):
        return (
            pltpu.make_async_copy(held.at[at, pl.ds(0, half)], keep.at[which], sems.at[at, 0]),
            pltpu.make_async_copy(held.at[at, pl.ds(half, half)], send.at[which], sems.at[at, 1]),
        )

    @pl.when(flow >= 2)
    def _():
        for copy in copies(flow - 2, slot):
            copy.wait()

    chunk = 16
    for first in range(0, BLOCKS, chunk):
        part = jnp.dot(
            left[first * per : (first + chunk) * per, :],
            right[...],
            preferred_element_type=jnp.float32,
        )
        for block in range(chunk):
            place = places[flow, first + block]
            held[slot, pl.ds(pl.multiple_of(place * per, 8), per), :] = part[
                block * per : (block + 1) * per
            ]
    for copy in copies(flow, slot):
        copy.start()

    @pl.when(flow == FLOWS - 1)
    def _():
        for copy in copies(flow - 1, 1 - slot):
            copy.wait()
        for copy in copies(flow, slot):
            copy.wait()


def weight_grad(places, left, right):
    rows, depth = left.shape
    cols = right.shape[1] // FLOWS
    half = jax.ShapeDtypeStruct((FLOWS, rows // 2, cols), jnp.float32)
    return pl.pallas_call(
        weight_grad_kernel,
        grid=(FLOWS,),
        in_specs=[
            pl.BlockSpec(memory_space=pltpu.SMEM),
            pl.BlockSpec((rows, depth), lambda flow: (0, 0)),
            pl.BlockSpec((depth, cols), lambda flow: (0, flow)),
        ],
        out_specs=[pl.BlockSpec(memory_space=pl.ANY), pl.BlockSpec(memory_space=pl.ANY)],
        out_shape=[half, half],
        scratch_shapes=[
            pltpu.VMEM((2, rows, cols), jnp.float32),
            pltpu.SemaphoreType.DMA((2, 2)),
        ],
        compiler_params=pltpu.CompilerParams(vmem_limit_bytes=32 * 1024 * 1024),
        cost_estimate=pl.CostEstimate(
            flops=2 * rows * depth * cols * FLOWS,
            bytes_accessed=4 * rows * cols * FLOWS + 2 * depth * (rows + cols * FLOWS),
            transcendentals=0,
        ),
    )(places, left, right)


def halve(kept, got, step):
    stay, go = [], []
    for one, other in zip(kept, got):
        rows = one.shape[0] // 2
        stay.append(one[:rows] + other[:rows])
        go.append(one[rows:] + other[rows:])
    return stay, go


def pass_on(parts, step):
    return [
        lax.ppermute(part, ("dp", "tensor"), flow_pairs(flow, step))
        for flow, part in enumerate(parts)
    ]


def reduce_flows(kept, sent, first, last):
    for step in range(first, last):
        got = pass_on(sent, step)
        if step == DIMS - 1:
            return [one + other for one, other in zip(kept, got)], None
        kept, sent = halve(kept, got, step)
    return kept, sent


def sum_over_dp(values):
    for dim in range(DIMS):
        pairs = [(index, partner(index, dim)) for index in range(BLOCKS)]
        values = values + lax.ppermute(values, "dp", pairs)
    return values


def dot_first(left, right, precision=None):
    return lax.dot_general(
        left,
        right,
        (((0,), (0,)), ((), ())),
        precision=precision,
        preferred_element_type=jnp.float32,
    )


def dot_last(left, right, precision=None):
    return lax.dot_general(
        left,
        right,
        (((1,), (1,)), ((), ())),
        precision=precision,
        preferred_element_type=jnp.float32,
    )


def segment_rows(lengths, row_count):
    seq_ends = jnp.cumsum(lengths)
    positions = jnp.arange(row_count, dtype=jnp.int32)
    segment = jnp.sum((positions[:, None] >= seq_ends[None, :]).astype(jnp.int32), axis=1)
    valid_rows = (positions < seq_ends[-1]).astype(jnp.float32)
    return (segment, valid_rows)


def lag_mask(segment, offset):
    same_seq = (segment[offset:] == segment[:-offset]).astype(jnp.float32)
    return jnp.concatenate([jnp.zeros((offset,), jnp.float32), same_seq])


def shift_down(values, offset):
    return jnp.concatenate(
        [jnp.zeros((offset, values.shape[1]), values.dtype), values[:-offset]], axis=0
    )


def shift_upward(values, offset):
    return jnp.concatenate(
        [values[offset:], jnp.zeros((offset, values.shape[1]), values.dtype)], axis=0
    )


def causal_conv(values, weight, bias, segment):
    total = bias[None, :] + weight[0][None, :] * values
    for offset in range(1, weight.shape[0]):
        keep = lag_mask(segment, offset)
        total = total + weight[offset][None, :] * shift_down(values, offset) * keep[:, None]
    return total


def conv_backward(grad_pre, values, weight, segment):
    tap_grads = [jnp.sum(grad_pre * values, axis=0)]
    grad_values = grad_pre * weight[0][None, :]
    for offset in range(1, weight.shape[0]):
        keep = lag_mask(segment, offset)[:, None]
        tap_grads.append(jnp.sum(grad_pre * shift_down(values, offset) * keep, axis=0))
        grad_values = grad_values + shift_upward(grad_pre * keep, offset) * weight[offset][None, :]
    return (jnp.stack(tap_grads), jnp.sum(grad_pre, axis=0), grad_values)


def silu_slope(values):
    sigma = jax.nn.sigmoid(values)
    return sigma * (1.0 + values * (1.0 - sigma))


def local(
    tokens,
    seq_lengths,
    norm_in,
    proj_gate,
    proj_inner,
    proj_state,
    proj_step,
    conv_inner,
    bias_inner,
    conv_state,
    bias_state,
    step_bias,
    decay_log,
    skip_gain,
    norm_out,
    proj_out,
    cotangent,
):
    row_count = tokens.shape[0]
    heads_local = proj_step.shape[1]
    inner_local = proj_inner.shape[1]
    head_size = inner_local // heads_local
    state_size = proj_state.shape[1] // 2
    tensor_count = lax.axis_size("tensor")
    inner_total = inner_local * tensor_count
    segment, valid_rows = segment_rows(seq_lengths[0], row_count)
    positions = jnp.arange(row_count, dtype=jnp.int32)
    causal = (
        (positions[:, None] >= positions[None, :]) & (segment[:, None] == segment[None, :])
    ).astype(jnp.float32)
    hidden = tokens.astype(jnp.float32)
    rstd_in = lax.rsqrt(jnp.mean(hidden * hidden, axis=1, keepdims=True) + EPS)
    normed = (hidden * rstd_in * norm_in[None, :]).astype(jnp.bfloat16)
    gate_raw = jnp.dot(normed, proj_gate, preferred_element_type=jnp.float32)
    inner_raw = jnp.dot(normed, proj_inner, preferred_element_type=jnp.float32)
    state_raw = jnp.dot(normed, proj_state, preferred_element_type=jnp.float32)
    step_raw = jnp.dot(normed, proj_step, preferred_element_type=jnp.float32)
    inner_pre = causal_conv(inner_raw, conv_inner, bias_inner, segment)
    xconv = jax.nn.silu(inner_pre)
    state_pre = causal_conv(state_raw, conv_state, bias_state, segment)
    stateconv = jax.nn.silu(state_pre)
    step_pre = step_raw + step_bias[None, :]
    step_size = jax.nn.softplus(step_pre)
    decay_rate = -jnp.exp(decay_log)
    cumulative = jnp.cumsum(step_size * decay_rate[None, :], axis=0)
    input_map = stateconv[:, :state_size].astype(jnp.bfloat16)
    output_map = stateconv[:, state_size:].astype(jnp.bfloat16)
    scores = dot_last(output_map, input_map)
    head_values = (
        xconv.astype(jnp.bfloat16).reshape(row_count, heads_local, head_size).transpose(1, 0, 2)
    )

    def head_kernel(cum_head):
        log_gap = cum_head[:, None] - cum_head[None, :]
        return jnp.exp(jnp.where(causal > 0, log_gap, 0.0)) * causal

    def head_forward(pack):
        values, cum_head, step_head = pack
        weights = (scores * head_kernel(cum_head) * step_head[None, :]).astype(jnp.bfloat16)
        return jnp.dot(weights, values, preferred_element_type=jnp.float32)

    head_packs = (head_values, cumulative.T, step_size.T)
    ssd_out = lax.map(head_forward, head_packs)
    skip_wide = jnp.repeat(skip_gain, head_size)
    mixed = ssd_out.transpose(1, 0, 2).reshape(row_count, inner_local) + skip_wide[None, :] * xconv
    gate_act = jax.nn.silu(gate_raw)
    gated = mixed * gate_act
    local_square = jnp.sum(gated * gated, axis=1)
    square_total = local_square + swap_tensor(local_square)
    scaled_in = (gated * norm_out[None, :]).astype(jnp.bfloat16)
    partial_value = jnp.dot(scaled_in, proj_out, preferred_element_type=jnp.float32)
    projected = partial_value + swap_tensor(partial_value)
    rstd_out = lax.rsqrt(square_total / inner_total + EPS)[:, None]
    block_out = (hidden + valid_rows[:, None] * rstd_out * projected).astype(jnp.bfloat16)
    grad_out = cotangent.astype(jnp.float32)
    masked = valid_rows[:, None] * grad_out
    grad_projected = (rstd_out * masked).astype(jnp.bfloat16)
    grad_rstd = jnp.sum(masked * projected, axis=1, keepdims=True)
    places = block_places()
    out_keep, out_send = weight_grad(places, grad_projected.T, scaled_in)
    out_flows = reduce_flows(list(out_keep), list(out_send), 0, 2)
    grad_scaled = dot_last(grad_projected, proj_out)
    grad_norm_out = jnp.sum(grad_scaled * gated, axis=0)
    grad_gated = grad_scaled * norm_out[None, :] - grad_rstd * rstd_out**3 / inner_total * gated
    grad_mixed = grad_gated * gate_act
    grad_gate = (grad_gated * mixed * silu_slope(gate_raw)).astype(jnp.bfloat16)
    normed_t = normed.T
    gate_keep, gate_send = weight_grad(places, normed_t, grad_gate)
    gate_flows = reduce_flows(list(gate_keep), list(gate_send), 0, 2)
    grad_skip_gain = jnp.sum(
        (grad_mixed * xconv).reshape(row_count, heads_local, head_size), axis=(0, 2)
    )
    grad_xconv = grad_mixed * skip_wide[None, :]
    grad_heads = (
        grad_mixed.astype(jnp.bfloat16)
        .reshape(row_count, heads_local, head_size)
        .transpose(1, 0, 2)
    )

    def head_backward(grad_scores, pack):
        values, cum_head, step_head, grad_head = pack
        kernel = head_kernel(cum_head)
        weights = (scores * kernel * step_head[None, :]).astype(jnp.bfloat16)
        grad_values = dot_first(weights, grad_head)
        grad_mix = dot_last(grad_head, values)
        shared = grad_mix * kernel
        grad_scores = grad_scores + shared * step_head[None, :]
        both = shared * scores
        flow = both * step_head[None, :]
        return (
            grad_scores,
            (grad_values, jnp.sum(both, axis=0), jnp.sum(flow, axis=1) - jnp.sum(flow, axis=0)),
        )

    grad_scores, (grad_values, grad_step_ssd, grad_cum) = lax.scan(
        head_backward, jnp.zeros((row_count, row_count), jnp.float32), head_packs + (grad_heads,)
    )
    grad_rate = jnp.cumsum(grad_cum[:, ::-1], axis=1)[:, ::-1].T
    grad_decay_log = jnp.sum(grad_rate * step_size, axis=0) * decay_rate
    grad_step = grad_step_ssd.T + grad_rate * decay_rate[None, :]
    grad_step_pre = grad_step * jax.nn.sigmoid(step_pre)
    grad_step_bias = jnp.sum(grad_step_pre, axis=0)
    grad_step_raw = grad_step_pre.astype(jnp.bfloat16)
    grad_xconv = grad_xconv + grad_values.transpose(1, 0, 2).reshape(row_count, inner_local)
    grad_conv_inner, grad_bias_inner, grad_inner_raw = conv_backward(
        grad_xconv * silu_slope(inner_pre), inner_raw, conv_inner, segment
    )
    grad_inner_raw = grad_inner_raw.astype(jnp.bfloat16)
    grad_output_map = jnp.dot(
        grad_scores,
        input_map.astype(jnp.float32),
        precision=HIGH,
        preferred_element_type=jnp.float32,
    )
    grad_input_map = dot_first(grad_scores, output_map.astype(jnp.float32), HIGH)
    grad_stateconv = jnp.concatenate([grad_input_map, grad_output_map], axis=1)
    grad_stateconv = grad_stateconv + swap_tensor(grad_stateconv)
    grad_conv_full, grad_bias_full, grad_state_raw = conv_backward(
        grad_stateconv * silu_slope(state_pre), state_raw, conv_state, segment
    )
    share_cols = 2 * state_size // tensor_count
    col_start = lax.axis_index("tensor") * share_cols
    grad_state_part = lax.dynamic_slice_in_dim(grad_state_raw, col_start, share_cols, 1).astype(
        jnp.bfloat16
    )
    proj_state_part = lax.dynamic_slice_in_dim(proj_state, col_start, share_cols, 1)
    grad_conv_state = lax.dynamic_slice_in_dim(grad_conv_full, col_start, share_cols, 1)
    grad_bias_state = lax.dynamic_slice_in_dim(grad_bias_full, col_start, share_cols, 0)
    grad_normed = dot_last(grad_gate, proj_gate) + dot_last(grad_inner_raw, proj_inner)
    grad_normed = (
        grad_normed
        + dot_last(grad_step_raw, proj_step)
        + dot_last(grad_state_part, proj_state_part)
    )
    grad_normed = grad_normed + swap_tensor(grad_normed)
    flow_cols = inner_local // FLOWS
    extra = jnp.zeros((row_count, 128), jnp.bfloat16)
    extras = [grad_state_part, extra.at[:, :heads_local].set(grad_step_raw), extra]
    wide = []
    for flow in range(FLOWS):
        wide += [grad_inner_raw[:, flow * flow_cols : (flow + 1) * flow_cols], extras[flow]]
    inner_keep, inner_send = weight_grad(places, normed_t, jnp.concatenate(wide, axis=1))
    inner_flows = reduce_flows(list(inner_keep), list(inner_send), 0, 2)
    kept, sent = (
        [jnp.concatenate(group, axis=1) for group in zip(one, two, three)]
        for one, two, three in zip(out_flows, gate_flows, inner_flows)
    )
    kept, _ = reduce_flows(kept, sent, 2, DIMS)
    grad_norm_in = jnp.sum(grad_normed * hidden * rstd_in, axis=0)
    weighted = grad_normed * norm_in[None, :]
    grad_hidden = rstd_in * weighted - hidden * rstd_in**3 * jnp.mean(
        weighted * hidden, axis=1, keepdims=True
    )
    grad_tokens = (grad_out + grad_hidden).astype(jnp.bfloat16)
    grad_proj_out = jnp.concatenate([part[:, :flow_cols] for part in kept], axis=1).T
    grad_proj_gate = jnp.concatenate([part[:, flow_cols : 2 * flow_cols] for part in kept], axis=1)
    grad_proj_inner = jnp.concatenate(
        [part[:, 2 * flow_cols : 3 * flow_cols] for part in kept], axis=1
    )
    grad_proj_state = kept[0][:, 3 * flow_cols : 3 * flow_cols + share_cols]
    grad_proj_step = kept[1][:, 3 * flow_cols : 3 * flow_cols + heads_local]
    small = (
        grad_norm_in,
        grad_conv_inner,
        grad_bias_inner,
        grad_conv_state,
        grad_bias_state,
        grad_step_bias,
        grad_decay_log,
        grad_skip_gain,
        grad_norm_out,
    )
    flat = jnp.concatenate([part.reshape(-1) for part in small])
    flat = jnp.pad(flat, (0, -flat.shape[0] % 1024)).reshape(-1, 128)
    flat = sum_over_dp(flat).reshape(-1)
    summed, start = [], 0
    for part in small:
        summed.append(flat[start : start + part.size].reshape(part.shape))
        start += part.size
    (
        grad_norm_in,
        grad_conv_inner,
        grad_bias_inner,
        grad_conv_state,
        grad_bias_state,
        grad_step_bias,
        grad_decay_log,
        grad_skip_gain,
        grad_norm_out,
    ) = summed
    return (
        block_out,
        grad_tokens,
        grad_norm_in,
        grad_proj_gate,
        grad_proj_inner,
        grad_proj_state,
        grad_proj_step,
        grad_conv_inner,
        grad_bias_inner,
        grad_conv_state,
        grad_bias_state,
        grad_step_bias,
        grad_decay_log,
        grad_skip_gain,
        grad_norm_out,
        grad_proj_out,
    )


def solution(mesh):
    return jax.shard_map(
        local,
        mesh=mesh,
        in_specs=(
            P("dp", None),
            P("dp", None),
            P(),
            P(None, "tensor"),
            P(None, "tensor"),
            P(),
            P(None, "tensor"),
            P(None, "tensor"),
            P("tensor"),
            P(),
            P(),
            P("tensor"),
            P("tensor"),
            P("tensor"),
            P("tensor"),
            P("tensor", None),
            P("dp", None),
        ),
        out_specs=(
            P("dp", None),
            P("dp", None),
            P(),
            P("dp", "tensor"),
            P("dp", "tensor"),
            P("dp", "tensor"),
            P("dp", "tensor"),
            P(None, "tensor"),
            P("tensor"),
            P(None, "tensor"),
            P("tensor"),
            P("tensor"),
            P("tensor"),
            P("tensor"),
            P("tensor"),
            P("tensor", "dp"),
        ),
        check_vma=False,
    )
```

```python
import functools

import jax
import jax.numpy as jnp
from jax import lax
from jax.experimental import pallas as pl
from jax.experimental.pallas import tpu as pltpu
from jax.sharding import PartitionSpec as P

EPS = 1e-05
HIGH = lax.Precision.HIGHEST
FLOWS = 3
DIMS = 6
BLOCKS = 64
TILE = 256
CHUNK = 128
LIMIT = 60 * 1024 * 1024
HINT = 10**6


def cost(flops, bytes_accessed, transcendentals):
    return pl.CostEstimate(
        flops=flops // HINT, bytes_accessed=bytes_accessed // HINT, transcendentals=transcendentals // HINT
    )


def dot(left, right, precision=None):
    return jnp.dot(left, right, precision=precision, preferred_element_type=jnp.float32)


def dot_first(left, right, precision=None):
    return lax.dot_general(
        left,
        right,
        (((0,), (0,)), ((), ())),
        precision=precision,
        preferred_element_type=jnp.float32,
    )


def dot_last(left, right, precision=None):
    return lax.dot_general(
        left,
        right,
        (((1,), (1,)), ((), ())),
        precision=precision,
        preferred_element_type=jnp.float32,
    )


def chip_bits(index):
    bits = []
    for place in (4, 2, 0):
        coord = (index >> place) & 3
        bits += [(coord ^ (coord >> 1)) & 1, coord >> 1]
    return bits


def partner(index, dim):
    place = (4, 2, 0)[dim // 2]
    return index ^ ((3 if dim % 2 else 1) << place)


HALVINGS = 3


def flow_dim(core, flow, step):
    if step < HALVINGS:
        return HALVINGS * core + (flow + step) % HALVINGS
    return HALVINGS * (1 - core) + step - HALVINGS


def last_groups():
    groups = []
    for core in range(2):
        lines = {}
        for index in range(BLOCKS):
            bits = chip_bits(index)
            last = tuple(bits[flow_dim(core, 0, step)] for step in range(HALVINGS, DIMS))
            rest = tuple(bits[flow_dim(core, 0, step)] for step in range(HALVINGS))
            lines.setdefault(rest, []).append((last, 2 * index + core))
        groups += [[device for _, device in sorted(line)] for line in lines.values()]
    return groups


def flow_pairs(flow, step):
    return [
        (2 * index + core, 2 * partner(index, flow_dim(core, flow, step)) + core)
        for index in range(BLOCKS)
        for core in range(2)
    ]


def swap_tensor(values):
    return lax.ppermute(values, "tensor", [(0, 1), (1, 0)])


def block_order():
    index = lax.axis_index("dp")
    core = lax.axis_index("tensor")
    mine = chip_bits(index)
    place = jnp.arange(BLOCKS, dtype=jnp.int32)
    orders = []
    for flow in range(FLOWS):
        by_core = []
        for which in range(2):
            bits = [None] * DIMS
            for step in range(DIMS):
                dim = flow_dim(which, flow, step)
                bits[dim] = (place >> (DIMS - 1 - step)) & 1
                if step < HALVINGS:
                    bits[dim] = bits[dim] ^ mine[dim]
            block = jnp.zeros((BLOCKS,), jnp.int32)
            for first in range(0, DIMS, 2):
                high = bits[first + 1]
                block = block * 4 + 2 * high + (bits[first] ^ high)
            by_core.append(block)
        orders.append(jnp.where(core == 0, by_core[0], by_core[1]))
    return jnp.stack(orders)


def ends_of(lengths):
    ends, total = [], 0
    for slot in range(lengths.shape[1]):
        total = total + lengths[0, slot]
        ends.append(total)
    return ends


def segment_of(positions, ends):
    segment = jnp.zeros(positions.shape, jnp.int32)
    for end in ends:
        segment = segment + (positions >= end).astype(jnp.int32)
    return segment


def fill_keeps(keeps, ends):
    rows = lax.broadcasted_iota(jnp.int32, keeps.shape[1:], 0)
    here = segment_of(rows, ends)
    for lag in range(1, keeps.shape[0] + 1):
        same = (segment_of(rows - lag, ends) == here) & (rows >= lag)
        keeps[lag - 1] = same.astype(jnp.float32)


def same_sequence(rows, ends, later):
    first = lax.broadcasted_iota(jnp.int32, (rows, rows), later)
    second = lax.broadcasted_iota(jnp.int32, (rows, rows), 1 - later)
    same = segment_of(first, ends) == segment_of(second, ends)
    return (same & (first >= second)).astype(jnp.float32)


def wide(mask, cols):
    return mask if cols == CHUNK else jnp.concatenate([mask] * (cols // CHUNK), axis=1)


def conv_forward(values, taps, bias, keeps):
    total = bias + taps[0:1] * values
    for lag in range(1, taps.shape[0]):
        keep = wide(keeps[lag - 1], values.shape[1])
        total = total + taps[lag : lag + 1] * pltpu.roll(values, lag, 0) * keep
    return total


def conv_backward(grad_pre, values, taps, keeps):
    rows, cols = values.shape
    tap_grads = [jnp.sum(grad_pre * values, axis=0, keepdims=True)]
    grad_values = grad_pre * taps[0:1]
    for lag in range(1, taps.shape[0]):
        kept = grad_pre * wide(keeps[lag - 1], cols)
        tap_grads.append(jnp.sum(kept * pltpu.roll(values, lag, 0), axis=0, keepdims=True))
        grad_values = grad_values + pltpu.roll(kept, rows - lag, 0) * taps[lag : lag + 1]
    return jnp.concatenate(tap_grads, axis=0), jnp.sum(grad_pre, axis=0, keepdims=True), grad_values


def softplus(values):
    return jnp.maximum(values, 0.0) + jnp.log1p(jnp.exp(-jnp.abs(values)))


def head_row(values, first):
    channel = lax.broadcasted_iota(jnp.int32, (1, TILE), 1)
    row = jnp.zeros((1, TILE), jnp.float32)
    for head in range(TILE // 64):
        row = jnp.where(channel // 64 == head, values[first + head], row)
    return row


def forward_kernel(
    lengths,
    skip,
    tokens,
    norm_in,
    proj_gate,
    proj_inner,
    proj_state,
    proj_step,
    conv_inner,
    gains,
    conv_state,
    bias_state,
    step_bias,
    decay_log,
    proj_out,
    cotangent,
    normed,
    gate_raw,
    inner_raw,
    inner_pre,
    mixed,
    scaled,
    partial,
    row_sums,
    state_raw,
    state_pre,
    maps,
    step_pre,
    cumul,
    keeps,
    scores,
    cum_rows,
    step_rows,
    reach_rows,
    reach_cols,
    square_cols,
    along_cols,
    *,
    tiles,
):
    tile = pl.program_id(0)
    rows = tokens.shape[0]
    heads = step_bias.shape[1]
    chunks = rows // CHUNK

    @pl.when(tile == 0)
    def _():
        ends = ends_of(lengths)
        fill_keeps(keeps, ends)
        for chunk in range(chunks):
            at = slice(chunk * CHUNK, (chunk + 1) * CHUNK)
            hidden = tokens[at, :].astype(jnp.float32)
            rstd = lax.rsqrt(jnp.mean(hidden * hidden, axis=1, keepdims=True) + EPS)
            normed[at, :] = (hidden * rstd * norm_in[...]).astype(jnp.bfloat16)
        raw = dot(normed[...], proj_state[...])
        state_raw[...] = raw
        pre = conv_forward(raw, conv_state, bias_state[...], keeps)
        state_pre[...] = pre
        maps[...] = jax.nn.silu(pre).astype(jnp.bfloat16)
        states = maps.shape[1] // 2
        scores[...] = dot_last(maps[:, states:], maps[:, :states]) * same_sequence(rows, ends, 0)
        step_pre[...] = jnp.zeros(step_pre.shape, jnp.float32)
        step_pre[:, :heads] = dot_last(normed[...], proj_step[...]) + step_bias[...]
        steps = softplus(step_pre[...])
        cumul[...] = jnp.zeros(cumul.shape, jnp.float32)
        cumul[:, :heads] = steps[:, :heads] * -jnp.exp(decay_log[...])
        earlier = lax.broadcasted_iota(jnp.int32, (rows, rows), 0) >= lax.broadcasted_iota(
            jnp.int32, (rows, rows), 1
        )
        total = dot(earlier.astype(jnp.float32), cumul[...], HIGH)
        cumul[...] = total
        total_rows = total.T
        steps_rows = steps.T
        cum_rows[...] = total_rows
        step_rows[...] = steps_rows
        for chunk in range(1, chunks):
            start = chunk * CHUNK
            reach_rows[chunk - 1, :, :start] = (
                jnp.exp(total_rows[:, start - 1 : start] - total_rows[:, :start])
                * steps_rows[:, :start]
            )
            reach_cols[start : start + CHUNK, :] = jnp.exp(
                total[start : start + CHUNK] - total[start - 1 : start]
            )
        square_cols[...] = jnp.zeros(square_cols.shape, jnp.float32)
        along_cols[...] = jnp.zeros(along_cols.shape, jnp.float32)

    @pl.when(tile < tiles)
    def _():
        gate = dot(normed[...], proj_gate[...])
        gate_raw[...] = gate
        inner = dot(normed[...], proj_inner[...])
        inner_raw[...] = inner
        pre = conv_forward(inner, conv_inner, gains[0:1, :], keeps)
        inner_pre[...] = pre
        xconv = jax.nn.silu(pre)
        values = xconv.astype(jnp.bfloat16)
        first = tile * (TILE // 64)
        back = lax.rem(CHUNK - first, CHUNK)
        cum_cols = pltpu.roll(cumul[...], back, 1)
        near_cols = pltpu.roll(reach_cols[...], back, 1)
        skip_row = head_row(skip, first)
        lane = lax.broadcasted_iota(jnp.int32, (rows, CHUNK), 1)
        for pair in range(TILE // CHUNK):
            cols = slice(pair * CHUNK, (pair + 1) * CHUNK)
            two = values[:, cols]
            outs = []
            for head in (2 * pair, 2 * pair + 1):
                cum_row = cum_rows[pl.ds(first + head, 1), :]
                step_row = step_rows[pl.ds(first + head, 1), :]
                strips = []
                for chunk in range(chunks):
                    start, stop = chunk * CHUNK, (chunk + 1) * CHUNK
                    gap = cum_cols[start:stop, head : head + 1] - cum_row[:, start:stop]
                    weights = (
                        scores[start:stop, start:stop]
                        * jnp.exp(jnp.minimum(gap, 0.0))
                        * step_row[:, start:stop]
                    ).astype(jnp.bfloat16)
                    if chunk:
                        reach = reach_rows[chunk - 1, pl.ds(first + head, 1), :][:, :start]
                        far = scores[start:stop, :start] * near_cols[start:stop, head : head + 1] * reach
                        weights = jnp.concatenate([far.astype(jnp.bfloat16), weights], axis=1)
                    strips.append(dot(weights, two[:stop]))
                outs.append(jnp.concatenate(strips, axis=0))
            whole = jnp.where(lane < 64, outs[0], outs[1]) + skip_row[:, cols] * xconv[:, cols]
            mixed[:, cols] = whole
            gated = whole * jax.nn.silu(gate[:, cols])
            square_cols[...] += gated * gated
            place = pl.multiple_of(tile * TILE + pair * CHUNK, CHUNK)
            scaled[:, pl.ds(place, CHUNK)] = (gated * gains[1:2, cols]).astype(jnp.bfloat16)

    @pl.when(tile >= tiles)
    def _():
        part = dot(scaled[...], proj_out[...])
        partial[...] = part
        products = part * cotangent[...].astype(jnp.float32)
        along_cols[...] += products[:, :CHUNK] + products[:, CHUNK:]

    @pl.when(tile == pl.num_programs(0) - 1)
    def _():
        row_sums[...] = jnp.zeros(row_sums.shape, jnp.float32)
        row_sums[0:1, :] = jnp.sum(square_cols[...].T, axis=0, keepdims=True)
        row_sums[1:2, :] = jnp.sum(along_cols[...].T, axis=0, keepdims=True)


def tile_cols(tile):
    return (0, tile)


def fixed(tile):
    return (0, 0)


def forward(
    lengths,
    skip,
    tokens,
    norm_in,
    proj_gate,
    proj_inner,
    proj_state,
    proj_step,
    conv_inner,
    gains,
    conv_state,
    bias_state,
    step_bias,
    decay_log,
    proj_out,
    cotangent,
):
    rows, width = tokens.shape
    inner = proj_gate.shape[1]
    taps = conv_inner.shape[0]
    states = proj_state.shape[1]
    heads = proj_step.shape[0]
    f32, bf16 = jnp.float32, jnp.bfloat16
    smem = pl.BlockSpec(memory_space=pltpu.SMEM)

    def whole(*shape):
        return pl.BlockSpec(shape, fixed)

    tiles = inner // TILE

    def strip(count):
        return pl.BlockSpec((count, TILE), lambda tile: (0, jnp.minimum(tile, tiles - 1)))

    def later(count):
        return pl.BlockSpec((count, TILE), lambda tile: (0, jnp.maximum(tile - tiles, 0)))

    return pl.pallas_call(
        functools.partial(forward_kernel, tiles=tiles),
        grid=(tiles + width // TILE,),
        in_specs=[
            smem,
            smem,
            whole(rows, width),
            whole(1, width),
            strip(width),
            strip(width),
            whole(width, states),
            whole(heads, width),
            strip(taps),
            strip(2),
            whole(taps, states),
            whole(1, states),
            whole(1, heads),
            whole(1, heads),
            later(inner),
            later(rows),
        ],
        out_specs=[
            whole(rows, width),
            strip(rows),
            strip(rows),
            strip(rows),
            strip(rows),
            whole(rows, inner),
            later(rows),
            whole(8, rows),
            whole(rows, states),
            whole(rows, states),
            whole(rows, states),
            whole(rows, CHUNK),
            whole(rows, CHUNK),
        ],
        out_shape=[
            jax.ShapeDtypeStruct((rows, width), bf16),
            jax.ShapeDtypeStruct((rows, inner), f32),
            jax.ShapeDtypeStruct((rows, inner), f32),
            jax.ShapeDtypeStruct((rows, inner), f32),
            jax.ShapeDtypeStruct((rows, inner), f32),
            jax.ShapeDtypeStruct((rows, inner), bf16),
            jax.ShapeDtypeStruct((rows, width), f32),
            jax.ShapeDtypeStruct((8, rows), f32),
            jax.ShapeDtypeStruct((rows, states), f32),
            jax.ShapeDtypeStruct((rows, states), f32),
            jax.ShapeDtypeStruct((rows, states), bf16),
            jax.ShapeDtypeStruct((rows, CHUNK), f32),
            jax.ShapeDtypeStruct((rows, CHUNK), f32),
        ],
        scratch_shapes=[
            pltpu.VMEM((taps - 1, rows, CHUNK), f32),
            pltpu.VMEM((rows, rows), f32),
            pltpu.VMEM((CHUNK, rows), f32),
            pltpu.VMEM((CHUNK, rows), f32),
            pltpu.VMEM((rows // CHUNK - 1, CHUNK, rows), f32),
            pltpu.VMEM((rows, CHUNK), f32),
            pltpu.VMEM((rows, CHUNK), f32),
            pltpu.VMEM((rows, CHUNK), f32),
        ],
        compiler_params=pltpu.CompilerParams(vmem_limit_bytes=LIMIT),
        cost_estimate=cost(
            flops=2 * rows * width * (2 * inner + states + heads) + 2 * rows * rows * inner,
            bytes_accessed=4 * width * inner + 18 * rows * inner,
            transcendentals=4 * rows * inner,
        ),
        name="layer_forward",
    )(
        lengths,
        skip,
        tokens,
        norm_in,
        proj_gate,
        proj_inner,
        proj_state,
        proj_step,
        conv_inner,
        gains,
        conv_state,
        bias_state,
        step_bias,
        decay_log,
        proj_out,
        cotangent,
    )


def scale_row(row_sums, came, lengths, inner_total):
    rstd = lax.rsqrt((row_sums[0:1, :] + came[0:1, :]) / inner_total + EPS)
    rows = lax.broadcasted_iota(jnp.int32, rstd.shape, 1)
    return rstd, (rows < ends_of(lengths)[-1]).astype(jnp.float32)


def turned(values):
    count = values.shape[1]
    row = lax.broadcasted_iota(jnp.int32, (count, count), 0)
    col = lax.broadcasted_iota(jnp.int32, (count, count), 1)
    return dot_last((row == col).astype(jnp.bfloat16), values)


def store_flow(held, sems, flow, count, compute, keeps, sends):
    half = held.shape[1] // 2
    slot = lax.rem(flow, 2)

    def copy_out(which_flow, which):
        to = (keeps, sends)[which][which_flow]
        at = which_flow % 2
        return pltpu.make_async_copy(
            held.at[at, pl.ds(which * half, half)], to, sems.at[at, which]
        )

    for done in range(count - 2):

        @pl.when(flow == done + 2)
        def _(done=done):
            copy_out(done, 0).wait()
            copy_out(done, 1).wait()

    block = half // 2
    for which in (1, 0):
        for part in range(2):
            at = slice(which * half + part * block, which * half + (part + 1) * block)
            compute(slot, at)
        for each in range(count):

            @pl.when(flow == each)
            def _(each=each, which=which):
                copy_out(each, which).start()

    @pl.when(flow == count - 1)
    def _():
        for each in (count - 2, count - 1):
            copy_out(each, 0).wait()
            copy_out(each, 1).wait()


def out_grad_kernel(
    lengths,
    blocks,
    row_sums,
    came,
    cotangent,
    scaled,
    normed,
    arranged,
    keep_one,
    keep_two,
    keep_three,
    send_one,
    send_two,
    send_three,
    normed_t,
    cotangent_t,
    grad_projected,
    held,
    sems,
    *,
    inner_total,
    tiles,
):
    step = pl.program_id(0)

    @pl.when(step < tiles)
    def _():
        rstd, valid = scale_row(row_sums, came, lengths, inner_total)
        at = pl.ds(pl.multiple_of(step * TILE, TILE), TILE)
        cotangent_t[at, :] = turned(cotangent[...]) * (rstd * valid)
        normed_t[at, :] = turned(normed[...])

    @pl.when(step >= tiles)
    def _():
        per = normed_t.shape[0] // BLOCKS
        flow = step - tiles
        for place in range(0, BLOCKS, 2):
            at = slice(place * per, (place + 2) * per)
            rows = [
                pl.ds(pl.multiple_of(blocks[flow, place + more] * per, 8), per) for more in range(2)
            ]
            arranged[0, at, :] = jnp.concatenate(
                [normed_t[one, :] for one in rows], axis=0
            ).astype(jnp.bfloat16)
            grad_projected[at, :] = jnp.concatenate(
                [cotangent_t[one, :] for one in rows], axis=0
            ).astype(jnp.bfloat16)

        def compute(slot, at):
            held[slot, at, :] = dot(grad_projected[at, :], scaled[...])

        store_flow(
            held,
            sems,
            flow,
            FLOWS,
            compute,
            (keep_one, keep_two, keep_three),
            (send_one, send_two, send_three),
        )


def out_grad(lengths, blocks, row_sums, came, cotangent, scaled, normed, inner_total):
    rows, width = cotangent.shape
    inner = scaled.shape[1]
    tiles = width // TILE
    share = inner // FLOWS
    smem = pl.BlockSpec(memory_space=pltpu.SMEM)
    row = pl.BlockSpec((8, rows), fixed)
    cols = pl.BlockSpec((rows, TILE), lambda step: (0, jnp.minimum(step, tiles - 1)))
    return pl.pallas_call(
        functools.partial(out_grad_kernel, inner_total=inner_total, tiles=tiles),
        grid=(tiles + FLOWS,),
        in_specs=[
            smem,
            smem,
            row,
            row,
            cols,
            pl.BlockSpec((rows, share), lambda step: (0, jnp.maximum(step - tiles, 0))),
            cols,
        ],
        out_specs=[
            pl.BlockSpec((1, width, rows), lambda step: (jnp.maximum(step - tiles, 0), 0, 0)),
        ]
        + [pl.BlockSpec(memory_space=pl.ANY)] * (2 * FLOWS),
        out_shape=[jax.ShapeDtypeStruct((FLOWS, width, rows), jnp.bfloat16)]
        + [jax.ShapeDtypeStruct((width // 2, share), jnp.float32)] * (2 * FLOWS),
        scratch_shapes=[
            pltpu.VMEM((width, rows), jnp.float32),
            pltpu.VMEM((width, rows), jnp.float32),
            pltpu.VMEM((width, rows), jnp.bfloat16),
            pltpu.VMEM((2, width, share), jnp.float32),
            pltpu.SemaphoreType.DMA((2, 2)),
        ],
        compiler_params=pltpu.CompilerParams(vmem_limit_bytes=LIMIT),
        cost_estimate=cost(
            flops=2 * rows * inner * width,
            bytes_accessed=4 * inner * width + 14 * rows * width,
            transcendentals=0,
        ),
        name="out_grad",
    )(lengths, blocks, row_sums, came, cotangent, scaled, normed)


def backward_kernel(
    lengths,
    skip,
    row_sums,
    came,
    cotangent,
    proj_out,
    gains,
    gate_raw,
    mixed,
    inner_raw,
    inner_pre,
    conv_inner,
    maps,
    step_pre,
    cumul,
    arranged,
    *rest,
    origin,
    inner_total,
):
    (
        grad_gate,
        grad_inner,
        grad_scores,
        grad_steps,
        grad_flows,
        sums,
        keep_one,
        keep_two,
        keep_three,
        send_one,
        send_two,
        send_three,
        grad_projected,
        slope_cols,
        keeps,
        scores,
        cum_rows,
        near_rows,
        far_cols,
        step_cols,
        held,
        sems,
    ) = rest[-22:]
    tile = pl.program_id(0)
    rows = cotangent.shape[0]
    chunks = rows // CHUNK

    @pl.when(tile == 0)
    def _():
        ends = ends_of(lengths)
        fill_keeps(keeps, ends)
        rstd, valid = scale_row(row_sums, came, lengths, inner_total)
        slope = (row_sums[1:2, :] + came[1:2, :]) * valid * (rstd * rstd * rstd) / inner_total
        scale_cols = jnp.broadcast_to(rstd * valid, (CHUNK, rows)).T
        slope_cols[...] = jnp.broadcast_to(slope, (CHUNK, rows)).T
        for chunk in range(chunks):
            at = slice(chunk * CHUNK, (chunk + 1) * CHUNK)
            grad_projected[at, :] = (
                cotangent[at, :].astype(jnp.float32) * scale_cols[at, 0:1]
            ).astype(jnp.bfloat16)
        states = maps.shape[1] // 2
        scores[...] = dot_last(maps[:, :states], maps[:, states:]) * same_sequence(rows, ends, 1)
        total = cumul[...]
        total_rows = total.T
        cum_rows[...] = total_rows
        step_cols[...] = softplus(step_pre[...])
        for chunk in range(chunks - 1):
            start, stop = chunk * CHUNK, (chunk + 1) * CHUNK
            near_rows[chunk, :, stop:] = jnp.exp(
                total_rows[:, stop:] - total_rows[:, stop - 1 : stop]
            )
            far_cols[start:stop, :] = jnp.exp(total[stop - 1 : stop] - total[start:stop])
        grad_scores[...] = jnp.zeros(grad_scores.shape, jnp.float32)
        grad_steps[...] = jnp.zeros(grad_steps.shape, jnp.float32)
        grad_flows[...] = jnp.zeros(grad_flows.shape, jnp.float32)

    first = (tile + origin) * (TILE // 64)
    back = lax.rem(CHUNK - first, CHUNK)
    cum_turned = pltpu.roll(cumul[...], back, 1)
    far_turned = pltpu.roll(far_cols[...], back, 1)
    step_turned = pltpu.roll(step_cols[...], back, 1)
    skip_row = head_row(skip, first)
    lane = lax.broadcasted_iota(jnp.int32, (rows, CHUNK), 1)
    grad_scaled = dot_last(grad_projected[...], proj_out[...])
    for pair in range(TILE // CHUNK):
        cols = slice(pair * CHUNK, (pair + 1) * CHUNK)
        raw = gate_raw[:, cols]
        sigma = jax.nn.sigmoid(raw)
        act = raw * sigma
        mix = mixed[:, cols]
        gated = mix * act
        grad_wide = grad_scaled[:, cols]
        sums[0:1, cols] = jnp.sum(grad_wide * gated, axis=0, keepdims=True)
        grad_gated = grad_wide * gains[1:2, cols] - slope_cols[...] * gated
        grad_mixed = grad_gated * act
        grad_gate[:, cols] = (grad_gated * mix * (sigma * (1.0 + raw * (1.0 - sigma)))).astype(
            jnp.bfloat16
        )
        pre = inner_pre[:, cols]
        sigma = jax.nn.sigmoid(pre)
        xconv = pre * sigma
        sums[1:2, cols] = jnp.sum(grad_mixed * xconv, axis=0, keepdims=True)
        values = xconv.astype(jnp.bfloat16)
        grad_ssd = grad_mixed.astype(jnp.bfloat16)
        outs = []
        for half in range(2):
            head = 2 * pair + half
            mine = (lane < 64) if half == 0 else (lane >= 64)
            own = jnp.where(mine, values, jnp.zeros_like(values))
            middle = rows // 2
            late = dot_last(own, grad_ssd[middle:])
            early = dot_last(own[:middle], grad_ssd[:middle])
            cum_row = cum_rows[pl.ds(first + head, 1), :]
            flows = [jnp.zeros((8, CHUNK), jnp.float32) for _ in range(chunks)]
            strips, ups = [], []
            for chunk in range(chunks):
                start, stop = chunk * CHUNK, (chunk + 1) * CHUNK
                step_col = step_turned[start:stop, head : head + 1]
                cum_col = cum_turned[start:stop, head : head + 1]
                if chunk < chunks - 1:
                    far_col = far_turned[start:stop, head : head + 1]
                    far_step = far_col * step_col
                    near_row = near_rows[chunk, pl.ds(first + head, 1), :]
                weights, far_sum = [], None
                for other in range(chunk, chunks):
                    begin, end = other * CHUNK, (other + 1) * CHUNK
                    if begin < middle:
                        grad_mix = early[start:stop, begin:end]
                    else:
                        grad_mix = late[start:stop, begin - middle : end - middle]
                    score = scores[start:stop, begin:end]
                    product = grad_mix * score
                    if other == chunk:
                        kernel = jnp.exp(jnp.minimum(cum_row[:, begin:end] - cum_col, 0.0))
                        weighted = kernel * step_col
                        near_sum = product * kernel
                    else:
                        weighted = far_step * near_row[:, begin:end]
                        part = product * near_row[:, begin:end]
                        far_sum = part if far_sum is None else far_sum + part
                    grad_scores[start:stop, begin:end] += grad_mix * weighted
                    weights.append((score * weighted).astype(jnp.bfloat16))
                    flow = product * weighted
                    flows[other] = flows[other] + jnp.sum(
                        flow.reshape(CHUNK // 8, 8, CHUNK), axis=0
                    )
                up = jnp.sum(near_sum, axis=1, keepdims=True)
                if far_sum is not None:
                    up = up + far_col * jnp.sum(far_sum, axis=1, keepdims=True)
                ups.append(up)
                strips.append(
                    dot(
                        jnp.concatenate(weights, axis=1) if len(weights) > 1 else weights[0],
                        grad_ssd[start:],
                    )
                )
            outs.append(jnp.concatenate(strips, axis=0))
            grad_steps[...] += jnp.where(lane == first + head, jnp.concatenate(ups, axis=0), 0.0)
            grad_flows[pl.ds(first + head, 1), :] = jnp.concatenate(
                [jnp.sum(flow, axis=0, keepdims=True) for flow in flows], axis=1
            )
        grad_xconv = grad_mixed * skip_row[:, cols] + jnp.where(lane < 64, outs[0], outs[1])
        grad_pre = grad_xconv * (sigma * (1.0 + pre * (1.0 - sigma)))
        tap_grads, bias_grad, grad_raw = conv_backward(
            grad_pre, inner_raw[:, cols], conv_inner[:, cols], keeps
        )
        sums[2:3, cols] = bias_grad
        sums[3:7, cols] = tap_grads
        grad_inner[:, cols] = grad_raw.astype(jnp.bfloat16)

    def compute(slot, at):
        lines = arranged[0, at, :]
        held[slot, at, :TILE] = dot(lines, grad_gate[...])
        held[slot, at, TILE:] = dot(lines, grad_inner[...])

    store_flow(
        held,
        sems,
        tile,
        FLOWS,
        compute,
        (keep_one, keep_two, keep_three),
        (send_one, send_two, send_three),
    )


def backward(
    lengths,
    skip,
    row_sums,
    came,
    cotangent,
    proj_out,
    gains,
    gate_raw,
    mixed,
    inner_raw,
    inner_pre,
    conv_inner,
    maps,
    step_pre,
    cumul,
    arranged,
    after,
    origin,
    inner_total,
):
    tiles = FLOWS
    rows, width = cotangent.shape
    taps = conv_inner.shape[0]
    states = maps.shape[1]
    f32, bf16 = jnp.float32, jnp.bfloat16
    smem = pl.BlockSpec(memory_space=pltpu.SMEM)

    def whole(*shape):
        return pl.BlockSpec(shape, fixed)

    def strip(count):
        return pl.BlockSpec((count, TILE), lambda tile: (0, tile + origin))

    return pl.pallas_call(
        functools.partial(backward_kernel, origin=origin, inner_total=inner_total),
        grid=(tiles,),
        in_specs=[
            smem,
            smem,
            whole(8, rows),
            whole(8, rows),
            whole(rows, width),
            pl.BlockSpec((TILE, width), lambda tile: (tile + origin, 0)),
            strip(2),
            strip(rows),
            strip(rows),
            strip(rows),
            strip(rows),
            strip(taps),
            whole(rows, states),
            whole(rows, CHUNK),
            whole(rows, CHUNK),
            pl.BlockSpec((1, width, rows), lambda tile: (tile, 0, 0)),
        ]
        + [pl.BlockSpec(memory_space=pl.ANY)] * len(after),
        out_specs=[
            pl.BlockSpec((rows, TILE), tile_cols),
            pl.BlockSpec((rows, TILE), tile_cols),
            whole(rows, rows),
            whole(rows, CHUNK),
            whole(CHUNK, rows),
            pl.BlockSpec((8, TILE), tile_cols),
        ]
        + [pl.BlockSpec(memory_space=pl.ANY)] * (2 * FLOWS),
        out_shape=[
            jax.ShapeDtypeStruct((rows, TILE * tiles), bf16),
            jax.ShapeDtypeStruct((rows, TILE * tiles), bf16),
            jax.ShapeDtypeStruct((rows, rows), f32),
            jax.ShapeDtypeStruct((rows, CHUNK), f32),
            jax.ShapeDtypeStruct((CHUNK, rows), f32),
            jax.ShapeDtypeStruct((8, TILE * tiles), f32),
        ]
        + [jax.ShapeDtypeStruct((width // 2, 2 * TILE), f32)] * (2 * FLOWS),
        scratch_shapes=[
            pltpu.VMEM((rows, width), bf16),
            pltpu.VMEM((rows, CHUNK), f32),
            pltpu.VMEM((taps - 1, rows, CHUNK), f32),
            pltpu.VMEM((rows, rows), f32),
            pltpu.VMEM((CHUNK, rows), f32),
            pltpu.VMEM((rows // CHUNK - 1, CHUNK, rows), f32),
            pltpu.VMEM((rows, CHUNK), f32),
            pltpu.VMEM((rows, CHUNK), f32),
            pltpu.VMEM((2, width, 2 * TILE), f32),
            pltpu.SemaphoreType.DMA((2, 2)),
        ],
        compiler_params=pltpu.CompilerParams(vmem_limit_bytes=LIMIT),
        cost_estimate=cost(
            flops=6 * rows * width * TILE * tiles + 4 * rows * rows * TILE * tiles,
            bytes_accessed=2 * width * TILE * tiles + 20 * rows * TILE * tiles,
            transcendentals=4 * rows * TILE * tiles,
        ),
        name="layer_backward",
    )(
        lengths,
        skip,
        row_sums,
        came,
        cotangent,
        proj_out,
        gains,
        gate_raw,
        mixed,
        inner_raw,
        inner_pre,
        conv_inner,
        maps,
        step_pre,
        cumul,
        arranged,
        *after,
    )


def scan_kernel(
    lengths,
    core,
    scores_one,
    scores_two,
    steps_one,
    steps_two,
    flows_one,
    flows_two,
    maps,
    step_pre,
    decay_log,
    *rest,
):
    own, other, grad_step, sums, rates = rest[-5:]
    rows = maps.shape[0]
    states = maps.shape[1] // 2
    heads = decay_log.shape[1]
    grad_scores = (scores_one[...] + scores_two[...]) * same_sequence(rows, ends_of(lengths), 1)
    grad_input = dot(grad_scores, maps[:, states:].astype(jnp.float32), HIGH)
    grad_output = dot_first(grad_scores, maps[:, :states].astype(jnp.float32), HIGH)
    first = core[0] == 0
    own[...] = jnp.where(first, grad_input, grad_output)
    other[...] = jnp.where(first, grad_output, grad_input)
    pre = step_pre[...]
    steps = softplus(pre)
    rates[...] = jnp.zeros(rates.shape, jnp.float32)
    rates[0:1, :heads] = -jnp.exp(decay_log[...])
    rate = rates[0:1, :]
    direct = steps_one[...] + steps_two[...]
    grad_cum = (flows_one[...] + flows_two[...]).T - steps * direct
    later = lax.broadcasted_iota(jnp.int32, (rows, rows), 0) <= lax.broadcasted_iota(
        jnp.int32, (rows, rows), 1
    )
    grad_rate = dot(later.astype(jnp.float32), grad_cum, HIGH)
    grad_pre = (direct + grad_rate * rate) * jax.nn.sigmoid(pre)
    grad_step[...] = grad_pre.astype(jnp.bfloat16)
    sums[...] = jnp.zeros(sums.shape, jnp.float32)
    sums[0:1, :] = jnp.sum(grad_pre, axis=0, keepdims=True)
    sums[1:2, :] = jnp.sum(grad_rate * steps, axis=0, keepdims=True) * rate


def scan_gradients(lengths, core, one, two, maps, step_pre, decay_log, after):
    rows = maps.shape[0]
    states = maps.shape[1] // 2
    vmem = pl.BlockSpec(memory_space=pltpu.VMEM)
    smem = pl.BlockSpec(memory_space=pltpu.SMEM)
    return pl.pallas_call(
        scan_kernel,
        in_specs=[smem, smem] + [vmem] * 9 + [pl.BlockSpec(memory_space=pl.ANY)] * len(after),
        out_specs=[vmem] * 4,
        out_shape=[
            jax.ShapeDtypeStruct((rows, states), jnp.float32),
            jax.ShapeDtypeStruct((rows, states), jnp.float32),
            jax.ShapeDtypeStruct((rows, CHUNK), jnp.bfloat16),
            jax.ShapeDtypeStruct((8, CHUNK), jnp.float32),
        ],
        scratch_shapes=[pltpu.VMEM((8, CHUNK), jnp.float32)],
        compiler_params=pltpu.CompilerParams(vmem_limit_bytes=LIMIT),
        cost_estimate=cost(
            flops=36 * rows * rows * states, bytes_accessed=16 * rows * rows, transcendentals=0
        ),
        name="scan_gradients",
    )(lengths, core, one[0], two[0], one[1], two[1], one[2], two[2], maps, step_pre, decay_log, *after)


def state_kernel(lengths, core, own, came, state_raw, state_pre, conv_state, grad_state, sums, keeps):
    fill_keeps(keeps, ends_of(lengths))
    cols = own.shape[1]
    first = core[0] == 0
    pre = jnp.where(first, state_pre[:, :cols], state_pre[:, cols:])
    raw = jnp.where(first, state_raw[:, :cols], state_raw[:, cols:])
    taps = jnp.where(first, conv_state[:, :cols], conv_state[:, cols:])
    sigma = jax.nn.sigmoid(pre)
    grad_pre = (own[...] + came[...]) * (sigma * (1.0 + pre * (1.0 - sigma)))
    tap_grads, bias_grad, grad_raw = conv_backward(grad_pre, raw, taps, keeps)
    grad_state[...] = grad_raw.astype(jnp.bfloat16)
    sums[...] = jnp.zeros(sums.shape, jnp.float32)
    sums[0:1, :] = bias_grad
    sums[1:5, :] = tap_grads


def state_gradients(lengths, core, own, came, state_raw, state_pre, conv_state):
    rows, cols = own.shape
    vmem = pl.BlockSpec(memory_space=pltpu.VMEM)
    smem = pl.BlockSpec(memory_space=pltpu.SMEM)
    return pl.pallas_call(
        state_kernel,
        in_specs=[smem, smem] + [vmem] * 5,
        out_specs=[vmem] * 2,
        out_shape=[
            jax.ShapeDtypeStruct((rows, cols), jnp.bfloat16),
            jax.ShapeDtypeStruct((8, cols), jnp.float32),
        ],
        scratch_shapes=[pltpu.VMEM((conv_state.shape[0] - 1, rows, CHUNK), jnp.float32)],
        compiler_params=pltpu.CompilerParams(vmem_limit_bytes=LIMIT),
        cost_estimate=cost(
            flops=40 * rows * cols, bytes_accessed=24 * rows * cols, transcendentals=rows * cols
        ),
        name="state_gradients",
    )(lengths, core, own, came, state_raw, state_pre, conv_state)


def weight_grad_kernel(left, *refs, count):
    flow = pl.program_id(0)
    rights, outs = refs[:count], refs[count + 1 :]
    parts = [dot(left[0], right[...]) for right in rights]
    for which, out in enumerate(outs):

        @pl.when(flow == which)
        def _(out=out):
            start = 0
            for part in parts:
                out[:, start : start + part.shape[1]] = part
                start += part.shape[1]


def weight_grad(arranged, rights, half, after, flows=FLOWS):
    _, width, depth = arranged.shape
    shares = [right.shape[1] // flows for right in rights]
    cols = sum(shares)
    rows = width // 2
    parts = 2
    block = rows // parts
    return pl.pallas_call(
        functools.partial(weight_grad_kernel, count=len(rights)),
        grid=(flows, parts),
        in_specs=[
            pl.BlockSpec((1, block, depth), lambda flow, part: (flow, half * parts + part, 0))
        ]
        + [pl.BlockSpec((depth, share), lambda flow, part: (0, flow)) for share in shares]
        + [pl.BlockSpec(memory_space=pl.ANY)],
        out_specs=[
            pl.BlockSpec(
                (block, cols),
                lambda flow, part, which=which: (
                    jnp.clip(parts * (flow - which) + part, 0, parts - 1),
                    0,
                ),
            )
            for which in range(flows)
        ],
        out_shape=[jax.ShapeDtypeStruct((rows, cols), jnp.float32)] * flows,
        compiler_params=pltpu.CompilerParams(vmem_limit_bytes=LIMIT),
        cost_estimate=cost(
            flops=2 * rows * depth * cols * flows,
            bytes_accessed=4 * rows * cols * flows + 2 * depth * (rows + cols) * flows,
            transcendentals=0,
        ),
        name="weight_grad",
    )(arranged, *rights, after)


def add_rows_kernel(*refs, shapes, outs):
    at = 0
    for flow, (joined, counts) in enumerate(shapes):
        wides = refs[at : at + joined]
        at += joined
        out = refs[len(refs) - outs + (flow if outs > 1 else 0)]
        base = sum(cols for before in shapes[:flow] for _, cols in before[1]) if outs == 1 else 0
        start = 0
        for count, cols in counts:
            total = refs[at][...]
            for more in range(1, count):
                total = total + refs[at + more][...]
            for wide_ref in wides:
                if start + cols <= wide_ref.shape[1]:
                    total = total + wide_ref[:, start : start + cols]
            out[:, base + start : base + start + cols] = total
            at += count
            start += cols


def add_rows(flows, start, rows, after=None, together=False, rooms=None, into=None):
    parts = 4 if rows >= 192 else 1
    block = rows // parts
    shapes, flat = [], []
    for joined, groups in flows:
        shapes.append((len(joined), tuple((len(group), group[0].shape[1]) for group in groups)))
        flat += list(joined) + [part for group in groups for part in group]
    in_specs = [
        pl.BlockSpec((block, part.shape[1]), lambda part: (start // block + part, 0))
        for part in flat
    ]
    widths = [sum(cols for _, cols in counts) for _, counts in shapes]
    if together:
        widths = [sum(widths)]
    aliases, places = {}, [0] * len(widths)
    if after is not None:
        flat.append(after)
        in_specs.append(pl.BlockSpec(memory_space=pl.ANY))
    totals = [cols + room for cols, room in zip(widths, rooms or [0] * len(widths))]
    if into is not None:
        aliases = {len(flat) + which: which for which in range(len(into))}
        flat += into
        in_specs += [pl.BlockSpec(memory_space=pl.ANY)] * len(into)
        totals = [part.shape[1] for part in into]
        places = [(total - 1) // cols - (1 if total % cols else 0) for total, cols in zip(totals, widths)]
    return pl.pallas_call(
        functools.partial(add_rows_kernel, shapes=tuple(shapes), outs=len(widths)),
        grid=(parts,),
        in_specs=in_specs,
        out_specs=[
            pl.BlockSpec((block, cols), lambda part, place=place: (part, place))
            for cols, place in zip(widths, places)
        ],
        out_shape=[jax.ShapeDtypeStruct((rows, cols), jnp.float32) for cols in totals],
        input_output_aliases=aliases,
        compiler_params=pltpu.CompilerParams(vmem_limit_bytes=LIMIT),
        cost_estimate=cost(
            flops=rows * sum(widths), bytes_accessed=16 * rows * sum(widths), transcendentals=0
        ),
        name="add_rows",
    )(*flat)


def last_rows_kernel(parts, out_grad_out, out_gate, out_inner, out_state, out_step):
    total = parts[0]
    for more in range(1, parts.shape[0]):
        total = total + parts[more]
    share = out_grad_out.shape[0] // FLOWS
    start = 0
    for flow in range(FLOWS):
        out_grad_out[flow * share : (flow + 1) * share, :] = total[:, start : start + share].T
        start += share
        for group in range(2):
            first = (group * FLOWS + flow) * TILE
            out_gate[:, first : first + TILE] = total[:, start : start + TILE]
            out_inner[:, first : first + TILE] = total[:, start + TILE : start + 2 * TILE]
            start += 2 * TILE
        if flow < 2:
            side = (out_state, out_step)[flow]
            side[...] = total[:, start : start + side.shape[1]]
            start += CHUNK


def last_rows(parts, inner, states, heads):
    rows = parts.shape[1]
    outs = [(inner, rows), (rows, inner), (rows, inner), (rows, states), (rows, heads)]
    return pl.pallas_call(
        last_rows_kernel,
        grid=(1,),
        in_specs=[pl.BlockSpec(parts.shape, lambda _: (0, 0, 0))],
        out_specs=[pl.BlockSpec(shape, fixed) for shape in outs],
        out_shape=[jax.ShapeDtypeStruct(shape, jnp.float32) for shape in outs],
        compiler_params=pltpu.CompilerParams(vmem_limit_bytes=LIMIT),
        cost_estimate=cost(
            flops=8 * rows * inner, bytes_accessed=80 * rows * inner, transcendentals=0
        ),
        name="last_rows",
    )(parts)


def normed_grad_kernel(
    core, gate_one, inner_one, gate_two, inner_two, state, step, gate, inner, proj_state, proj_step, partial, *rest
):
    out = rest[-2]
    half = gate_one.shape[1]
    states = state.shape[1]
    heads = proj_step.shape[0]
    total = dot_last(gate_one[...], gate[:, :half]) + dot_last(inner_one[...], inner[:, :half])
    total = total + dot_last(gate_two[...], gate[:, half:]) + dot_last(inner_two[...], inner[:, half:])
    chosen = jnp.where(core[0] == 0, proj_state[:, :states], proj_state[:, states:])
    out[...] = total + dot_last(state[...], chosen) + dot(step[:, :heads], proj_step[...])


def normed_grad(core, one, two, state, step, proj_gate, proj_inner, proj_state, proj_step, partial, after):
    rows = state.shape[0]
    width, inner = proj_gate.shape

    def whole(values):
        return pl.BlockSpec(values.shape, fixed)

    def lines(values):
        return pl.BlockSpec((TILE, values.shape[1]), lambda tile: (tile, 0))

    return pl.pallas_call(
        normed_grad_kernel,
        grid=(width // TILE,),
        in_specs=[pl.BlockSpec(memory_space=pltpu.SMEM)]
        + [whole(part) for part in (*one, *two, state, step)]
        + [lines(proj_gate), lines(proj_inner), lines(proj_state)]
        + [pl.BlockSpec((proj_step.shape[0], TILE), tile_cols)]
        + [pl.BlockSpec(memory_space=pl.ANY)] * (1 + len(after)),
        out_specs=[pl.BlockSpec((rows, TILE), tile_cols), pl.BlockSpec(memory_space=pl.ANY)],
        out_shape=[jax.ShapeDtypeStruct((rows, width), jnp.float32)] * 2,
        input_output_aliases={11: 1},
        compiler_params=pltpu.CompilerParams(vmem_limit_bytes=LIMIT),
        cost_estimate=cost(
            flops=4 * rows * inner * width,
            bytes_accessed=4 * inner * width + 8 * rows * width,
            transcendentals=0,
        ),
        name="normed_grad",
    )(
        core, *one, *two, state, step, proj_gate, proj_inner, proj_state, proj_step, partial, *after
    )


def tokens_grad_kernel(
    own, came, tokens, cotangent, norm_in, one, two, state, head, grad_tokens, sums
):
    step = pl.program_id(0)
    hidden = tokens[...].astype(jnp.float32)
    rstd = lax.rsqrt(jnp.mean(hidden * hidden, axis=1, keepdims=True) + EPS)
    grad_normed = own[...] + came[...]
    weighted = grad_normed * norm_in[...]
    back = jnp.mean(weighted * hidden, axis=1, keepdims=True)
    grad_hidden = rstd * weighted - hidden * (rstd * rstd * rstd * back)
    grad_tokens[...] = (cotangent[...].astype(jnp.float32) + grad_hidden).astype(jnp.bfloat16)
    part = jnp.sum(grad_normed * hidden * rstd, axis=0, keepdims=True)
    half = one.shape[1]
    width = part.shape[1]

    @pl.when(step == 0)
    def _():
        sums[:, :half] = one[...]
        sums[:, half:width] = two[...]
        sums[:, width : width + CHUNK] = state[...]
        sums[:, width + CHUNK :] = head[...]
        sums[7:8, :width] = part

    @pl.when(step > 0)
    def _():
        sums[7:8, :width] += part


def tokens_grad(own, came, tokens, cotangent, norm_in, one, two, state, head):
    rows, width = tokens.shape
    lines = pl.BlockSpec((CHUNK, width), lambda step: (step, 0))

    def whole(values):
        return pl.BlockSpec(values.shape, fixed)

    return pl.pallas_call(
        tokens_grad_kernel,
        grid=(rows // CHUNK,),
        in_specs=[lines] * 4 + [whole(part) for part in (norm_in, one, two, state, head)],
        out_specs=[lines, pl.BlockSpec((8, width + 2 * CHUNK), fixed)],
        out_shape=[
            jax.ShapeDtypeStruct((rows, width), jnp.bfloat16),
            jax.ShapeDtypeStruct((8, width + 2 * CHUNK), jnp.float32),
        ],
        compiler_params=pltpu.CompilerParams(vmem_limit_bytes=LIMIT),
        cost_estimate=cost(
            flops=12 * rows * width, bytes_accessed=14 * rows * width, transcendentals=0
        ),
        name="tokens_grad",
    )(own, came, tokens, cotangent, norm_in, one, two, state, head)


def block_out_kernel(
    lengths, row_sums, row_came, own, came, tokens, out, cols, *, inner_total
):
    step = pl.program_id(0)

    @pl.when(step == 0)
    def _():
        rstd, valid = scale_row(row_sums, row_came, lengths, inner_total)
        cols[...] = jnp.broadcast_to(rstd * valid, (CHUNK, rstd.shape[1])).T

    scale = cols[pl.ds(pl.multiple_of(step * CHUNK, CHUNK), CHUNK), 0:1]
    out[...] = (tokens[...].astype(jnp.float32) + scale * (own[...] + came[...])).astype(
        jnp.bfloat16
    )


def finish_block(lengths, row_sums, row_came, own, came, tokens, inner_total):
    rows, width = tokens.shape
    lines = pl.BlockSpec((CHUNK, width), lambda step: (step, 0))
    row = pl.BlockSpec((8, rows), fixed)
    return pl.pallas_call(
        functools.partial(block_out_kernel, inner_total=inner_total),
        grid=(rows // CHUNK,),
        in_specs=[pl.BlockSpec(memory_space=pltpu.SMEM), row, row, lines, lines, lines],
        out_specs=lines,
        out_shape=jax.ShapeDtypeStruct((rows, width), jnp.bfloat16),
        scratch_shapes=[pltpu.VMEM((rows, CHUNK), jnp.float32)],
        compiler_params=pltpu.CompilerParams(vmem_limit_bytes=LIMIT),
        cost_estimate=cost(
            flops=3 * rows * width, bytes_accessed=12 * rows * width, transcendentals=0
        ),
        name="block_out",
    )(lengths, row_sums, row_came, own, came, tokens)


def pass_on(part, flow, step):
    return lax.ppermute(part, ("dp", "tensor"), flow_pairs(flow, step))


def sum_over_dp(values):
    for dim in range(0, DIMS, 2):
        others = [
            lax.ppermute(
                values,
                "dp",
                [
                    (index, partner(partner(index, dim) if one else index, dim + 1) if two else partner(index, dim))
                    for index in range(BLOCKS)
                ],
            )
            for one, two in ((1, 0), (0, 1), (1, 1))
        ]
        values = (values + others[0]) + (others[1] + others[2])
    return values


def local(
    tokens,
    seq_lengths,
    norm_in,
    proj_gate,
    proj_inner,
    proj_state,
    proj_step,
    conv_inner,
    bias_inner,
    conv_state,
    bias_state,
    step_bias,
    decay_log,
    skip_gain,
    norm_out,
    proj_out,
    cotangent,
):
    width = tokens.shape[1]
    row_count = tokens.shape[0]
    heads_local = proj_step.shape[1]
    inner_local = proj_inner.shape[1]
    state_size = proj_state.shape[1] // 2
    tensor_count = lax.axis_size("tensor")
    inner_total = inner_local * tensor_count
    core = lax.axis_index("tensor").reshape(1)
    blocks = block_order()
    gains = jnp.stack([bias_inner, norm_out])
    norm_row = norm_in[None, :]
    step_t = proj_step.T
    (
        normed,
        gate_raw,
        inner_raw,
        inner_pre,
        mixed,
        scaled_in,
        partial_value,
        row_sums,
        state_raw,
        state_pre,
        maps,
        step_pre,
        cumul,
    ) = forward(
        seq_lengths,
        skip_gain,
        tokens,
        norm_row,
        proj_gate,
        proj_inner,
        proj_state,
        step_t,
        conv_inner,
        gains,
        conv_state,
        bias_state[None, :],
        step_bias[None, :],
        decay_log[None, :],
        proj_out,
        cotangent,
    )
    row_came = swap_tensor(row_sums)
    arranged, *out_halves = out_grad(
        seq_lengths, blocks, row_sums, row_came, cotangent, scaled_in, normed, inner_total
    )

    def first_halving(outs):
        keeps, sends = outs[: len(outs) // 2], outs[len(outs) // 2 :]
        return [[kept, pass_on(sent, flow, 0)] for flow, (kept, sent) in enumerate(zip(keeps, sends))]

    flows_out = first_halving(out_halves)

    def run_backward(origin, after):
        return backward(
            seq_lengths,
            skip_gain,
            row_sums,
            row_came,
            cotangent,
            proj_out,
            gains,
            gate_raw,
            mixed,
            inner_raw,
            inner_pre,
            conv_inner,
            maps,
            step_pre,
            cumul,
            arranged,
            after,
            origin,
            inner_total,
        )

    one = run_backward(0, out_halves[:1])
    flows_one = first_halving(one[6:])
    two = run_backward(FLOWS, [one[6]] + [terms[1] for terms in flows_out])
    flows_two = first_halving(two[6:])
    own, other, grad_step_raw, head_sums = scan_gradients(
        seq_lengths,
        core,
        one[2:5],
        two[2:5],
        maps,
        step_pre,
        decay_log[None, :],
        [terms[1] for terms in flows_one],
    )
    grad_state_part, state_sums = state_gradients(
        seq_lengths, core, own, swap_tensor(other), state_raw, state_pre, conv_state
    )
    side = jnp.concatenate([grad_state_part, grad_step_raw], axis=1)
    side_flows = side.shape[1] // CHUNK
    side_sends = weight_grad(arranged, [side], 1, side, side_flows)
    side_keeps = weight_grad(arranged, [side], 0, side_sends[0], side_flows)
    flows_side = first_halving(side_keeps + side_sends)

    rows = width // 4
    rooms = [inner_local // FLOWS + (CHUNK if flow < side_flows else 0) for flow in range(FLOWS)]
    goes = add_rows(
        [([], [flows_out[flow], flows_one[flow]]) for flow in range(FLOWS)],
        rows,
        rows,
        own,
        rooms=rooms,
    )
    some = add_rows([([], [terms]) for terms in flows_side], rows, rows, into=goes[:side_flows])
    goes = add_rows(
        [([], [terms]) for terms in flows_two], rows, rows, into=[*some, *goes[side_flows:]]
    )
    came = [pass_on(go, flow, 1) for flow, go in enumerate(goes)]
    groups = [[flows_out[flow], flows_one[flow], flows_two[flow]] for flow in range(FLOWS)]
    for flow in range(side_flows):
        groups[flow].append(flows_side[flow])
    stays = add_rows([([], group) for group in groups], 0, rows, goes[0])
    grad_normed, partial_late = normed_grad(
        core,
        one[:2],
        two[:2],
        grad_state_part,
        grad_step_raw,
        proj_gate,
        proj_inner,
        proj_state,
        step_t,
        partial_value,
        [goes[0]],
    )
    grad_tokens, sums = tokens_grad(
        grad_normed,
        swap_tensor(grad_normed),
        tokens,
        cotangent,
        norm_row,
        one[5],
        two[5],
        state_sums,
        head_sums,
    )
    rows = width // 8
    flows = [([], [[stays[flow], came[flow]]]) for flow in range(FLOWS)]
    more = add_rows(flows, rows, rows, grad_normed)
    came_more = [pass_on(go, flow, 2) for flow, go in enumerate(more)]
    stays = add_rows(flows, 0, rows, more[0])
    (left,) = add_rows(
        [([], [[stays[flow], came_more[flow]]]) for flow in range(FLOWS)],
        0,
        rows,
        sums,
        together=True,
    )
    groups = last_groups()
    members = len(groups[0])
    parts = lax.all_to_all(
        left.reshape(members, rows // members, -1),
        ("dp", "tensor"),
        0,
        0,
        axis_index_groups=groups,
    )
    grad_proj_out, grad_proj_gate, grad_proj_inner, grad_proj_state, grad_proj_step = last_rows(
        parts, inner_local, 2 * state_size // tensor_count, heads_local
    )

    block_out = finish_block(
        seq_lengths,
        row_sums,
        row_came,
        partial_late,
        swap_tensor(partial_late),
        tokens,
        inner_total,
    )
    sums = sum_over_dp(sums)
    state_sums = sums[:, inner_local : inner_local + CHUNK]
    head_sums = sums[:, inner_local + CHUNK :]
    grad_norm_in = sums[7, :width]
    grad_norm_out = sums[0, :inner_local]
    grad_skip_gain = jnp.sum(sums[1, :inner_local].reshape(heads_local, -1), axis=1)
    grad_bias_inner = sums[2, :inner_local]
    grad_conv_inner = sums[3:7, :inner_local]
    grad_bias_state = state_sums[0]
    grad_conv_state = state_sums[1:5]
    grad_step_bias = head_sums[0, :heads_local]
    grad_decay_log = head_sums[1, :heads_local]
    return (
        block_out,
        grad_tokens,
        grad_norm_in,
        grad_proj_gate,
        grad_proj_inner,
        grad_proj_state,
        grad_proj_step,
        grad_conv_inner,
        grad_bias_inner,
        grad_conv_state,
        grad_bias_state,
        grad_step_bias,
        grad_decay_log,
        grad_skip_gain,
        grad_norm_out,
        grad_proj_out,
    )


def solution(mesh):
    return jax.shard_map(
        local,
        mesh=mesh,
        in_specs=(
            P("dp", None),
            P("dp", None),
            P(),
            P(None, "tensor"),
            P(None, "tensor"),
            P(),
            P(None, "tensor"),
            P(None, "tensor"),
            P("tensor"),
            P(),
            P(),
            P("tensor"),
            P("tensor"),
            P("tensor"),
            P("tensor"),
            P("tensor", None),
            P("dp", None),
        ),
        out_specs=(
            P("dp", None),
            P("dp", None),
            P(),
            P("dp", "tensor"),
            P("dp", "tensor"),
            P("dp", "tensor"),
            P("dp", "tensor"),
            P(None, "tensor"),
            P("tensor"),
            P(None, "tensor"),
            P("tensor"),
            P("tensor"),
            P("tensor"),
            P("tensor"),
            P("tensor"),
            P("tensor", "dp"),
        ),
        check_vma=False,
    )
```

```python
import functools

import jax
import jax.numpy as jnp
from jax import lax
from jax.experimental import pallas as pl
from jax.experimental.pallas import tpu as pltpu
from jax.sharding import PartitionSpec as P

EPS = 1e-05
FLOWS = 3
DIMS = 6
BLOCKS = 64
TILE = 256
CHUNK = 128
LIMIT = 63 * 1024 * 1024
HINT = 10**6


def cost(flops, bytes_accessed, transcendentals):
    return pl.CostEstimate(
        flops=flops // HINT, bytes_accessed=bytes_accessed // HINT, transcendentals=transcendentals // HINT
    )


def dot(left, right):
    return jnp.dot(left, right, preferred_element_type=jnp.float32)


def thirds(values):
    high = values.astype(jnp.bfloat16)
    rest = values - high.astype(jnp.float32)
    middle = rest.astype(jnp.bfloat16)
    return high, middle, (rest - middle.astype(jnp.float32)).astype(jnp.bfloat16)


def dot_exact(left, right, how=None):
    how = how or dot
    if left.dtype == jnp.bfloat16:
        one, two, three = [how(left, part) for part in thirds(right)]
    else:
        one, two, three = [how(part, right) for part in thirds(left)]
    return one + (two + three)


def dot_first(left, right):
    return lax.dot_general(
        left,
        right,
        (((0,), (0,)), ((), ())),
        preferred_element_type=jnp.float32,
    )


def dot_last(left, right):
    return lax.dot_general(
        left,
        right,
        (((1,), (1,)), ((), ())),
        preferred_element_type=jnp.float32,
    )


def chip_bits(index):
    bits = []
    for place in (4, 2, 0):
        coord = (index >> place) & 3
        bits += [(coord ^ (coord >> 1)) & 1, coord >> 1]
    return bits


def partner(index, dim):
    place = (4, 2, 0)[dim // 2]
    return index ^ ((3 if dim % 2 else 1) << place)


HALVINGS = 3


def flow_dim(core, flow, step):
    return 2 * ((flow + step) % HALVINGS) + (core if step < HALVINGS else 1 - core)


def cube_groups(first, stop):
    groups = []
    for core in range(2):
        lines = {}
        for index in range(BLOCKS):
            bits = chip_bits(index)
            dims = [flow_dim(core, 0, step) for step in range(DIMS)]
            inside = tuple(bits[dim] for dim in dims[first:stop])
            outside = tuple(bits[dim] for dim in dims[:first] + dims[stop:])
            lines.setdefault(outside, []).append((inside, 2 * index + core))
        groups += [[device for _, device in sorted(line)] for line in lines.values()]
    return groups


def flow_pairs(flow, step):
    return [
        (2 * index + core, 2 * partner(index, flow_dim(core, flow, step)) + core)
        for index in range(BLOCKS)
        for core in range(2)
    ]


def swap_tensor(values):
    return lax.ppermute(values, "tensor", [(0, 1), (1, 0)])


def block_order():
    index = lax.axis_index("dp")
    core = lax.axis_index("tensor")
    mine = chip_bits(index)
    place = jnp.arange(BLOCKS, dtype=jnp.int32)
    orders = []
    for flow in range(FLOWS):
        by_core = []
        for which in range(2):
            bits = [None] * DIMS
            for step in range(DIMS):
                dim = flow_dim(which, flow, step)
                bits[dim] = ((place >> (DIMS - 1 - step)) & 1) ^ mine[dim]
            block = jnp.zeros((BLOCKS,), jnp.int32)
            for first in range(0, DIMS, 2):
                high = bits[first + 1]
                block = block * 4 + 2 * high + (bits[first] ^ high)
            by_core.append(block)
        orders.append(jnp.where(core == 0, by_core[0], by_core[1]))
    return jnp.stack(orders)


def ends_of(lengths):
    ends, total = [], 0
    for slot in range(lengths.shape[1]):
        total = total + lengths[0, slot]
        ends.append(total)
    return ends


def segment_of(positions, ends):
    segment = jnp.zeros(positions.shape, jnp.int32)
    for end in ends:
        segment = segment + (positions >= end).astype(jnp.int32)
    return segment


def fill_keeps(keeps, ends):
    rows = lax.broadcasted_iota(jnp.int32, keeps.shape[1:], 0)
    here = segment_of(rows, ends)
    for lag in range(1, keeps.shape[0] + 1):
        same = (segment_of(rows - lag, ends) == here) & (rows >= lag)
        keeps[lag - 1] = same.astype(jnp.float32)


def same_sequence(rows, ends, later):
    first = lax.broadcasted_iota(jnp.int32, (rows, rows), later)
    second = lax.broadcasted_iota(jnp.int32, (rows, rows), 1 - later)
    same = segment_of(first, ends) == segment_of(second, ends)
    return (same & (first >= second)).astype(jnp.float32)


def wide(mask, cols):
    return mask if cols == CHUNK else jnp.concatenate([mask] * (cols // CHUNK), axis=1)


def lagged_rows(values, keeps):
    cols = values.shape[1]
    return [values] + [
        pltpu.roll(values, lag, 0) * wide(keeps[lag - 1], cols)
        for lag in range(1, keeps.shape[0] + 1)
    ]


def conv_forward(lines, taps, bias):
    total = bias + taps[0:1] * lines[0]
    for lag in range(1, len(lines)):
        total = total + taps[lag : lag + 1] * lines[lag]
    return total


def conv_backward(grad_pre, lines, taps, keeps):
    rows, cols = grad_pre.shape
    tap_grads = [jnp.sum(grad_pre * line, axis=0, keepdims=True) for line in lines]
    grad_values = grad_pre * taps[0:1]
    for lag in range(1, len(lines)):
        kept = grad_pre * wide(keeps[lag - 1], cols)
        grad_values = grad_values + pltpu.roll(kept, rows - lag, 0) * taps[lag : lag + 1]
    return jnp.concatenate(tap_grads, axis=0), jnp.sum(grad_pre, axis=0, keepdims=True), grad_values


def by_head(pair):
    lane = lax.broadcasted_iota(jnp.int32, pair.shape, 1)
    none = jnp.zeros_like(pair)
    return jnp.concatenate(
        [jnp.where(lane < CHUNK // 2, pair, none), jnp.where(lane < CHUNK // 2, none, pair)], axis=0
    )


def softplus(values):
    return jnp.maximum(values, 0.0) + jnp.log1p(jnp.exp(-jnp.abs(values)))


def head_row(values, first):
    channel = lax.broadcasted_iota(jnp.int32, (1, TILE), 1)
    row = jnp.zeros((1, TILE), jnp.float32)
    for head in range(TILE // 64):
        row = jnp.where(channel // 64 == head, values[first + head], row)
    return row


def forward_kernel(
    lengths,
    skip,
    tokens,
    norm_in,
    bias_inner,
    norm_out,
    proj_gate,
    proj_inner,
    proj_state,
    proj_step,
    conv_inner,
    conv_state,
    bias_state,
    step_bias,
    decay_log,
    proj_out,
    cotangent,
    normed,
    gate_raw,
    inner_raw,
    mixed,
    scaled,
    partial,
    row_sums,
    state_raw,
    state_pre,
    maps,
    step_pre,
    cumul,
    gains,
    rstd_in,
    keeps,
    scores,
    cum_rows,
    step_rows,
    reach_rows,
    reach_cols,
    square_cols,
    along_cols,
    weights,
    *,
    tiles,
):
    tile = pl.program_id(0)
    rows = tokens.shape[0]
    heads = step_bias.shape[1]
    chunks = rows // CHUNK

    @pl.when(tile == 0)
    def _():
        ends = ends_of(lengths)
        fill_keeps(keeps, ends)
        gains[...] = jnp.zeros(gains.shape, jnp.float32)
        for row, source in enumerate((bias_inner, norm_out, norm_in)):
            for part in range(source.shape[0]):
                gains[row : row + 1, part * CHUNK : (part + 1) * CHUNK] = source[part : part + 1, :]
        for chunk in range(chunks):
            at = slice(chunk * CHUNK, (chunk + 1) * CHUNK)
            hidden = tokens[at, :].astype(jnp.float32)
            rstd = lax.rsqrt(jnp.mean(hidden * hidden, axis=1, keepdims=True) + EPS)
            normed[at, :] = (hidden * rstd * gains[2:3, :]).astype(jnp.bfloat16)
            rstd_in[at, :] = jnp.broadcast_to(rstd, (CHUNK, CHUNK))
        raw = dot(normed[...], proj_state[...])
        state_raw[...] = raw
        pre = conv_forward(lagged_rows(raw, keeps), conv_state, bias_state[...])
        state_pre[...] = pre
        maps[...] = jax.nn.silu(pre).astype(jnp.bfloat16)
        states = maps.shape[1] // 2
        scores[...] = dot_last(maps[:, states:], maps[:, :states]) * same_sequence(rows, ends, 0)
        step_pre[...] = jnp.zeros(step_pre.shape, jnp.float32)
        step_pre[:, :heads] = dot_last(normed[...], proj_step[...]) + step_bias[...]
        steps = softplus(step_pre[...])
        cumul[...] = jnp.zeros(cumul.shape, jnp.float32)
        cumul[:, :heads] = steps[:, :heads] * -jnp.exp(decay_log[...])
        earlier = lax.broadcasted_iota(jnp.int32, (rows, rows), 0) >= lax.broadcasted_iota(
            jnp.int32, (rows, rows), 1
        )
        total = dot_exact(earlier.astype(jnp.bfloat16), cumul[...])
        cumul[...] = total
        total_rows = total.T
        steps_rows = steps.T
        cum_rows[...] = total_rows
        step_rows[...] = steps_rows
        for chunk in range(1, chunks):
            start = chunk * CHUNK
            reach_rows[chunk - 1, :, :start] = (
                jnp.exp(total_rows[:, start - 1 : start] - total_rows[:, :start])
                * steps_rows[:, :start]
            )
            reach_cols[start : start + CHUNK, :] = jnp.exp(
                total[start : start + CHUNK] - total[start - 1 : start]
            )
        square_cols[...] = jnp.zeros(square_cols.shape, jnp.float32)
        along_cols[...] = jnp.zeros(along_cols.shape, jnp.float32)
        weights[...] = jnp.zeros(weights.shape, weights.dtype)

    @pl.when(tile < tiles)
    def _():
        gate = dot(normed[...], proj_gate[...])
        gate_raw[...] = gate
        inner = dot(normed[...], proj_inner[...])
        inner_raw[...] = inner
        here = pl.ds(pl.multiple_of(tile * TILE, TILE), TILE)
        pre = conv_forward(lagged_rows(inner, keeps), conv_inner, gains[0:1, here])
        xconv = jax.nn.silu(pre)
        values = xconv.astype(jnp.bfloat16)
        first = tile * (TILE // 64)
        back = lax.rem(CHUNK - first, CHUNK)
        cum_cols = pltpu.roll(cumul[...], back, 1)
        near_cols = pltpu.roll(reach_cols[...], back, 1)
        skip_row = head_row(skip, first)
        for pair in range(TILE // CHUNK):
            cols = slice(pair * CHUNK, (pair + 1) * CHUNK)
            two = values[:, cols]
            for half in range(2):
                head = 2 * pair + half
                cum_row = cum_rows[pl.ds(first + head, 1), :]
                step_row = step_rows[pl.ds(first + head, 1), :]
                for chunk in range(chunks):
                    start, stop = chunk * CHUNK, (chunk + 1) * CHUNK
                    base = half * rows
                    gap = cum_cols[start:stop, head : head + 1] - cum_row[:, start:stop]
                    weights[pair, start:stop, base + start : base + stop] = (
                        scores[start:stop, start:stop]
                        * (jnp.exp(jnp.minimum(gap, 0.0)) * step_row[:, start:stop])
                    ).astype(jnp.bfloat16)
                    if chunk:
                        reach = reach_rows[chunk - 1, pl.ds(first + head, 1), :][:, :start]
                        weights[pair, start:stop, base : base + start] = (
                            scores[start:stop, :start]
                            * (near_cols[start:stop, head : head + 1] * reach)
                        ).astype(jnp.bfloat16)
            ssd = dot(weights[pair], by_head(two))
            whole = ssd + skip_row[:, cols] * xconv[:, cols]
            mixed[:, cols] = whole
            gated = whole * jax.nn.silu(gate[:, cols])
            square_cols[...] += gated * gated
            place = pl.multiple_of(tile * TILE + pair * CHUNK, CHUNK)
            scaled[:, pl.ds(place, CHUNK)] = (gated * gains[1:2, pl.ds(place, CHUNK)]).astype(jnp.bfloat16)

    @pl.when(tile >= tiles)
    def _():
        part = dot(scaled[...], proj_out[...])
        partial[...] = part
        products = part * cotangent[...].astype(jnp.float32)
        for start in range(0, products.shape[1], CHUNK):
            along_cols[...] += products[:, start : start + CHUNK]

    @pl.when(tile == pl.num_programs(0) - 1)
    def _():
        row_sums[...] = jnp.zeros(row_sums.shape, jnp.float32)
        row_sums[0:1, :] = jnp.sum(square_cols[...].T, axis=0, keepdims=True)
        row_sums[1:2, :] = jnp.sum(along_cols[...].T, axis=0, keepdims=True)


def tile_cols(tile):
    return (0, tile)


def fixed(tile):
    return (0, 0)


def forward(
    lengths,
    skip,
    tokens,
    norm_in,
    bias_inner,
    norm_out,
    proj_gate,
    proj_inner,
    proj_state,
    proj_step,
    conv_inner,
    conv_state,
    bias_state,
    step_bias,
    decay_log,
    proj_out,
    cotangent,
):
    rows, width = tokens.shape
    inner = proj_gate.shape[1]
    taps = conv_inner.shape[0]
    states = proj_state.shape[1]
    heads = proj_step.shape[0]
    f32, bf16 = jnp.float32, jnp.bfloat16
    smem = pl.BlockSpec(memory_space=pltpu.SMEM)

    def whole(*shape):
        return pl.BlockSpec(shape, fixed)

    tiles = inner // TILE

    def strip(count):
        return pl.BlockSpec((count, TILE), lambda tile: (0, jnp.minimum(tile, tiles - 1)))

    def later(count):
        return pl.BlockSpec((count, 2 * TILE), lambda tile: (0, jnp.maximum(tile - tiles, 0)))

    return pl.pallas_call(
        functools.partial(forward_kernel, tiles=tiles),
        grid=(tiles + width // (2 * TILE),),
        in_specs=[
            smem,
            smem,
            whole(rows, width),
            whole(*norm_in.shape),
            whole(*norm_in.shape),
            whole(*norm_in.shape),
            strip(width),
            strip(width),
            whole(width, states),
            whole(heads, width),
            strip(taps),
            whole(taps, states),
            whole(1, states),
            whole(1, heads),
            whole(1, heads),
            later(inner),
            later(rows),
        ],
        out_specs=[
            whole(rows, width),
            strip(rows),
            strip(rows),
            strip(rows),
            whole(rows, inner),
            later(rows),
            whole(8, rows),
            whole(rows, states),
            whole(rows, states),
            whole(rows, states),
            whole(rows, CHUNK),
            whole(rows, CHUNK),
            whole(8, inner),
            whole(rows, CHUNK),
        ],
        out_shape=[
            jax.ShapeDtypeStruct((rows, width), bf16),
            jax.ShapeDtypeStruct((rows, inner), f32),
            jax.ShapeDtypeStruct((rows, inner), f32),
            jax.ShapeDtypeStruct((rows, inner), f32),
            jax.ShapeDtypeStruct((rows, inner), bf16),
            jax.ShapeDtypeStruct((rows, width), f32),
            jax.ShapeDtypeStruct((8, rows), f32),
            jax.ShapeDtypeStruct((rows, states), f32),
            jax.ShapeDtypeStruct((rows, states), f32),
            jax.ShapeDtypeStruct((rows, states), bf16),
            jax.ShapeDtypeStruct((rows, CHUNK), f32),
            jax.ShapeDtypeStruct((rows, CHUNK), f32),
            jax.ShapeDtypeStruct((8, inner), f32),
            jax.ShapeDtypeStruct((rows, CHUNK), f32),
        ],
        scratch_shapes=[
            pltpu.VMEM((taps - 1, rows, CHUNK), f32),
            pltpu.VMEM((rows, rows), f32),
            pltpu.VMEM((CHUNK, rows), f32),
            pltpu.VMEM((CHUNK, rows), f32),
            pltpu.VMEM((rows // CHUNK - 1, CHUNK, rows), f32),
            pltpu.VMEM((rows, CHUNK), f32),
            pltpu.VMEM((rows, CHUNK), f32),
            pltpu.VMEM((rows, CHUNK), f32),
            pltpu.VMEM((TILE // CHUNK, rows, 2 * rows), bf16),
        ],
        compiler_params=pltpu.CompilerParams(vmem_limit_bytes=LIMIT),
        cost_estimate=cost(
            flops=2 * rows * width * (2 * inner + states + heads) + 2 * rows * rows * inner,
            bytes_accessed=4 * width * inner + 18 * rows * inner,
            transcendentals=4 * rows * inner,
        ),
        name="layer_forward",
    )(
        lengths,
        skip,
        tokens,
        norm_in,
        bias_inner,
        norm_out,
        proj_gate,
        proj_inner,
        proj_state,
        proj_step,
        conv_inner,
        conv_state,
        bias_state,
        step_bias,
        decay_log,
        proj_out,
        cotangent,
    )


def scale_row(row_sums, came, lengths, inner_total):
    rstd = lax.rsqrt((row_sums[0:1, :] + came[0:1, :]) / inner_total + EPS)
    rows = lax.broadcasted_iota(jnp.int32, rstd.shape, 1)
    return rstd, (rows < ends_of(lengths)[-1]).astype(jnp.float32)


def turned(values):
    count = values.shape[1]
    row = lax.broadcasted_iota(jnp.int32, (count, count), 0)
    col = lax.broadcasted_iota(jnp.int32, (count, count), 1)
    return dot_last((row == col).astype(jnp.bfloat16), values)


def store_flow(held, sems, flow, count, compute, keeps, sends):
    half = held.shape[1] // 2
    slot = lax.rem(flow, 2)

    def copy_out(which_flow, which):
        to = (keeps, sends)[which][which_flow]
        at = which_flow % 2
        return pltpu.make_async_copy(
            held.at[at, pl.ds(which * half, half)], to, sems.at[at, which]
        )

    for done in range(count - 2):

        @pl.when(flow == done + 2)
        def _(done=done):
            copy_out(done, 0).wait()
            copy_out(done, 1).wait()

    for which in (1, 0):
        compute(slot, slice(which * half, (which + 1) * half))
        for each in range(count):

            @pl.when(flow == each)
            def _(each=each, which=which):
                copy_out(each, which).start()

    @pl.when(flow == count - 1)
    def _():
        for each in (count - 2, count - 1):
            copy_out(each, 0).wait()
            copy_out(each, 1).wait()


def out_grad_kernel(
    lengths,
    blocks,
    row_sums,
    came,
    cotangent,
    scaled,
    normed,
    arranged,
    keep_one,
    keep_two,
    keep_three,
    send_one,
    send_two,
    send_three,
    normed_t,
    cotangent_t,
    grad_projected,
    held,
    sems,
    *,
    inner_total,
    tiles,
):
    step = pl.program_id(0)

    @pl.when(step < tiles)
    def _():
        rstd, valid = scale_row(row_sums, came, lengths, inner_total)
        at = pl.ds(pl.multiple_of(step * TILE, TILE), TILE)
        cotangent_t[at, :] = turned(cotangent[...]) * (rstd * valid)
        normed_t[at, :] = turned(normed[...])

    @pl.when(step >= tiles)
    def _():
        per = normed_t.shape[0] // BLOCKS
        flow = step - tiles
        for place in range(0, BLOCKS, 2):
            at = slice(place * per, (place + 2) * per)
            rows = [
                pl.ds(pl.multiple_of(blocks[flow, place + more] * per, 8), per) for more in range(2)
            ]
            arranged[0, at, :] = jnp.concatenate(
                [normed_t[one, :] for one in rows], axis=0
            ).astype(jnp.bfloat16)
            grad_projected[at, :] = jnp.concatenate(
                [cotangent_t[one, :] for one in rows], axis=0
            ).astype(jnp.bfloat16)

        def compute(slot, at):
            held[slot, at, :] = dot(grad_projected[at, :], scaled[...])

        store_flow(
            held,
            sems,
            flow,
            FLOWS,
            compute,
            (keep_one, keep_two, keep_three),
            (send_one, send_two, send_three),
        )


def out_grad(lengths, blocks, row_sums, came, cotangent, scaled, normed, inner_total):
    rows, width = cotangent.shape
    inner = scaled.shape[1]
    tiles = width // TILE
    share = inner // FLOWS
    smem = pl.BlockSpec(memory_space=pltpu.SMEM)
    row = pl.BlockSpec((8, rows), fixed)
    cols = pl.BlockSpec((rows, TILE), lambda step: (0, jnp.minimum(step, tiles - 1)))
    return pl.pallas_call(
        functools.partial(out_grad_kernel, inner_total=inner_total, tiles=tiles),
        grid=(tiles + FLOWS,),
        in_specs=[
            smem,
            smem,
            row,
            row,
            cols,
            pl.BlockSpec((rows, share), lambda step: (0, jnp.maximum(step - tiles, 0))),
            cols,
        ],
        out_specs=[
            pl.BlockSpec((1, width, rows), lambda step: (jnp.maximum(step - tiles, 0), 0, 0)),
        ]
        + [pl.BlockSpec(memory_space=pl.ANY)] * (2 * FLOWS),
        out_shape=[jax.ShapeDtypeStruct((FLOWS, width, rows), jnp.bfloat16)]
        + [jax.ShapeDtypeStruct((width // 2, share), jnp.float32)] * (2 * FLOWS),
        scratch_shapes=[
            pltpu.VMEM((width, rows), jnp.float32),
            pltpu.VMEM((width, rows), jnp.float32),
            pltpu.VMEM((width, rows), jnp.bfloat16),
            pltpu.VMEM((2, width, share), jnp.float32),
            pltpu.SemaphoreType.DMA((2, 2)),
        ],
        compiler_params=pltpu.CompilerParams(vmem_limit_bytes=LIMIT),
        cost_estimate=cost(
            flops=2 * rows * inner * width,
            bytes_accessed=4 * inner * width + 14 * rows * width,
            transcendentals=0,
        ),
        name="out_grad",
    )(lengths, blocks, row_sums, came, cotangent, scaled, normed)


def backward_kernel(
    lengths,
    skip,
    row_sums,
    came,
    cotangent,
    proj_out,
    gains,
    gate_raw,
    mixed,
    inner_raw,
    conv_inner,
    maps,
    step_pre,
    cumul,
    arranged,
    *rest,
    origin,
    inner_total,
):
    (
        grad_gate,
        grad_inner,
        grad_scores,
        flows,
        sums,
        keep_one,
        keep_two,
        keep_three,
        send_one,
        send_two,
        send_three,
        grad_projected,
        slope_cols,
        keeps,
        scores,
        cum_rows,
        near_rows,
        far_cols,
        step_cols,
        held,
        sems,
        weights,
        both,
    ) = rest[-23:]
    tile = pl.program_id(0)
    rows = cotangent.shape[0]
    chunks = rows // CHUNK

    @pl.when(tile == 0)
    def _():
        ends = ends_of(lengths)
        fill_keeps(keeps, ends)
        rstd, valid = scale_row(row_sums, came, lengths, inner_total)
        slope = (row_sums[1:2, :] + came[1:2, :]) * valid * (rstd * rstd * rstd) / inner_total
        scale_cols = jnp.broadcast_to(rstd * valid, (CHUNK, rows)).T
        slope_cols[...] = jnp.broadcast_to(slope, (CHUNK, rows)).T
        for chunk in range(chunks):
            at = slice(chunk * CHUNK, (chunk + 1) * CHUNK)
            grad_projected[at, :] = (
                cotangent[at, :].astype(jnp.float32) * scale_cols[at, 0:1]
            ).astype(jnp.bfloat16)
        states = maps.shape[1] // 2
        scores[...] = dot_last(maps[:, :states], maps[:, states:]) * same_sequence(rows, ends, 1)
        total = cumul[...]
        total_rows = total.T
        cum_rows[...] = total_rows
        step_cols[...] = softplus(step_pre[...])
        for chunk in range(chunks - 1):
            start, stop = chunk * CHUNK, (chunk + 1) * CHUNK
            near_rows[chunk, :, stop:] = jnp.exp(
                total_rows[:, stop:] - total_rows[:, stop - 1 : stop]
            )
            far_cols[start:stop, :] = jnp.exp(total[stop - 1 : stop] - total[start:stop])
        grad_scores[...] = jnp.zeros(grad_scores.shape, jnp.float32)
        weights[...] = jnp.zeros(weights.shape, weights.dtype)
        flows[...] = jnp.zeros(flows.shape, jnp.float32)

    first = (tile + origin) * (TILE // 64)
    back = lax.rem(CHUNK - first, CHUNK)
    cum_turned = pltpu.roll(cumul[...], back, 1)
    far_turned = pltpu.roll(far_cols[...], back, 1)
    step_turned = pltpu.roll(step_cols[...], back, 1)
    skip_row = head_row(skip, first)
    lane = lax.broadcasted_iota(jnp.int32, (rows, CHUNK), 1)
    grad_scaled = dot_last(grad_projected[...], proj_out[...])
    for pair in range(TILE // CHUNK):
        cols = slice(pair * CHUNK, (pair + 1) * CHUNK)
        raw = gate_raw[:, cols]
        sigma = jax.nn.sigmoid(raw)
        act = raw * sigma
        mix = mixed[:, cols]
        gated = mix * act
        grad_wide = grad_scaled[:, cols]
        sums[0:1, cols] = jnp.sum(grad_wide * gated, axis=0, keepdims=True)
        grad_gated = grad_wide * gains[1:2, cols] - slope_cols[...] * gated
        grad_mixed = grad_gated * act
        gate_grad = (grad_gated * mix * (sigma * (1.0 + raw * (1.0 - sigma)))).astype(jnp.bfloat16)
        grad_gate[:, cols] = gate_grad
        both[:, cols] = gate_grad
        lines = lagged_rows(inner_raw[:, cols], keeps)
        pre = conv_forward(lines, conv_inner[:, cols], gains[0:1, cols])
        sigma = jax.nn.sigmoid(pre)
        xconv = pre * sigma
        sums[1:2, cols] = jnp.sum(grad_mixed * xconv, axis=0, keepdims=True)
        values = xconv.astype(jnp.bfloat16)
        grad_ssd = grad_mixed.astype(jnp.bfloat16)
        middle = rows // 2
        heads_own = by_head(values)
        stacked = jnp.concatenate(
            [
                heads_own[:middle],
                heads_own[rows : rows + middle],
                heads_own[middle:rows],
                heads_own[rows + middle :],
            ],
            axis=0,
        )
        early = dot_last(stacked[:rows], grad_ssd[:middle])
        late = dot_last(stacked, grad_ssd[middle:])
        for half in range(2):
            head = 2 * pair + half
            base = half * rows
            cum_row = cum_rows[pl.ds(first + head, 1), :]
            for chunk in range(chunks):
                start, stop = chunk * CHUNK, (chunk + 1) * CHUNK
                step_col = step_turned[start:stop, head : head + 1]
                cum_col = cum_turned[start:stop, head : head + 1]
                if chunk < chunks - 1:
                    far_step = far_turned[start:stop, head : head + 1] * step_col
                    near_row = near_rows[chunk, pl.ds(first + head, 1), :]
                line = start + half * middle if start < middle else start + (1 + half) * middle
                for other in range(chunk, chunks):
                    begin, end = other * CHUNK, (other + 1) * CHUNK
                    if begin < middle:
                        grad_mix = early[line : line + CHUNK, begin:end]
                    else:
                        grad_mix = late[line : line + CHUNK, begin - middle : end - middle]
                    if other == chunk:
                        gap = cum_row[:, begin:end] - cum_col
                        weighted = jnp.exp(jnp.minimum(gap, 0.0)) * step_col
                    else:
                        weighted = far_step * near_row[:, begin:end]
                    grad_scores[start:stop, begin:end] += grad_mix * weighted
                    weights[pair, start:stop, base + begin : base + end] = (
                        scores[start:stop, begin:end] * weighted
                    ).astype(jnp.bfloat16)
        grad_values = dot(weights[pair], by_head(grad_ssd))
        taken = values.astype(jnp.float32) * grad_values
        given = grad_ssd.astype(jnp.float32) * (mix - skip_row[:, cols] * xconv)
        channel = lax.broadcasted_iota(jnp.int32, (2 * CHUNK, CHUNK), 0)
        target = lax.broadcasted_iota(jnp.int32, (2 * CHUNK, CHUNK), 1)
        head = first + 2 * pair + lax.rem(channel // 64, 2)
        chosen = head + jnp.where(channel < CHUNK, 0, CHUNK // 2) == target
        flows[...] += dot_exact(
            jnp.concatenate([taken, given], axis=1), chosen.astype(jnp.bfloat16)
        )
        grad_xconv = grad_mixed * skip_row[:, cols] + grad_values
        grad_pre = grad_xconv * (sigma * (1.0 + pre * (1.0 - sigma)))
        tap_grads, bias_grad, grad_raw = conv_backward(
            grad_pre, lines, conv_inner[:, cols], keeps
        )
        sums[2:3, cols] = bias_grad
        sums[3:7, cols] = tap_grads
        grad_raw = grad_raw.astype(jnp.bfloat16)
        grad_inner[:, cols] = grad_raw
        both[:, TILE + pair * CHUNK : TILE + (pair + 1) * CHUNK] = grad_raw

    def compute(slot, at):
        held[slot, at, :] = dot(arranged[0, at, :], both[...])

    store_flow(
        held,
        sems,
        tile,
        FLOWS,
        compute,
        (keep_one, keep_two, keep_three),
        (send_one, send_two, send_three),
    )


def backward(
    lengths,
    skip,
    row_sums,
    came,
    cotangent,
    proj_out,
    gains,
    gate_raw,
    mixed,
    inner_raw,
    conv_inner,
    maps,
    step_pre,
    cumul,
    arranged,
    after,
    origin,
    inner_total,
):
    tiles = FLOWS
    rows, width = cotangent.shape
    taps = conv_inner.shape[0]
    states = maps.shape[1]
    f32, bf16 = jnp.float32, jnp.bfloat16
    smem = pl.BlockSpec(memory_space=pltpu.SMEM)

    def whole(*shape):
        return pl.BlockSpec(shape, fixed)

    def strip(count):
        return pl.BlockSpec((count, TILE), lambda tile: (0, tile + origin))

    return pl.pallas_call(
        functools.partial(backward_kernel, origin=origin, inner_total=inner_total),
        grid=(tiles,),
        in_specs=[
            smem,
            smem,
            whole(8, rows),
            whole(8, rows),
            whole(rows, width),
            pl.BlockSpec((TILE, width), lambda tile: (tile + origin, 0)),
            strip(8),
            strip(rows),
            strip(rows),
            strip(rows),
            strip(taps),
            whole(rows, states),
            whole(rows, CHUNK),
            whole(rows, CHUNK),
            pl.BlockSpec((1, width, rows), lambda tile: (tile, 0, 0)),
        ]
        + [pl.BlockSpec(memory_space=pl.ANY)] * len(after),
        out_specs=[
            pl.BlockSpec((rows, TILE), tile_cols),
            pl.BlockSpec((rows, TILE), tile_cols),
            whole(rows, rows),
            whole(rows, CHUNK),
            pl.BlockSpec((8, TILE), tile_cols),
        ]
        + [pl.BlockSpec(memory_space=pl.ANY)] * (2 * FLOWS),
        out_shape=[
            jax.ShapeDtypeStruct((rows, TILE * tiles), bf16),
            jax.ShapeDtypeStruct((rows, TILE * tiles), bf16),
            jax.ShapeDtypeStruct((rows, rows), f32),
            jax.ShapeDtypeStruct((rows, CHUNK), f32),
            jax.ShapeDtypeStruct((8, TILE * tiles), f32),
        ]
        + [jax.ShapeDtypeStruct((width // 2, 2 * TILE), f32)] * (2 * FLOWS),
        scratch_shapes=[
            pltpu.VMEM((rows, width), bf16),
            pltpu.VMEM((rows, CHUNK), f32),
            pltpu.VMEM((taps - 1, rows, CHUNK), f32),
            pltpu.VMEM((rows, rows), f32),
            pltpu.VMEM((CHUNK, rows), f32),
            pltpu.VMEM((rows // CHUNK - 1, CHUNK, rows), f32),
            pltpu.VMEM((rows, CHUNK), f32),
            pltpu.VMEM((rows, CHUNK), f32),
            pltpu.VMEM((2, width, 2 * TILE), f32),
            pltpu.SemaphoreType.DMA((2, 2)),
            pltpu.VMEM((TILE // CHUNK, rows, 2 * rows), bf16),
            pltpu.VMEM((rows, 2 * TILE), bf16),
        ],
        compiler_params=pltpu.CompilerParams(vmem_limit_bytes=LIMIT),
        cost_estimate=cost(
            flops=6 * rows * width * TILE * tiles + 4 * rows * rows * TILE * tiles,
            bytes_accessed=2 * width * TILE * tiles + 20 * rows * TILE * tiles,
            transcendentals=4 * rows * TILE * tiles,
        ),
        name="layer_backward",
    )(
        lengths,
        skip,
        row_sums,
        came,
        cotangent,
        proj_out,
        gains,
        gate_raw,
        mixed,
        inner_raw,
        conv_inner,
        maps,
        step_pre,
        cumul,
        arranged,
        *after,
    )


def scan_kernel(
    lengths,
    core,
    scores_one,
    scores_two,
    flows_one,
    flows_two,
    maps,
    step_pre,
    decay_log,
    *rest,
):
    own, other, grad_step, sums, rates = rest[-5:]
    rows = maps.shape[0]
    states = maps.shape[1] // 2
    heads = decay_log.shape[1]
    grad_scores = (scores_one[...] + scores_two[...]) * same_sequence(rows, ends_of(lengths), 1)
    grad_input = dot_exact(grad_scores, maps[:, states:])
    grad_output = dot_exact(grad_scores, maps[:, :states], dot_first)
    first = core[0] == 0
    own[...] = jnp.where(first, grad_input, grad_output)
    other[...] = jnp.where(first, grad_output, grad_input)
    pre = step_pre[...]
    steps = softplus(pre)
    rates[...] = jnp.zeros(rates.shape, jnp.float32)
    rates[0:1, :heads] = -jnp.exp(decay_log[...])
    rate = rates[0:1, :]
    flows = flows_one[...] + flows_two[...]
    lane = lax.broadcasted_iota(jnp.int32, flows.shape, 1)
    taken = jnp.where(lane < CHUNK // 2, flows, 0.0)
    grad_cum = jnp.where(lane < CHUNK // 2, pltpu.roll(flows, CHUNK // 2, 1) - flows, 0.0)
    later = lax.broadcasted_iota(jnp.int32, (rows, rows), 0) <= lax.broadcasted_iota(
        jnp.int32, (rows, rows), 1
    )
    grad_rate = dot_exact(later.astype(jnp.bfloat16), grad_cum)
    sigma = jax.nn.sigmoid(pre)
    share = jnp.where(pre < -30.0, 1.0, sigma / jnp.maximum(steps, 1e-30))
    grad_pre = taken * share + grad_rate * rate * sigma
    grad_step[...] = grad_pre.astype(jnp.bfloat16)
    sums[...] = jnp.zeros(sums.shape, jnp.float32)
    sums[0:1, :] = jnp.sum(grad_pre, axis=0, keepdims=True)
    sums[1:2, :] = jnp.sum(grad_rate * steps, axis=0, keepdims=True) * rate


def scan_gradients(lengths, core, one, two, maps, step_pre, decay_log, after):
    rows = maps.shape[0]
    states = maps.shape[1] // 2
    vmem = pl.BlockSpec(memory_space=pltpu.VMEM)
    smem = pl.BlockSpec(memory_space=pltpu.SMEM)
    return pl.pallas_call(
        scan_kernel,
        in_specs=[smem, smem] + [vmem] * 7 + [pl.BlockSpec(memory_space=pl.ANY)] * len(after),
        out_specs=[vmem] * 4,
        out_shape=[
            jax.ShapeDtypeStruct((rows, states), jnp.float32),
            jax.ShapeDtypeStruct((rows, states), jnp.float32),
            jax.ShapeDtypeStruct((rows, CHUNK), jnp.bfloat16),
            jax.ShapeDtypeStruct((8, CHUNK), jnp.float32),
        ],
        scratch_shapes=[pltpu.VMEM((8, CHUNK), jnp.float32)],
        compiler_params=pltpu.CompilerParams(vmem_limit_bytes=LIMIT),
        cost_estimate=cost(
            flops=36 * rows * rows * states, bytes_accessed=16 * rows * rows, transcendentals=0
        ),
        name="scan_gradients",
    )(lengths, core, one[0], two[0], one[1], two[1], maps, step_pre, decay_log, *after)


def state_kernel(
    lengths,
    core,
    own,
    came,
    state_raw,
    state_pre,
    conv_state,
    grad_step,
    arranged,
    grad_state,
    sums,
    send_state,
    send_step,
    keep_state,
    keep_step,
    keeps,
):
    flow = pl.program_id(0)
    half = arranged.shape[1] // 2

    @pl.when(flow == 0)
    def _():
        fill_keeps(keeps, ends_of(lengths))
        cols = own.shape[1]
        first = core[0] == 0
        pre = jnp.where(first, state_pre[:, :cols], state_pre[:, cols:])
        raw = jnp.where(first, state_raw[:, :cols], state_raw[:, cols:])
        taps = jnp.where(first, conv_state[:, :cols], conv_state[:, cols:])
        sigma = jax.nn.sigmoid(pre)
        grad_pre = (own[...] + came[...]) * (sigma * (1.0 + pre * (1.0 - sigma)))
        tap_grads, bias_grad, grad_raw = conv_backward(
            grad_pre, lagged_rows(raw, keeps), taps, keeps
        )
        grad_state[...] = grad_raw.astype(jnp.bfloat16)
        sums[...] = jnp.zeros(sums.shape, jnp.float32)
        sums[0:1, :] = bias_grad
        sums[1:5, :] = tap_grads
        send_state[...] = dot(arranged[0, half:], grad_state[...])
        keep_state[...] = dot(arranged[0, :half], grad_state[...])

    @pl.when(flow == 1)
    def _():
        send_step[...] = dot(arranged[0, half:], grad_step[...])
        keep_step[...] = dot(arranged[0, :half], grad_step[...])


def state_gradients(lengths, core, own, came, state_raw, state_pre, conv_state, grad_step, arranged):
    rows, cols = own.shape
    _, width, _ = arranged.shape
    smem = pl.BlockSpec(memory_space=pltpu.SMEM)

    def whole(values):
        return pl.BlockSpec(values.shape, lambda flow: (0, 0))

    half = jax.ShapeDtypeStruct((width // 2, CHUNK), jnp.float32)
    outs = [
        jax.ShapeDtypeStruct((rows, cols), jnp.bfloat16),
        jax.ShapeDtypeStruct((8, cols), jnp.float32),
        half,
        half,
        half,
        half,
    ]
    return pl.pallas_call(
        state_kernel,
        grid=(2,),
        in_specs=[smem, smem]
        + [whole(part) for part in (own, came, state_raw, state_pre, conv_state, grad_step)]
        + [pl.BlockSpec((1, width, rows), lambda flow: (flow, 0, 0))],
        out_specs=[whole(part) for part in outs],
        out_shape=outs,
        scratch_shapes=[pltpu.VMEM((conv_state.shape[0] - 1, rows, CHUNK), jnp.float32)],
        compiler_params=pltpu.CompilerParams(vmem_limit_bytes=LIMIT),
        cost_estimate=cost(
            flops=40 * rows * cols, bytes_accessed=24 * rows * cols, transcendentals=rows * cols
        ),
        name="state_gradients",
    )(lengths, core, own, came, state_raw, state_pre, conv_state, grad_step, arranged)


def add_rows_kernel(*refs, shapes, outs):
    at = 0
    for flow, (joined, counts) in enumerate(shapes):
        wides = refs[at : at + joined]
        at += joined
        out = refs[len(refs) - outs + (flow if outs > 1 else 0)]
        base = sum(cols for before in shapes[:flow] for _, cols in before[1]) if outs == 1 else 0
        start = 0
        for count, cols in counts:
            total = refs[at][...]
            for more in range(1, count):
                total = total + refs[at + more][...]
            for wide_ref in wides:
                if start + cols <= wide_ref.shape[1]:
                    total = total + wide_ref[:, start : start + cols]
            out[:, base + start : base + start + cols] = total
            at += count
            start += cols


def add_rows(flows, start, rows, after=None, together=False):
    parts = 4 if rows >= 192 else 1
    block = rows // parts
    shapes, flat = [], []
    for joined, groups in flows:
        shapes.append((len(joined), tuple((len(group), group[0].shape[1]) for group in groups)))
        flat += list(joined) + [part for group in groups for part in group]
    in_specs = [
        pl.BlockSpec((block, part.shape[1]), lambda part: (start // block + part, 0))
        for part in flat
    ]
    widths = [sum(cols for _, cols in counts) for _, counts in shapes]
    if together:
        widths = [sum(widths)]
    if after is not None:
        flat.append(after)
        in_specs.append(pl.BlockSpec(memory_space=pl.ANY))
    return pl.pallas_call(
        functools.partial(add_rows_kernel, shapes=tuple(shapes), outs=len(widths)),
        grid=(parts,),
        in_specs=in_specs,
        out_specs=[pl.BlockSpec((block, cols), lambda part: (part, 0)) for cols in widths],
        out_shape=[jax.ShapeDtypeStruct((rows, cols), jnp.float32) for cols in widths],
        compiler_params=pltpu.CompilerParams(vmem_limit_bytes=LIMIT),
        cost_estimate=cost(
            flops=rows * sum(widths), bytes_accessed=16 * rows * sum(widths), transcendentals=0
        ),
        name="add_rows",
    )(*flat)


def spread_kernel(one, two, state, head, own, came, held_back, out, same):
    half = one.shape[1]
    width = 2 * half
    for member in range(out.shape[0]):
        out[member, :, :half] = one[...]
        out[member, :, half:width] = two[...]
        out[member, :, width : width + CHUNK] = state[...]
        out[member, :, width + CHUNK :] = head[...]
        out[member, 7:8, :width] = own[...] + came[...]


def spread(one, two, state, head, own, came, members, held_back):
    vmem = pl.BlockSpec(memory_space=pltpu.VMEM)
    shape = (members, 8, 2 * one.shape[1] + 2 * CHUNK)
    return pl.pallas_call(
        spread_kernel,
        in_specs=[vmem] * 6 + [pl.BlockSpec(memory_space=pl.ANY)],
        out_specs=[vmem, pl.BlockSpec(memory_space=pl.ANY)],
        out_shape=[
            jax.ShapeDtypeStruct(shape, jnp.float32),
            jax.ShapeDtypeStruct(held_back.shape, held_back.dtype),
        ],
        input_output_aliases={6: 1},
        compiler_params=pltpu.CompilerParams(vmem_limit_bytes=LIMIT),
        cost_estimate=cost(flops=8 * shape[2], bytes_accessed=4 * 64 * shape[2], transcendentals=0),
        name="spread",
    )(one, two, state, head, own, came, held_back)


def late_sums(refs, count, more):
    flows = [refs[flow * (2 + more) : (flow + 1) * (2 + more)] for flow in range(FLOWS)]
    totals = []
    for terms in flows:
        total = terms[0][...]
        for term in terms[1:]:
            total = total + term[...]
        totals.append(total)
    small, lines = refs[count], refs[count + 1 : count + 1 + 2 * more]
    total = small[0]
    for member in range(1, small.shape[0]):
        total = total + small[member]
    for upper, lower in zip(lines[::2], lines[1::2]):
        cols = upper.shape[1]
        total = total + jnp.concatenate([upper[...], lower[:, : total.shape[1] - cols]], axis=1)
    return totals, total


def late_specs(stays, came, later, small, rows, index, after=None):
    flat = []
    for flow in range(FLOWS):
        flat += [stays[flow], came[flow]] + [parts[flow] for parts in later]
    specs = [pl.BlockSpec((rows, part.shape[1]), lambda _: (index, 0)) for part in flat]
    specs.append(pl.BlockSpec(small.shape, lambda _: (0, 0, 0)))
    for parts in later:
        last = parts[0].shape[0] // 8
        for place in (last - 2, last - 1):
            specs.append(pl.BlockSpec((8, parts[0].shape[1]), lambda _, place=place: (place, 0)))
    flat += [small] + [parts[0] for parts in later for _ in range(2)]
    if after is not None:
        flat.append(after)
        specs.append(pl.BlockSpec(memory_space=pl.ANY))
    return flat, specs


def go_kernel(*refs, count, more):
    outs = refs[-FLOWS:]
    totals, small = late_sums(refs, count, more)
    for flow, total in enumerate(totals):
        rows, cols = total.shape
        outs[flow][:rows, :] = total
        if flow == 0:
            outs[0][rows : rows + 8, :] = small[:, :cols]
            outs[0][rows + 8 :, : small.shape[1] - cols] = small[:, cols:]
            outs[0][rows + 8 :, small.shape[1] - cols :] = jnp.zeros(
                (8, 2 * cols - small.shape[1]), jnp.float32
            )


def go_rows(stays, came, later, small, rows, after):
    flat, specs = late_specs(stays, came, later, small, rows, 1, after)
    shapes = [
        (rows + (16 if flow == 0 else 0), stays[flow].shape[1]) for flow in range(FLOWS)
    ]
    return pl.pallas_call(
        functools.partial(go_kernel, count=FLOWS * (2 + len(later)), more=len(later)),
        grid=(1,),
        in_specs=specs,
        out_specs=[pl.BlockSpec(shape, fixed) for shape in shapes],
        out_shape=[jax.ShapeDtypeStruct(shape, jnp.float32) for shape in shapes],
        compiler_params=pltpu.CompilerParams(vmem_limit_bytes=LIMIT),
        cost_estimate=cost(flops=rows, bytes_accessed=rows, transcendentals=0),
        name="go_rows",
    )(*flat)


def last_rows_kernel(*refs, count, more):
    totals, sums = late_sums(refs, count, more)
    (
        out_grad_out,
        out_gate,
        out_inner,
        out_state,
        out_step,
        out_norm_in,
        out_conv_inner,
        out_bias_inner,
        out_conv_state,
        out_bias_state,
        out_step_bias,
        out_decay,
        out_skip,
        out_norm_out,
    ) = refs[-14:]
    share = out_grad_out.shape[1] // FLOWS
    for flow, total in enumerate(totals):
        out_grad_out[:, flow * share : (flow + 1) * share] = total[:, :share]
        start = share
        for group in range(2):
            first = (group * FLOWS + flow) * TILE
            out_gate[:, first : first + TILE] = total[:, start : start + TILE]
            out_inner[:, first : first + TILE] = total[:, start + TILE : start + 2 * TILE]
            start += 2 * TILE
        if flow < 2:
            side = (out_state, out_step)[flow]
            side[...] = total[:, start : start + side.shape[1]]
    inner = out_gate.shape[1]
    for out, row in ((out_norm_out, 0), (out_bias_inner, 2), (out_norm_in, 7)):
        for part in range(out.shape[0]):
            out[part : part + 1, :] = sums[row : row + 1, part * CHUNK : (part + 1) * CHUNK]
    out_conv_inner[...] = sums[3:7, :inner]
    out_bias_state[...] = sums[0:1, inner : inner + CHUNK]
    out_conv_state[...] = sums[1:5, inner : inner + CHUNK]
    heads = out_skip.shape[1]
    out_step_bias[...] = sums[0:1, inner + CHUNK : inner + CHUNK + heads]
    out_decay[...] = sums[1:2, inner + CHUNK : inner + CHUNK + heads]
    channel = lax.broadcasted_iota(jnp.int32, (inner, CHUNK), 0)
    target = lax.broadcasted_iota(jnp.int32, (inner, CHUNK), 1)
    by_head_sums = dot_exact(sums[:, :inner], (channel // 64 == target).astype(jnp.bfloat16))
    out_skip[...] = by_head_sums[1:2, :heads]


def last_rows(stays, came, later, small, rows, inner, states, heads, taps):
    flat, specs = late_specs(stays, came, later, small, rows, 0)
    vector = (inner // CHUNK, CHUNK)
    outs = [(rows, inner), (rows, inner), (rows, inner), (rows, states), (rows, heads)]
    outs += [vector, (taps, inner), vector, (taps, states), (1, states)]
    outs += [(1, heads), (1, heads), (1, heads), vector]
    return pl.pallas_call(
        functools.partial(last_rows_kernel, count=FLOWS * (2 + len(later)), more=len(later)),
        grid=(1,),
        in_specs=specs,
        out_specs=[pl.BlockSpec(shape, fixed) for shape in outs],
        out_shape=[jax.ShapeDtypeStruct(shape, jnp.float32) for shape in outs],
        compiler_params=pltpu.CompilerParams(vmem_limit_bytes=LIMIT),
        cost_estimate=cost(
            flops=8 * rows * inner, bytes_accessed=80 * rows * inner, transcendentals=0
        ),
        name="last_rows",
    )(*flat)


def normed_grad_kernel(
    core, gate_one, inner_one, gate_two, inner_two, state, step, gate, inner, proj_state, proj_step, tokens, rstd_in, partial, *rest
):
    out, norm_row = rest[-3], rest[-1]
    tile = pl.program_id(0)
    half = gate_one.shape[1]
    states = state.shape[1]
    heads = proj_step.shape[0]
    total = dot_last(gate_one[...], gate[:, :half]) + dot_last(inner_one[...], inner[:, :half])
    total = total + dot_last(gate_two[...], gate[:, half:]) + dot_last(inner_two[...], inner[:, half:])
    chosen = jnp.where(core[0] == 0, proj_state[:, :states], proj_state[:, states:])
    total = total + dot_last(state[...], chosen) + dot(step[:, :heads], proj_step[...])
    out[...] = total
    scaled = total * tokens[...].astype(jnp.float32) * wide(rstd_in[...], TILE)
    here = pl.ds(pl.multiple_of(tile * TILE, TILE), TILE)
    norm_row[0:1, here] = jnp.sum(scaled, axis=0, keepdims=True)


def normed_grad(
    core, one, two, state, step, proj_gate, proj_inner, proj_state, proj_step, tokens, rstd_in, partial, after
):
    rows = state.shape[0]
    width, inner = proj_gate.shape

    def whole(values):
        return pl.BlockSpec(values.shape, fixed)

    def lines(values):
        return pl.BlockSpec((TILE, values.shape[1]), lambda tile: (tile, 0))

    return pl.pallas_call(
        normed_grad_kernel,
        grid=(width // TILE,),
        in_specs=[pl.BlockSpec(memory_space=pltpu.SMEM)]
        + [whole(part) for part in (*one, *two, state, step)]
        + [lines(proj_gate), lines(proj_inner), lines(proj_state)]
        + [pl.BlockSpec((proj_step.shape[0], TILE), tile_cols)]
        + [pl.BlockSpec((rows, TILE), tile_cols), whole(rstd_in)]
        + [pl.BlockSpec(memory_space=pl.ANY)] * (1 + len(after)),
        out_specs=[
            pl.BlockSpec((rows, TILE), tile_cols),
            pl.BlockSpec(memory_space=pl.ANY),
            pl.BlockSpec((1, width), fixed),
        ],
        out_shape=[jax.ShapeDtypeStruct((rows, width), jnp.float32)] * 2
        + [jax.ShapeDtypeStruct((1, width), jnp.float32)],
        input_output_aliases={13: 1},
        compiler_params=pltpu.CompilerParams(vmem_limit_bytes=LIMIT),
        cost_estimate=cost(
            flops=4 * rows * inner * width,
            bytes_accessed=4 * inner * width + 8 * rows * width,
            transcendentals=0,
        ),
        name="normed_grad",
    )(
        core,
        *one,
        *two,
        state,
        step,
        proj_gate,
        proj_inner,
        proj_state,
        proj_step,
        tokens,
        rstd_in,
        partial,
        *after,
    )


def tokens_grad_kernel(
    own, came, tokens, cotangent, gains, grad_tokens
):
    hidden = tokens[...].astype(jnp.float32)
    rstd = lax.rsqrt(jnp.mean(hidden * hidden, axis=1, keepdims=True) + EPS)
    grad_normed = own[...] + came[...]
    weighted = grad_normed * gains[2:3, :]
    back = jnp.mean(weighted * hidden, axis=1, keepdims=True)
    grad_hidden = rstd * weighted - hidden * (rstd * rstd * rstd * back)
    grad_tokens[...] = (cotangent[...].astype(jnp.float32) + grad_hidden).astype(jnp.bfloat16)


def tokens_grad(own, came, tokens, cotangent, gains):
    rows, width = tokens.shape
    lines = pl.BlockSpec((CHUNK, width), lambda step: (step, 0))

    return pl.pallas_call(
        tokens_grad_kernel,
        grid=(rows // CHUNK,),
        in_specs=[lines] * 4 + [pl.BlockSpec(gains.shape, fixed)],
        out_specs=lines,
        out_shape=jax.ShapeDtypeStruct((rows, width), jnp.bfloat16),
        compiler_params=pltpu.CompilerParams(vmem_limit_bytes=LIMIT),
        cost_estimate=cost(
            flops=12 * rows * width, bytes_accessed=14 * rows * width, transcendentals=0
        ),
        name="tokens_grad",
    )(own, came, tokens, cotangent, gains)


def block_out_kernel(
    lengths, row_sums, row_came, own, came, tokens, out, cols, *, inner_total
):
    step = pl.program_id(0)

    @pl.when(step == 0)
    def _():
        rstd, valid = scale_row(row_sums, row_came, lengths, inner_total)
        cols[...] = jnp.broadcast_to(rstd * valid, (CHUNK, rstd.shape[1])).T

    scale = cols[pl.ds(pl.multiple_of(step * CHUNK, CHUNK), CHUNK), 0:1]
    out[...] = (tokens[...].astype(jnp.float32) + scale * (own[...] + came[...])).astype(
        jnp.bfloat16
    )


def finish_block(lengths, row_sums, row_came, own, came, tokens, inner_total):
    rows, width = tokens.shape
    lines = pl.BlockSpec((CHUNK, width), lambda step: (step, 0))
    row = pl.BlockSpec((8, rows), fixed)
    return pl.pallas_call(
        functools.partial(block_out_kernel, inner_total=inner_total),
        grid=(rows // CHUNK,),
        in_specs=[pl.BlockSpec(memory_space=pltpu.SMEM), row, row, lines, lines, lines],
        out_specs=lines,
        out_shape=jax.ShapeDtypeStruct((rows, width), jnp.bfloat16),
        scratch_shapes=[pltpu.VMEM((rows, CHUNK), jnp.float32)],
        compiler_params=pltpu.CompilerParams(vmem_limit_bytes=LIMIT),
        cost_estimate=cost(
            flops=3 * rows * width, bytes_accessed=12 * rows * width, transcendentals=0
        ),
        name="block_out",
    )(lengths, row_sums, row_came, own, came, tokens)


def pass_on(part, flow, step):
    return lax.ppermute(part, ("dp", "tensor"), flow_pairs(flow, step))


def local(
    tokens,
    seq_lengths,
    norm_in,
    proj_gate,
    proj_inner,
    proj_state,
    proj_step,
    conv_inner,
    bias_inner,
    conv_state,
    bias_state,
    step_bias,
    decay_log,
    skip_gain,
    norm_out,
    proj_out,
    cotangent,
):
    width = tokens.shape[1]
    row_count = tokens.shape[0]
    heads_local = proj_step.shape[1]
    inner_local = proj_inner.shape[1]
    state_size = proj_state.shape[1] // 2
    tensor_count = lax.axis_size("tensor")
    inner_total = inner_local * tensor_count
    core = lax.axis_index("tensor").reshape(1)
    blocks = block_order()
    step_t = proj_step.T
    (
        normed,
        gate_raw,
        inner_raw,
        mixed,
        scaled_in,
        partial_value,
        row_sums,
        state_raw,
        state_pre,
        maps,
        step_pre,
        cumul,
        gains,
        rstd_in,
    ) = forward(
        seq_lengths,
        skip_gain,
        tokens,
        norm_in.reshape(-1, CHUNK),
        bias_inner.reshape(-1, CHUNK),
        norm_out.reshape(-1, CHUNK),
        proj_gate,
        proj_inner,
        proj_state,
        step_t,
        conv_inner,
        conv_state,
        bias_state[None, :],
        step_bias[None, :],
        decay_log[None, :],
        proj_out,
        cotangent,
    )
    row_came = swap_tensor(row_sums)
    arranged, *out_halves = out_grad(
        seq_lengths, blocks, row_sums, row_came, cotangent, scaled_in, normed, inner_total
    )

    def first_halving(outs):
        keeps, sends = outs[: len(outs) // 2], outs[len(outs) // 2 :]
        return [[kept, pass_on(sent, flow, 0)] for flow, (kept, sent) in enumerate(zip(keeps, sends))]

    flows_out = first_halving(out_halves)

    def run_backward(origin, after):
        return backward(
            seq_lengths,
            skip_gain,
            row_sums,
            row_came,
            cotangent,
            proj_out,
            gains,
            gate_raw,
            mixed,
            inner_raw,
            conv_inner,
            maps,
            step_pre,
            cumul,
            arranged,
            after,
            origin,
            inner_total,
        )

    one = run_backward(0, out_halves[:1])
    flows_one = first_halving(one[5:])
    two = run_backward(FLOWS, [one[5]] + [terms[1] for terms in flows_out])
    flows_two = first_halving(two[5:])
    own, other, grad_step_raw, head_sums = scan_gradients(
        seq_lengths,
        core,
        one[2:4],
        two[2:4],
        maps,
        step_pre,
        decay_log[None, :],
        [terms[1] for terms in flows_one],
    )
    grad_state_part, state_sums, *side_halves = state_gradients(
        seq_lengths,
        core,
        own,
        swap_tensor(other),
        state_raw,
        state_pre,
        conv_state,
        grad_step_raw,
        arranged,
    )
    flows_side = first_halving(side_halves[2:] + side_halves[:2])
    side_flows = len(flows_side)

    rows = width // 4
    groups = [[flows_out[flow], flows_one[flow], flows_two[flow]] for flow in range(FLOWS)]
    for flow in range(side_flows):
        groups[flow].append(flows_side[flow])
    goes = add_rows([([], group) for group in groups], rows, rows)
    came = [pass_on(go, flow, 1) for flow, go in enumerate(goes)]
    stays = add_rows([([], group) for group in groups], 0, rows, goes[0])
    grad_normed, partial_late, norm_row = normed_grad(
        core,
        one[:2],
        two[:2],
        grad_state_part,
        grad_step_raw,
        proj_gate,
        proj_inner,
        proj_state,
        step_t,
        tokens,
        rstd_in,
        partial_value,
        [goes[0]],
    )
    members = 1 << HALVINGS
    spread_sums, grad_normed = spread(
        one[4], two[4], state_sums, head_sums, norm_row, swap_tensor(norm_row), members, grad_normed
    )
    grad_tokens = tokens_grad(grad_normed, swap_tensor(grad_normed), tokens, cotangent, gains)
    small = lax.all_to_all(
        spread_sums,
        ("dp", "tensor"),
        0,
        0,
        axis_index_groups=cube_groups(0, HALVINGS),
    )
    rows = width // 8
    flows = [([], [[stays[flow], came[flow]]]) for flow in range(FLOWS)]
    more = add_rows(flows, rows, rows, spread_sums)
    came_more = [pass_on(go, flow, 2) for flow, go in enumerate(more)]
    stays = add_rows(flows, 0, rows, more[0])
    block_out = finish_block(
        seq_lengths,
        row_sums,
        row_came,
        partial_late,
        swap_tensor(partial_late),
        tokens,
        inner_total,
    )
    later = []
    for step in range(HALVINGS, DIMS):
        rows = width >> (step + 1)
        after = (None, block_out, grad_tokens)[step - HALVINGS]
        goes = go_rows(stays, came_more, later, small, rows, after)
        later.append([pass_on(go, flow, step) for flow, go in enumerate(goes)])
    (
        grad_proj_out,
        grad_proj_gate,
        grad_proj_inner,
        grad_proj_state,
        grad_proj_step,
        grad_norm_in,
        grad_conv_inner,
        grad_bias_inner,
        grad_conv_state,
        grad_bias_state,
        grad_step_bias,
        grad_decay_log,
        grad_skip_gain,
        grad_norm_out,
    ) = last_rows(
        stays,
        came_more,
        later,
        small,
        width // BLOCKS,
        inner_local,
        2 * state_size // tensor_count,
        heads_local,
        conv_inner.shape[0],
    )

    return (
        block_out,
        grad_tokens,
        grad_norm_in.reshape(-1),
        grad_proj_gate,
        grad_proj_inner,
        grad_proj_state,
        grad_proj_step,
        grad_conv_inner,
        grad_bias_inner.reshape(-1),
        grad_conv_state,
        grad_bias_state.reshape(-1),
        grad_step_bias.reshape(-1),
        grad_decay_log.reshape(-1),
        grad_skip_gain.reshape(-1),
        grad_norm_out.reshape(-1),
        grad_proj_out.T,
    )


def solution(mesh):
    return jax.shard_map(
        local,
        mesh=mesh,
        in_specs=(
            P("dp", None),
            P("dp", None),
            P(),
            P(None, "tensor"),
            P(None, "tensor"),
            P(),
            P(None, "tensor"),
            P(None, "tensor"),
            P("tensor"),
            P(),
            P(),
            P("tensor"),
            P("tensor"),
            P("tensor"),
            P("tensor"),
            P("tensor", None),
            P("dp", None),
        ),
        out_specs=(
            P("dp", None),
            P("dp", None),
            P(),
            P("dp", "tensor"),
            P("dp", "tensor"),
            P("dp", "tensor"),
            P("dp", "tensor"),
            P(None, "tensor"),
            P("tensor"),
            P(None, "tensor"),
            P("tensor"),
            P("tensor"),
            P("tensor"),
            P("tensor"),
            P("tensor"),
            P("tensor", "dp"),
        ),
        check_vma=False,
    )
```

```python
import functools

import jax
import jax.numpy as jnp
from jax import lax
from jax.experimental import pallas as pl
from jax.experimental.pallas import tpu as pltpu
from jax.sharding import PartitionSpec as P

EPS = 1e-05
FLOWS = 3
DIMS = 6
BLOCKS = 64
TILE = 256
WIDE = 512
CHUNK = 128
LIMIT = 65400 * 1024
HINT = 10**6


def cost(flops, bytes_accessed, transcendentals):
    return pl.CostEstimate(
        flops=flops // HINT, bytes_accessed=bytes_accessed // HINT, transcendentals=transcendentals // HINT
    )


def dot(left, right):
    return jnp.dot(left, right, preferred_element_type=jnp.float32)


def thirds(values):
    high = values.astype(jnp.bfloat16)
    rest = values - high.astype(jnp.float32)
    middle = rest.astype(jnp.bfloat16)
    return high, middle, (rest - middle.astype(jnp.float32)).astype(jnp.bfloat16)


def dot_exact(left, right, how=None):
    how = how or dot
    if left.dtype == jnp.bfloat16:
        one, two, three = [how(left, part) for part in thirds(right)]
    else:
        one, two, three = [how(part, right) for part in thirds(left)]
    return one + (two + three)


def dot_first(left, right):
    return lax.dot_general(
        left,
        right,
        (((0,), (0,)), ((), ())),
        preferred_element_type=jnp.float32,
    )


def dot_last(left, right):
    return lax.dot_general(
        left,
        right,
        (((1,), (1,)), ((), ())),
        preferred_element_type=jnp.float32,
    )


def chip_bits(index):
    bits = []
    for place in (4, 2, 0):
        coord = (index >> place) & 3
        bits += [(coord ^ (coord >> 1)) & 1, coord >> 1]
    return bits


def partner(index, dim):
    place = (4, 2, 0)[dim // 2]
    return index ^ ((3 if dim % 2 else 1) << place)


HALVINGS = 3


def flow_dim(core, flow, step):
    return 2 * ((flow + step) % HALVINGS) + (core if step < HALVINGS else 1 - core)


def cube_groups(first, stop):
    groups = []
    for core in range(2):
        lines = {}
        for index in range(BLOCKS):
            bits = chip_bits(index)
            dims = [flow_dim(core, 0, step) for step in range(DIMS)]
            inside = tuple(bits[dim] for dim in dims[first:stop])
            outside = tuple(bits[dim] for dim in dims[:first] + dims[stop:])
            lines.setdefault(outside, []).append((inside, 2 * index + core))
        groups += [[device for _, device in sorted(line)] for line in lines.values()]
    return groups


def flow_pairs(flow, step):
    return [
        (2 * index + core, 2 * partner(index, flow_dim(core, flow, step)) + core)
        for index in range(BLOCKS)
        for core in range(2)
    ]


def swap_tensor(values):
    return lax.ppermute(values, "tensor", [(0, 1), (1, 0)])


def block_order():
    index = lax.axis_index("dp")
    core = lax.axis_index("tensor")
    mine = chip_bits(index)
    place = jnp.arange(BLOCKS, dtype=jnp.int32)
    orders = []
    for flow in range(FLOWS):
        by_core = []
        for which in range(2):
            bits = [None] * DIMS
            for step in range(DIMS):
                dim = flow_dim(which, flow, step)
                bits[dim] = ((place >> (DIMS - 1 - step)) & 1) ^ mine[dim]
            block = jnp.zeros((BLOCKS,), jnp.int32)
            for first in range(0, DIMS, 2):
                high = bits[first + 1]
                block = block * 4 + 2 * high + (bits[first] ^ high)
            by_core.append(block)
        orders.append(jnp.where(core == 0, by_core[0], by_core[1]))
    return jnp.stack(orders)


def ends_of(lengths):
    ends, total = [], 0
    for slot in range(lengths.shape[1]):
        total = total + lengths[0, slot]
        ends.append(total)
    return ends


def segment_of(positions, ends):
    segment = jnp.zeros(positions.shape, jnp.int32)
    for end in ends:
        segment = segment + (positions >= end).astype(jnp.int32)
    return segment


def fill_keeps(keeps, ends):
    rows = lax.broadcasted_iota(jnp.int32, keeps.shape[1:], 0)
    here = segment_of(rows, ends)
    for lag in range(1, keeps.shape[0] + 1):
        same = (segment_of(rows - lag, ends) == here) & (rows >= lag)
        keeps[lag - 1] = same.astype(jnp.float32)


def same_sequence(rows, ends, later):
    first = lax.broadcasted_iota(jnp.int32, (rows, rows), later)
    second = lax.broadcasted_iota(jnp.int32, (rows, rows), 1 - later)
    same = segment_of(first, ends) == segment_of(second, ends)
    return (same & (first >= second)).astype(jnp.float32)


def wide(mask, cols):
    return mask if cols == CHUNK else jnp.concatenate([mask] * (cols // CHUNK), axis=1)


def lagged_rows(values, keeps):
    cols = values.shape[1]
    return [values] + [
        pltpu.roll(values, lag, 0) * wide(keeps[lag - 1], cols)
        for lag in range(1, keeps.shape[0] + 1)
    ]


def conv_forward(lines, taps, bias):
    total = bias + taps[0:1] * lines[0]
    for lag in range(1, len(lines)):
        total = total + taps[lag : lag + 1] * lines[lag]
    return total


def conv_backward(grad_pre, lines, taps, keeps):
    rows, cols = grad_pre.shape
    tap_grads = [jnp.sum(grad_pre * line, axis=0, keepdims=True) for line in lines]
    grad_values = grad_pre * taps[0:1]
    for lag in range(1, len(lines)):
        kept = grad_pre * wide(keeps[lag - 1], cols)
        grad_values = grad_values + pltpu.roll(kept, rows - lag, 0) * taps[lag : lag + 1]
    return jnp.concatenate(tap_grads, axis=0), jnp.sum(grad_pre, axis=0, keepdims=True), grad_values


def by_head(pair):
    lane = lax.broadcasted_iota(jnp.int32, pair.shape, 1)
    none = jnp.zeros_like(pair)
    return jnp.concatenate(
        [jnp.where(lane < CHUNK // 2, pair, none), jnp.where(lane < CHUNK // 2, none, pair)], axis=0
    )


def softplus(values):
    return jnp.maximum(values, 0.0) + jnp.log1p(jnp.exp(-jnp.abs(values)))


def head_row(values, first, count):
    channel = lax.broadcasted_iota(jnp.int32, (1, count), 1)
    row = jnp.zeros((1, count), jnp.float32)
    for head in range(count // 64):
        row = jnp.where(channel // 64 == head, values[first + head], row)
    return row


def forward_kernel(
    lengths,
    skip,
    tokens,
    norm_in,
    bias_inner,
    norm_out,
    proj_gate,
    proj_inner,
    proj_state,
    proj_step,
    conv_inner,
    conv_state,
    bias_state,
    step_bias,
    decay_log,
    proj_out,
    cotangent,
    normed,
    gate_raw,
    inner_raw,
    mixed,
    scaled,
    partial,
    row_sums,
    state_raw,
    state_pre,
    maps,
    step_pre,
    cumul,
    gains,
    rstd_in,
    keeps,
    scores,
    cum_rows,
    step_rows,
    reach_rows,
    reach_cols,
    square_cols,
    along_cols,
    weights,
    proj_in,
    cotangent_in,
    late_sems,
    early_in,
    early_sems,
    *,
    tiles,
):
    tile = pl.program_id(0)
    now = lax.rem(tile, 2)

    def early(which, slot):
        here = pl.ds(pl.multiple_of(which * WIDE, WIDE), WIDE)
        return [
            pltpu.make_async_copy(source.at[:, here], early_in.at[slot, at], early_sems.at[slot, at])
            for at, source in enumerate((proj_gate, proj_inner))
        ]

    @pl.when(tile == 0)
    def _():
        for copy in early(0, 0) + early(1, 1):
            copy.start()

    @pl.when((tile > 0) & (tile + 1 < tiles))
    def _():
        for copy in early(tile + 1, 1 - now):
            copy.start()

    def late(part):
        here = pl.ds(part * WIDE, WIDE)
        slot = part % 2
        return (
            pltpu.make_async_copy(proj_out.at[:, here], proj_in.at[slot], late_sems.at[slot, 0]),
            pltpu.make_async_copy(
                cotangent.at[:, here], cotangent_in.at[slot], late_sems.at[slot, 1]
            ),
        )

    for part in range(2):

        @pl.when(tile == tiles - 2 + part)
        def _(part=part):
            for copy in late(part):
                copy.start()

    rows = tokens.shape[0]
    heads = step_bias.shape[1]
    chunks = rows // CHUNK

    @pl.when(tile == 0)
    def _():
        ends = ends_of(lengths)
        fill_keeps(keeps, ends)
        gains[...] = jnp.zeros(gains.shape, jnp.float32)
        for row, source in enumerate((bias_inner, norm_out, norm_in)):
            for part in range(source.shape[0]):
                gains[row : row + 1, part * CHUNK : (part + 1) * CHUNK] = source[part : part + 1, :]
        for chunk in range(chunks):
            at = slice(chunk * CHUNK, (chunk + 1) * CHUNK)
            hidden = tokens[at, :].astype(jnp.float32)
            rstd = lax.rsqrt(jnp.mean(hidden * hidden, axis=1, keepdims=True) + EPS)
            normed[at, :] = (hidden * rstd * gains[2:3, :]).astype(jnp.bfloat16)
            rstd_in[at, :] = jnp.broadcast_to(rstd, (CHUNK, CHUNK))
        raw = dot(normed[...], proj_state[...])
        state_raw[...] = raw
        pre = conv_forward(lagged_rows(raw, keeps), conv_state, bias_state[...])
        state_pre[...] = pre
        maps[...] = jax.nn.silu(pre).astype(jnp.bfloat16)
        states = maps.shape[1] // 2
        scores[...] = dot_last(maps[:, states:], maps[:, :states]) * same_sequence(rows, ends, 0)
        step_pre[...] = jnp.zeros(step_pre.shape, jnp.float32)
        step_pre[:, :heads] = dot_last(normed[...], proj_step[...]) + step_bias[...]
        steps = softplus(step_pre[...])
        cumul[...] = jnp.zeros(cumul.shape, jnp.float32)
        cumul[:, :heads] = steps[:, :heads] * -jnp.exp(decay_log[...])
        earlier = lax.broadcasted_iota(jnp.int32, (rows, rows), 0) >= lax.broadcasted_iota(
            jnp.int32, (rows, rows), 1
        )
        total = dot_exact(earlier.astype(jnp.bfloat16), cumul[...])
        cumul[...] = total
        total_rows = total.T
        steps_rows = steps.T
        cum_rows[...] = total_rows
        step_rows[...] = steps_rows
        for chunk in range(1, chunks):
            start = chunk * CHUNK
            reach_rows[chunk - 1, :, :start] = (
                jnp.exp(total_rows[:, start - 1 : start] - total_rows[:, :start])
                * steps_rows[:, :start]
            )
            reach_cols[start : start + CHUNK, :] = jnp.exp(
                total[start : start + CHUNK] - total[start - 1 : start]
            )
        square_cols[...] = jnp.zeros(square_cols.shape, jnp.float32)
        along_cols[...] = jnp.zeros(along_cols.shape, jnp.float32)
        weights[...] = jnp.zeros(weights.shape, weights.dtype)

    @pl.when(tile < tiles)
    def _():
        for copy in early(tile, now):
            copy.wait()
        gate = dot(normed[...], early_in[now, 0])
        gate_raw[...] = gate
        inner = dot(normed[...], early_in[now, 1])
        inner_raw[...] = inner
        here = pl.ds(pl.multiple_of(tile * WIDE, WIDE), WIDE)
        pre = conv_forward(lagged_rows(inner, keeps), conv_inner, gains[0:1, here])
        xconv = jax.nn.silu(pre)
        values = xconv.astype(jnp.bfloat16)
        first = tile * (WIDE // 64)
        back = lax.rem(CHUNK - first, CHUNK)
        cum_cols = pltpu.roll(cumul[...], back, 1)
        near_cols = pltpu.roll(reach_cols[...], back, 1)
        skip_row = head_row(skip, first, WIDE)
        for pair in range(WIDE // CHUNK):
            cols = slice(pair * CHUNK, (pair + 1) * CHUNK)
            two = values[:, cols]
            for half in range(2):
                head = 2 * pair + half
                cum_row = cum_rows[pl.ds(first + head, 1), :]
                step_row = step_rows[pl.ds(first + head, 1), :]
                for chunk in range(chunks):
                    start, stop = chunk * CHUNK, (chunk + 1) * CHUNK
                    base = half * rows
                    gap = cum_cols[start:stop, head : head + 1] - cum_row[:, start:stop]
                    weights[pair, start:stop, base + start : base + stop] = (
                        scores[start:stop, start:stop]
                        * (jnp.exp(jnp.minimum(gap, 0.0)) * step_row[:, start:stop])
                    ).astype(jnp.bfloat16)
                    if chunk:
                        reach = reach_rows[chunk - 1, pl.ds(first + head, 1), :][:, :start]
                        weights[pair, start:stop, base : base + start] = (
                            scores[start:stop, :start]
                            * (near_cols[start:stop, head : head + 1] * reach)
                        ).astype(jnp.bfloat16)
            ssd = dot(weights[pair], by_head(two))
            whole = ssd + skip_row[:, cols] * xconv[:, cols]
            mixed[:, cols] = whole
            gated = whole * jax.nn.silu(gate[:, cols])
            square_cols[...] += gated * gated
            place = pl.multiple_of(tile * WIDE + pair * CHUNK, CHUNK)
            scaled[:, pl.ds(place, CHUNK)] = (gated * gains[1:2, pl.ds(place, CHUNK)]).astype(jnp.bfloat16)

    for part in range(proj_out.shape[1] // WIDE):

        @pl.when(tile == tiles + part)
        def _(part=part):
            slot = part % 2
            for copy in late(part):
                copy.wait()
            projected = dot(scaled[...], proj_in[slot])
            partial[...] = projected
            products = projected * cotangent_in[slot].astype(jnp.float32)
            for start in range(0, WIDE, CHUNK):
                along_cols[...] += products[:, start : start + CHUNK]
            if part + 2 < proj_out.shape[1] // WIDE:
                for copy in late(part + 2):
                    copy.start()

    @pl.when(tile == pl.num_programs(0) - 1)
    def _():
        row_sums[...] = jnp.zeros(row_sums.shape, jnp.float32)
        row_sums[0:1, :] = jnp.sum(square_cols[...].T, axis=0, keepdims=True)
        row_sums[1:2, :] = jnp.sum(along_cols[...].T, axis=0, keepdims=True)


def tile_cols(tile):
    return (0, tile)


def fixed(tile):
    return (0, 0)


def forward(
    lengths,
    skip,
    tokens,
    norm_in,
    bias_inner,
    norm_out,
    proj_gate,
    proj_inner,
    proj_state,
    proj_step,
    conv_inner,
    conv_state,
    bias_state,
    step_bias,
    decay_log,
    proj_out,
    cotangent,
):
    rows, width = tokens.shape
    inner = proj_gate.shape[1]
    taps = conv_inner.shape[0]
    states = proj_state.shape[1]
    heads = proj_step.shape[0]
    f32, bf16 = jnp.float32, jnp.bfloat16
    smem = pl.BlockSpec(memory_space=pltpu.SMEM)

    def whole(*shape):
        return pl.BlockSpec(shape, fixed)

    tiles = inner // WIDE

    def strip(count):
        return pl.BlockSpec((count, WIDE), lambda tile: (0, jnp.minimum(tile, tiles - 1)))

    def later(count):
        return pl.BlockSpec((count, WIDE), lambda tile: (0, jnp.maximum(tile - tiles, 0)))

    return pl.pallas_call(
        functools.partial(forward_kernel, tiles=tiles),
        grid=(tiles + width // (WIDE),),
        in_specs=[
            smem,
            smem,
            whole(rows, width),
            whole(*norm_in.shape),
            whole(*norm_in.shape),
            whole(*norm_in.shape),
            pl.BlockSpec(memory_space=pl.ANY),
            pl.BlockSpec(memory_space=pl.ANY),
            whole(width, states),
            whole(heads, width),
            strip(taps),
            whole(taps, states),
            whole(1, states),
            whole(1, heads),
            whole(1, heads),
            pl.BlockSpec(memory_space=pl.ANY),
            pl.BlockSpec(memory_space=pl.ANY),
        ],
        out_specs=[
            whole(rows, width),
            strip(rows),
            strip(rows),
            strip(rows),
            whole(rows, inner),
            later(rows),
            whole(8, rows),
            whole(rows, states),
            whole(rows, states),
            whole(rows, states),
            whole(rows, CHUNK),
            whole(rows, CHUNK),
            whole(8, inner),
            whole(rows, CHUNK),
        ],
        out_shape=[
            jax.ShapeDtypeStruct((rows, width), bf16),
            jax.ShapeDtypeStruct((rows, inner), f32),
            jax.ShapeDtypeStruct((rows, inner), f32),
            jax.ShapeDtypeStruct((rows, inner), f32),
            jax.ShapeDtypeStruct((rows, inner), bf16),
            jax.ShapeDtypeStruct((rows, width), f32),
            jax.ShapeDtypeStruct((8, rows), f32),
            jax.ShapeDtypeStruct((rows, states), f32),
            jax.ShapeDtypeStruct((rows, states), f32),
            jax.ShapeDtypeStruct((rows, states), bf16),
            jax.ShapeDtypeStruct((rows, CHUNK), f32),
            jax.ShapeDtypeStruct((rows, CHUNK), f32),
            jax.ShapeDtypeStruct((8, inner), f32),
            jax.ShapeDtypeStruct((rows, CHUNK), f32),
        ],
        scratch_shapes=[
            pltpu.VMEM((taps - 1, rows, CHUNK), f32),
            pltpu.VMEM((rows, rows), f32),
            pltpu.VMEM((CHUNK, rows), f32),
            pltpu.VMEM((CHUNK, rows), f32),
            pltpu.VMEM((rows // CHUNK - 1, CHUNK, rows), f32),
            pltpu.VMEM((rows, CHUNK), f32),
            pltpu.VMEM((rows, CHUNK), f32),
            pltpu.VMEM((rows, CHUNK), f32),
            pltpu.VMEM((WIDE // CHUNK, rows, 2 * rows), bf16),
            pltpu.VMEM((2, inner, WIDE), bf16),
            pltpu.VMEM((2, rows, WIDE), bf16),
            pltpu.SemaphoreType.DMA((2, 2)),
            pltpu.VMEM((2, 2, width, WIDE), bf16),
            pltpu.SemaphoreType.DMA((2, 2)),
        ],
        compiler_params=pltpu.CompilerParams(vmem_limit_bytes=LIMIT),
        cost_estimate=cost(
            flops=2 * rows * width * (2 * inner + states + heads) + 2 * rows * rows * inner,
            bytes_accessed=4 * width * inner + 18 * rows * inner,
            transcendentals=4 * rows * inner,
        ),
        name="layer_forward",
    )(
        lengths,
        skip,
        tokens,
        norm_in,
        bias_inner,
        norm_out,
        proj_gate,
        proj_inner,
        proj_state,
        proj_step,
        conv_inner,
        conv_state,
        bias_state,
        step_bias,
        decay_log,
        proj_out,
        cotangent,
    )


def scale_row(row_sums, came, lengths, inner_total):
    rstd = lax.rsqrt((row_sums[0:1, :] + came[0:1, :]) / inner_total + EPS)
    rows = lax.broadcasted_iota(jnp.int32, rstd.shape, 1)
    return rstd, (rows < ends_of(lengths)[-1]).astype(jnp.float32)


def turned(values):
    count = values.shape[1]
    row = lax.broadcasted_iota(jnp.int32, (count, count), 0)
    col = lax.broadcasted_iota(jnp.int32, (count, count), 1)
    return dot_last((row == col).astype(jnp.bfloat16), values)


def store_flow(held, sems, flow, count, compute, keeps, sends):
    half = held.shape[1] // 2
    slot = lax.rem(flow, 2)

    def copy_out(which_flow, which):
        to = (keeps, sends)[which][which_flow]
        at = which_flow % 2
        return pltpu.make_async_copy(
            held.at[at, pl.ds(which * half, half)], to, sems.at[at, which]
        )

    for done in range(count - 2):

        @pl.when(flow == done + 2)
        def _(done=done):
            copy_out(done, 0).wait()
            copy_out(done, 1).wait()

    for which in (1, 0):
        compute(slot, slice(which * half, (which + 1) * half))
        for each in range(count):

            @pl.when(flow == each)
            def _(each=each, which=which):
                copy_out(each, which).start()

    @pl.when(flow == count - 1)
    def _():
        for each in (count - 2, count - 1):
            copy_out(each, 0).wait()
            copy_out(each, 1).wait()


def out_grad_kernel(
    lengths,
    blocks,
    row_sums,
    came,
    cotangent,
    scaled,
    normed,
    arranged,
    keep_one,
    keep_two,
    keep_three,
    send_one,
    send_two,
    send_three,
    normed_t,
    cotangent_t,
    grad_projected,
    held,
    sems,
    *,
    inner_total,
    tiles,
):
    step = pl.program_id(0)

    @pl.when(step < tiles)
    def _():
        rstd, valid = scale_row(row_sums, came, lengths, inner_total)
        for part in range(WIDE // TILE):
            at = pl.ds(pl.multiple_of(step * WIDE + part * TILE, TILE), TILE)
            here = slice(part * TILE, (part + 1) * TILE)
            cotangent_t[at, :] = turned(cotangent[:, here]) * (rstd * valid)
            normed_t[at, :] = turned(normed[:, here])

    @pl.when(step >= tiles)
    def _():
        per = normed_t.shape[0] // BLOCKS
        flow = step - tiles
        for place in range(0, BLOCKS, 2):
            at = slice(place * per, (place + 2) * per)
            rows = [
                pl.ds(pl.multiple_of(blocks[flow, place + more] * per, 8), per) for more in range(2)
            ]
            arranged[0, at, :] = jnp.concatenate(
                [normed_t[one, :] for one in rows], axis=0
            ).astype(jnp.bfloat16)
            grad_projected[at, :] = jnp.concatenate(
                [cotangent_t[one, :] for one in rows], axis=0
            ).astype(jnp.bfloat16)

        def compute(slot, at):
            held[slot, at, :] = dot(grad_projected[at, :], scaled[...])

        store_flow(
            held,
            sems,
            flow,
            FLOWS,
            compute,
            (keep_one, keep_two, keep_three),
            (send_one, send_two, send_three),
        )


def out_grad(lengths, blocks, row_sums, came, cotangent, scaled, normed, inner_total):
    rows, width = cotangent.shape
    inner = scaled.shape[1]
    tiles = width // WIDE
    share = inner // FLOWS
    smem = pl.BlockSpec(memory_space=pltpu.SMEM)
    row = pl.BlockSpec((8, rows), fixed)
    cols = pl.BlockSpec((rows, WIDE), lambda step: (0, jnp.minimum(step, tiles - 1)))
    return pl.pallas_call(
        functools.partial(out_grad_kernel, inner_total=inner_total, tiles=tiles),
        grid=(tiles + FLOWS,),
        in_specs=[
            smem,
            smem,
            row,
            row,
            cols,
            pl.BlockSpec((rows, share), lambda step: (0, jnp.maximum(step - tiles, 0))),
            cols,
        ],
        out_specs=[
            pl.BlockSpec((1, width, rows), lambda step: (jnp.maximum(step - tiles, 0), 0, 0)),
        ]
        + [pl.BlockSpec(memory_space=pl.ANY)] * (2 * FLOWS),
        out_shape=[jax.ShapeDtypeStruct((FLOWS, width, rows), jnp.bfloat16)]
        + [jax.ShapeDtypeStruct((width // 2, share), jnp.float32)] * (2 * FLOWS),
        scratch_shapes=[
            pltpu.VMEM((width, rows), jnp.float32),
            pltpu.VMEM((width, rows), jnp.float32),
            pltpu.VMEM((width, rows), jnp.bfloat16),
            pltpu.VMEM((2, width, share), jnp.float32),
            pltpu.SemaphoreType.DMA((2, 2)),
        ],
        compiler_params=pltpu.CompilerParams(vmem_limit_bytes=LIMIT),
        cost_estimate=cost(
            flops=2 * rows * inner * width,
            bytes_accessed=4 * inner * width + 14 * rows * width,
            transcendentals=0,
        ),
        name="out_grad",
    )(lengths, blocks, row_sums, came, cotangent, scaled, normed)


def backward_kernel(
    lengths,
    skip,
    row_sums,
    came,
    cotangent,
    proj_out,
    gains,
    gate_raw,
    mixed,
    inner_raw,
    conv_inner,
    maps,
    step_pre,
    cumul,
    arranged,
    *rest,
    origin,
    inner_total,
):
    (
        grad_gate,
        grad_inner,
        grad_scores,
        flows,
        sums,
        keep_one,
        keep_two,
        keep_three,
        send_one,
        send_two,
        send_three,
        grad_projected,
        slope_cols,
        keeps,
        scores,
        cum_rows,
        near_rows,
        far_cols,
        step_cols,
        held,
        sems,
        weights,
        both,
        lines_in,
        lines_sem,
    ) = rest[-25:]
    tile = pl.program_id(0)
    fetch = pltpu.make_async_copy(arranged.at[tile], lines_in, lines_sem)
    fetch.start()
    rows = cotangent.shape[0]
    chunks = rows // CHUNK

    @pl.when(tile == 0)
    def _():
        ends = ends_of(lengths)
        fill_keeps(keeps, ends)
        rstd, valid = scale_row(row_sums, came, lengths, inner_total)
        slope = (row_sums[1:2, :] + came[1:2, :]) * valid * (rstd * rstd * rstd) / inner_total
        scale_cols = jnp.broadcast_to(rstd * valid, (CHUNK, rows)).T
        slope_cols[...] = jnp.broadcast_to(slope, (CHUNK, rows)).T
        for chunk in range(chunks):
            at = slice(chunk * CHUNK, (chunk + 1) * CHUNK)
            grad_projected[at, :] = (
                cotangent[at, :].astype(jnp.float32) * scale_cols[at, 0:1]
            ).astype(jnp.bfloat16)
        states = maps.shape[1] // 2
        scores[...] = dot_last(maps[:, :states], maps[:, states:]) * same_sequence(rows, ends, 1)
        total = cumul[...]
        total_rows = total.T
        cum_rows[...] = total_rows
        step_cols[...] = softplus(step_pre[...])
        for chunk in range(chunks - 1):
            start, stop = chunk * CHUNK, (chunk + 1) * CHUNK
            near_rows[chunk, :, stop:] = jnp.exp(
                total_rows[:, stop:] - total_rows[:, stop - 1 : stop]
            )
            far_cols[start:stop, :] = jnp.exp(total[stop - 1 : stop] - total[start:stop])
        grad_scores[...] = jnp.zeros(grad_scores.shape, jnp.float32)
        weights[...] = jnp.zeros(weights.shape, weights.dtype)
        flows[...] = jnp.zeros(flows.shape, jnp.float32)

    first = (tile + origin) * (TILE // 64)
    back = lax.rem(CHUNK - first, CHUNK)
    cum_turned = pltpu.roll(cumul[...], back, 1)
    far_turned = pltpu.roll(far_cols[...], back, 1)
    step_turned = pltpu.roll(step_cols[...], back, 1)
    skip_row = head_row(skip, first, TILE)
    lane = lax.broadcasted_iota(jnp.int32, (rows, CHUNK), 1)
    grad_scaled = dot_last(grad_projected[...], proj_out[...])
    for pair in range(TILE // CHUNK):
        cols = slice(pair * CHUNK, (pair + 1) * CHUNK)
        raw = gate_raw[:, cols]
        sigma = jax.nn.sigmoid(raw)
        act = raw * sigma
        mix = mixed[:, cols]
        gated = mix * act
        grad_wide = grad_scaled[:, cols]
        sums[0:1, cols] = jnp.sum(grad_wide * gated, axis=0, keepdims=True)
        grad_gated = grad_wide * gains[1:2, cols] - slope_cols[...] * gated
        grad_mixed = grad_gated * act
        gate_grad = (grad_gated * mix * (sigma * (1.0 + raw * (1.0 - sigma)))).astype(jnp.bfloat16)
        grad_gate[:, cols] = gate_grad
        both[:, cols] = gate_grad
        lines = lagged_rows(inner_raw[:, cols], keeps)
        pre = conv_forward(lines, conv_inner[:, cols], gains[0:1, cols])
        sigma = jax.nn.sigmoid(pre)
        xconv = pre * sigma
        sums[1:2, cols] = jnp.sum(grad_mixed * xconv, axis=0, keepdims=True)
        values = xconv.astype(jnp.bfloat16)
        grad_ssd = grad_mixed.astype(jnp.bfloat16)
        middle = rows // 2
        heads_own = by_head(values)
        stacked = jnp.concatenate(
            [
                heads_own[:middle],
                heads_own[rows : rows + middle],
                heads_own[middle:rows],
                heads_own[rows + middle :],
            ],
            axis=0,
        )
        early = dot_last(stacked[:rows], grad_ssd[:middle])
        late = dot_last(stacked, grad_ssd[middle:])
        for half in range(2):
            head = 2 * pair + half
            base = half * rows
            cum_row = cum_rows[pl.ds(first + head, 1), :]
            for chunk in range(chunks):
                start, stop = chunk * CHUNK, (chunk + 1) * CHUNK
                step_col = step_turned[start:stop, head : head + 1]
                cum_col = cum_turned[start:stop, head : head + 1]
                if chunk < chunks - 1:
                    far_step = far_turned[start:stop, head : head + 1] * step_col
                    near_row = near_rows[chunk, pl.ds(first + head, 1), :]
                line = start + half * middle if start < middle else start + (1 + half) * middle
                for other in range(chunk, chunks):
                    begin, end = other * CHUNK, (other + 1) * CHUNK
                    if begin < middle:
                        grad_mix = early[line : line + CHUNK, begin:end]
                    else:
                        grad_mix = late[line : line + CHUNK, begin - middle : end - middle]
                    if other == chunk:
                        gap = cum_row[:, begin:end] - cum_col
                        weighted = jnp.exp(jnp.minimum(gap, 0.0)) * step_col
                    else:
                        weighted = far_step * near_row[:, begin:end]
                    grad_scores[start:stop, begin:end] += grad_mix * weighted
                    weights[pair, start:stop, base + begin : base + end] = (
                        scores[start:stop, begin:end] * weighted
                    ).astype(jnp.bfloat16)
        grad_values = dot(weights[pair], by_head(grad_ssd))
        taken = values.astype(jnp.float32) * grad_values
        given = grad_ssd.astype(jnp.float32) * (mix - skip_row[:, cols] * xconv)
        channel = lax.broadcasted_iota(jnp.int32, (2 * CHUNK, CHUNK), 0)
        target = lax.broadcasted_iota(jnp.int32, (2 * CHUNK, CHUNK), 1)
        head = first + 2 * pair + lax.rem(channel // 64, 2)
        chosen = head + jnp.where(channel < CHUNK, 0, CHUNK // 2) == target
        flows[...] += dot_exact(
            jnp.concatenate([taken, given], axis=1), chosen.astype(jnp.bfloat16)
        )
        grad_xconv = grad_mixed * skip_row[:, cols] + grad_values
        grad_pre = grad_xconv * (sigma * (1.0 + pre * (1.0 - sigma)))
        tap_grads, bias_grad, grad_raw = conv_backward(
            grad_pre, lines, conv_inner[:, cols], keeps
        )
        sums[2:3, cols] = bias_grad
        sums[3:7, cols] = tap_grads
        grad_raw = grad_raw.astype(jnp.bfloat16)
        grad_inner[:, cols] = grad_raw
        both[:, TILE + pair * CHUNK : TILE + (pair + 1) * CHUNK] = grad_raw

    def compute(slot, at):
        held[slot, at, :] = dot(lines_in[at, :], both[...])

    fetch.wait()
    store_flow(
        held,
        sems,
        tile,
        FLOWS,
        compute,
        (keep_one, keep_two, keep_three),
        (send_one, send_two, send_three),
    )


def backward(
    lengths,
    skip,
    row_sums,
    came,
    cotangent,
    proj_out,
    gains,
    gate_raw,
    mixed,
    inner_raw,
    conv_inner,
    maps,
    step_pre,
    cumul,
    arranged,
    after,
    origin,
    inner_total,
):
    tiles = FLOWS
    rows, width = cotangent.shape
    taps = conv_inner.shape[0]
    states = maps.shape[1]
    f32, bf16 = jnp.float32, jnp.bfloat16
    smem = pl.BlockSpec(memory_space=pltpu.SMEM)

    def whole(*shape):
        return pl.BlockSpec(shape, fixed)

    def strip(count):
        return pl.BlockSpec((count, TILE), lambda tile: (0, tile + origin))

    return pl.pallas_call(
        functools.partial(backward_kernel, origin=origin, inner_total=inner_total),
        grid=(tiles,),
        in_specs=[
            smem,
            smem,
            whole(8, rows),
            whole(8, rows),
            whole(rows, width),
            pl.BlockSpec((TILE, width), lambda tile: (tile + origin, 0)),
            strip(8),
            strip(rows),
            strip(rows),
            strip(rows),
            strip(taps),
            whole(rows, states),
            whole(rows, CHUNK),
            whole(rows, CHUNK),
            pl.BlockSpec(memory_space=pl.ANY),
        ]
        + [pl.BlockSpec(memory_space=pl.ANY)] * len(after),
        out_specs=[
            pl.BlockSpec((rows, TILE), tile_cols),
            pl.BlockSpec((rows, TILE), tile_cols),
            whole(rows, rows),
            whole(rows, CHUNK),
            pl.BlockSpec((8, TILE), tile_cols),
        ]
        + [pl.BlockSpec(memory_space=pl.ANY)] * (2 * FLOWS),
        out_shape=[
            jax.ShapeDtypeStruct((rows, TILE * tiles), bf16),
            jax.ShapeDtypeStruct((rows, TILE * tiles), bf16),
            jax.ShapeDtypeStruct((rows, rows), f32),
            jax.ShapeDtypeStruct((rows, CHUNK), f32),
            jax.ShapeDtypeStruct((8, TILE * tiles), f32),
        ]
        + [jax.ShapeDtypeStruct((width // 2, 2 * TILE), f32)] * (2 * FLOWS),
        scratch_shapes=[
            pltpu.VMEM((rows, width), bf16),
            pltpu.VMEM((rows, CHUNK), f32),
            pltpu.VMEM((taps - 1, rows, CHUNK), f32),
            pltpu.VMEM((rows, rows), f32),
            pltpu.VMEM((CHUNK, rows), f32),
            pltpu.VMEM((rows // CHUNK - 1, CHUNK, rows), f32),
            pltpu.VMEM((rows, CHUNK), f32),
            pltpu.VMEM((rows, CHUNK), f32),
            pltpu.VMEM((2, width, 2 * TILE), f32),
            pltpu.SemaphoreType.DMA((2, 2)),
            pltpu.VMEM((TILE // CHUNK, rows, 2 * rows), bf16),
            pltpu.VMEM((rows, 2 * TILE), bf16),
            pltpu.VMEM((width, rows), bf16),
            pltpu.SemaphoreType.DMA(()),
        ],
        compiler_params=pltpu.CompilerParams(vmem_limit_bytes=LIMIT),
        cost_estimate=cost(
            flops=6 * rows * width * TILE * tiles + 4 * rows * rows * TILE * tiles,
            bytes_accessed=2 * width * TILE * tiles + 20 * rows * TILE * tiles,
            transcendentals=4 * rows * TILE * tiles,
        ),
        name="layer_backward",
    )(
        lengths,
        skip,
        row_sums,
        came,
        cotangent,
        proj_out,
        gains,
        gate_raw,
        mixed,
        inner_raw,
        conv_inner,
        maps,
        step_pre,
        cumul,
        arranged,
        *after,
    )


def scan_kernel(
    lengths,
    core,
    scores_one,
    scores_two,
    flows_one,
    flows_two,
    maps,
    step_pre,
    decay_log,
    *rest,
):
    own, other, grad_step, sums, rates = rest[-5:]
    rows = maps.shape[0]
    states = maps.shape[1] // 2
    heads = decay_log.shape[1]
    grad_scores = (scores_one[...] + scores_two[...]) * same_sequence(rows, ends_of(lengths), 1)
    grad_input = dot_exact(grad_scores, maps[:, states:])
    grad_output = dot_exact(grad_scores, maps[:, :states], dot_first)
    first = core[0] == 0
    own[...] = jnp.where(first, grad_input, grad_output)
    other[...] = jnp.where(first, grad_output, grad_input)
    pre = step_pre[...]
    steps = softplus(pre)
    rates[...] = jnp.zeros(rates.shape, jnp.float32)
    rates[0:1, :heads] = -jnp.exp(decay_log[...])
    rate = rates[0:1, :]
    flows = flows_one[...] + flows_two[...]
    lane = lax.broadcasted_iota(jnp.int32, flows.shape, 1)
    taken = jnp.where(lane < CHUNK // 2, flows, 0.0)
    grad_cum = jnp.where(lane < CHUNK // 2, pltpu.roll(flows, CHUNK // 2, 1) - flows, 0.0)
    later = lax.broadcasted_iota(jnp.int32, (rows, rows), 0) <= lax.broadcasted_iota(
        jnp.int32, (rows, rows), 1
    )
    grad_rate = dot_exact(later.astype(jnp.bfloat16), grad_cum)
    sigma = jax.nn.sigmoid(pre)
    share = jnp.where(pre < -30.0, 1.0, sigma / jnp.maximum(steps, 1e-30))
    grad_pre = taken * share + grad_rate * rate * sigma
    grad_step[...] = grad_pre.astype(jnp.bfloat16)
    sums[...] = jnp.zeros(sums.shape, jnp.float32)
    sums[0:1, :] = jnp.sum(grad_pre, axis=0, keepdims=True)
    sums[1:2, :] = jnp.sum(grad_rate * steps, axis=0, keepdims=True) * rate


def scan_gradients(lengths, core, one, two, maps, step_pre, decay_log, after):
    rows = maps.shape[0]
    states = maps.shape[1] // 2
    vmem = pl.BlockSpec(memory_space=pltpu.VMEM)
    smem = pl.BlockSpec(memory_space=pltpu.SMEM)
    return pl.pallas_call(
        scan_kernel,
        in_specs=[smem, smem] + [vmem] * 7 + [pl.BlockSpec(memory_space=pl.ANY)] * len(after),
        out_specs=[vmem] * 4,
        out_shape=[
            jax.ShapeDtypeStruct((rows, states), jnp.float32),
            jax.ShapeDtypeStruct((rows, states), jnp.float32),
            jax.ShapeDtypeStruct((rows, CHUNK), jnp.bfloat16),
            jax.ShapeDtypeStruct((8, CHUNK), jnp.float32),
        ],
        scratch_shapes=[pltpu.VMEM((8, CHUNK), jnp.float32)],
        compiler_params=pltpu.CompilerParams(vmem_limit_bytes=LIMIT),
        cost_estimate=cost(
            flops=36 * rows * rows * states, bytes_accessed=16 * rows * rows, transcendentals=0
        ),
        name="scan_gradients",
    )(lengths, core, one[0], two[0], one[1], two[1], maps, step_pre, decay_log, *after)


def state_kernel(
    lengths,
    core,
    own,
    came,
    state_raw,
    state_pre,
    conv_state,
    grad_step,
    arranged,
    grad_state,
    sums,
    send_state,
    send_step,
    keep_state,
    keep_step,
    keeps,
):
    flow = pl.program_id(0)
    half = arranged.shape[1] // 2

    @pl.when(flow == 0)
    def _():
        fill_keeps(keeps, ends_of(lengths))
        cols = own.shape[1]
        first = core[0] == 0
        pre = jnp.where(first, state_pre[:, :cols], state_pre[:, cols:])
        raw = jnp.where(first, state_raw[:, :cols], state_raw[:, cols:])
        taps = jnp.where(first, conv_state[:, :cols], conv_state[:, cols:])
        sigma = jax.nn.sigmoid(pre)
        grad_pre = (own[...] + came[...]) * (sigma * (1.0 + pre * (1.0 - sigma)))
        tap_grads, bias_grad, grad_raw = conv_backward(
            grad_pre, lagged_rows(raw, keeps), taps, keeps
        )
        grad_state[...] = grad_raw.astype(jnp.bfloat16)
        sums[...] = jnp.zeros(sums.shape, jnp.float32)
        sums[0:1, :] = bias_grad
        sums[1:5, :] = tap_grads
        send_state[...] = dot(arranged[0, half:], grad_state[...])
        keep_state[...] = dot(arranged[0, :half], grad_state[...])

    @pl.when(flow == 1)
    def _():
        send_step[...] = dot(arranged[0, half:], grad_step[...])
        keep_step[...] = dot(arranged[0, :half], grad_step[...])


def state_gradients(lengths, core, own, came, state_raw, state_pre, conv_state, grad_step, arranged):
    rows, cols = own.shape
    _, width, _ = arranged.shape
    smem = pl.BlockSpec(memory_space=pltpu.SMEM)

    def whole(values):
        return pl.BlockSpec(values.shape, lambda flow: (0, 0))

    half = jax.ShapeDtypeStruct((width // 2, CHUNK), jnp.float32)
    outs = [
        jax.ShapeDtypeStruct((rows, cols), jnp.bfloat16),
        jax.ShapeDtypeStruct((8, cols), jnp.float32),
        half,
        half,
        half,
        half,
    ]
    return pl.pallas_call(
        state_kernel,
        grid=(2,),
        in_specs=[smem, smem]
        + [whole(part) for part in (own, came, state_raw, state_pre, conv_state, grad_step)]
        + [pl.BlockSpec((1, width, rows), lambda flow: (flow, 0, 0))],
        out_specs=[whole(part) for part in outs],
        out_shape=outs,
        scratch_shapes=[pltpu.VMEM((conv_state.shape[0] - 1, rows, CHUNK), jnp.float32)],
        compiler_params=pltpu.CompilerParams(vmem_limit_bytes=LIMIT),
        cost_estimate=cost(
            flops=40 * rows * cols, bytes_accessed=24 * rows * cols, transcendentals=rows * cols
        ),
        name="state_gradients",
    )(lengths, core, own, came, state_raw, state_pre, conv_state, grad_step, arranged)


def add_rows_kernel(*refs, shapes, outs):
    at = 0
    for flow, (joined, counts) in enumerate(shapes):
        wides = refs[at : at + joined]
        at += joined
        out = refs[len(refs) - outs + (flow if outs > 1 else 0)]
        base = sum(cols for before in shapes[:flow] for _, cols in before[1]) if outs == 1 else 0
        start = 0
        for count, cols in counts:
            total = refs[at][...]
            for more in range(1, count):
                total = total + refs[at + more][...]
            for wide_ref in wides:
                if start + cols <= wide_ref.shape[1]:
                    total = total + wide_ref[:, start : start + cols]
            out[:, base + start : base + start + cols] = total
            at += count
            start += cols


def add_rows(flows, start, rows, after=None, together=False):
    parts = 4 if rows >= 192 else 1
    block = rows // parts
    shapes, flat = [], []
    for joined, groups in flows:
        shapes.append((len(joined), tuple((len(group), group[0].shape[1]) for group in groups)))
        flat += list(joined) + [part for group in groups for part in group]
    in_specs = [
        pl.BlockSpec((block, part.shape[1]), lambda part: (start // block + part, 0))
        for part in flat
    ]
    widths = [sum(cols for _, cols in counts) for _, counts in shapes]
    if together:
        widths = [sum(widths)]
    if after is not None:
        flat.append(after)
        in_specs.append(pl.BlockSpec(memory_space=pl.ANY))
    return pl.pallas_call(
        functools.partial(add_rows_kernel, shapes=tuple(shapes), outs=len(widths)),
        grid=(parts,),
        in_specs=in_specs,
        out_specs=[pl.BlockSpec((block, cols), lambda part: (part, 0)) for cols in widths],
        out_shape=[jax.ShapeDtypeStruct((rows, cols), jnp.float32) for cols in widths],
        compiler_params=pltpu.CompilerParams(vmem_limit_bytes=LIMIT),
        cost_estimate=cost(
            flops=rows * sum(widths), bytes_accessed=16 * rows * sum(widths), transcendentals=0
        ),
        name="add_rows",
    )(*flat)


def spread_kernel(one, two, state, head, own, came, *rest):
    out = rest[len(rest) // 2]
    half = one.shape[1]
    width = 2 * half
    for member in range(out.shape[0]):
        out[member, :, :half] = one[...]
        out[member, :, half:width] = two[...]
        out[member, :, width : width + CHUNK] = state[...]
        out[member, :, width + CHUNK :] = head[...]
        out[member, 7:8, :width] = own[...] + came[...]


def spread(one, two, state, head, own, came, members, held_back):
    vmem = pl.BlockSpec(memory_space=pltpu.VMEM)
    shape = (members, 8, 2 * one.shape[1] + 2 * CHUNK)
    return pl.pallas_call(
        spread_kernel,
        in_specs=[vmem] * 6 + [pl.BlockSpec(memory_space=pl.ANY)] * len(held_back),
        out_specs=[vmem] + [pl.BlockSpec(memory_space=pl.ANY)] * len(held_back),
        out_shape=[
            jax.ShapeDtypeStruct(shape, jnp.float32),
        ]
        + [jax.ShapeDtypeStruct(part.shape, part.dtype) for part in held_back],
        input_output_aliases={6 + at: 1 + at for at in range(len(held_back))},
        compiler_params=pltpu.CompilerParams(vmem_limit_bytes=LIMIT),
        cost_estimate=cost(flops=8 * shape[2], bytes_accessed=4 * 64 * shape[2], transcendentals=0),
        name="spread",
    )(one, two, state, head, own, came, *held_back)


def late_sums(refs, count, more):
    flows = [refs[flow * (2 + more) : (flow + 1) * (2 + more)] for flow in range(FLOWS)]
    totals = []
    for terms in flows:
        total = terms[0][...]
        for term in terms[1:]:
            total = total + term[...]
        totals.append(total)
    small, lines = refs[count], refs[count + 1 : count + 1 + 2 * more]
    total = small[0]
    for member in range(1, small.shape[0]):
        total = total + small[member]
    for upper, lower in zip(lines[::2], lines[1::2]):
        cols = upper.shape[1]
        total = total + jnp.concatenate([upper[...], lower[:, : total.shape[1] - cols]], axis=1)
    return totals, total


def late_specs(stays, came, later, small, rows, index, after=None):
    flat = []
    for flow in range(FLOWS):
        flat += [stays[flow], came[flow]] + [parts[flow] for parts in later]
    specs = [pl.BlockSpec((rows, part.shape[1]), lambda _: (index, 0)) for part in flat]
    specs.append(pl.BlockSpec(small.shape, lambda _: (0, 0, 0)))
    for parts in later:
        last = parts[0].shape[0] // 8
        for place in (last - 2, last - 1):
            specs.append(pl.BlockSpec((8, parts[0].shape[1]), lambda _, place=place: (place, 0)))
    flat += [small] + [parts[0] for parts in later for _ in range(2)]
    if after is not None:
        flat.append(after)
        specs.append(pl.BlockSpec(memory_space=pl.ANY))
    return flat, specs


def go_kernel(*refs, count, more):
    outs = refs[-FLOWS:]
    totals, small = late_sums(refs, count, more)
    for flow, total in enumerate(totals):
        rows, cols = total.shape
        outs[flow][:rows, :] = total
        if flow == 0:
            outs[0][rows : rows + 8, :] = small[:, :cols]
            outs[0][rows + 8 :, : small.shape[1] - cols] = small[:, cols:]
            outs[0][rows + 8 :, small.shape[1] - cols :] = jnp.zeros(
                (8, 2 * cols - small.shape[1]), jnp.float32
            )


def go_rows(stays, came, later, small, rows, after):
    flat, specs = late_specs(stays, came, later, small, rows, 1, after)
    shapes = [
        (rows + (16 if flow == 0 else 0), stays[flow].shape[1]) for flow in range(FLOWS)
    ]
    return pl.pallas_call(
        functools.partial(go_kernel, count=FLOWS * (2 + len(later)), more=len(later)),
        grid=(1,),
        in_specs=specs,
        out_specs=[pl.BlockSpec(shape, fixed) for shape in shapes],
        out_shape=[jax.ShapeDtypeStruct(shape, jnp.float32) for shape in shapes],
        compiler_params=pltpu.CompilerParams(vmem_limit_bytes=LIMIT),
        cost_estimate=cost(flops=rows, bytes_accessed=rows, transcendentals=0),
        name="go_rows",
    )(*flat)


def last_rows_kernel(*refs, count, more):
    totals, sums = late_sums(refs, count, more)
    (
        out_grad_out,
        out_gate,
        out_inner,
        out_state,
        out_step,
        out_norm_in,
        out_conv_inner,
        out_bias_inner,
        out_conv_state,
        out_bias_state,
        out_step_bias,
        out_decay,
        out_skip,
        out_norm_out,
    ) = refs[-14:]
    share = out_grad_out.shape[1] // FLOWS
    for flow, total in enumerate(totals):
        out_grad_out[:, flow * share : (flow + 1) * share] = total[:, :share]
        start = share
        for group in range(2):
            first = (group * FLOWS + flow) * TILE
            out_gate[:, first : first + TILE] = total[:, start : start + TILE]
            out_inner[:, first : first + TILE] = total[:, start + TILE : start + 2 * TILE]
            start += 2 * TILE
        if flow < 2:
            side = (out_state, out_step)[flow]
            side[...] = total[:, start : start + side.shape[1]]
    inner = out_gate.shape[1]
    for out, row in ((out_norm_out, 0), (out_bias_inner, 2), (out_norm_in, 7)):
        for part in range(out.shape[0]):
            out[part : part + 1, :] = sums[row : row + 1, part * CHUNK : (part + 1) * CHUNK]
    out_conv_inner[...] = sums[3:7, :inner]
    out_bias_state[...] = sums[0:1, inner : inner + CHUNK]
    out_conv_state[...] = sums[1:5, inner : inner + CHUNK]
    heads = out_skip.shape[1]
    out_step_bias[...] = sums[0:1, inner + CHUNK : inner + CHUNK + heads]
    out_decay[...] = sums[1:2, inner + CHUNK : inner + CHUNK + heads]
    channel = lax.broadcasted_iota(jnp.int32, (inner, CHUNK), 0)
    target = lax.broadcasted_iota(jnp.int32, (inner, CHUNK), 1)
    by_head_sums = dot_exact(sums[:, :inner], (channel // 64 == target).astype(jnp.bfloat16))
    out_skip[...] = by_head_sums[1:2, :heads]


def last_rows(stays, came, later, small, rows, inner, states, heads, taps):
    flat, specs = late_specs(stays, came, later, small, rows, 0)
    vector = (inner // CHUNK, CHUNK)
    outs = [(rows, inner), (rows, inner), (rows, inner), (rows, states), (rows, heads)]
    outs += [vector, (taps, inner), vector, (taps, states), (1, states)]
    outs += [(1, heads), (1, heads), (1, heads), vector]
    return pl.pallas_call(
        functools.partial(last_rows_kernel, count=FLOWS * (2 + len(later)), more=len(later)),
        grid=(1,),
        in_specs=specs,
        out_specs=[pl.BlockSpec(shape, fixed) for shape in outs],
        out_shape=[jax.ShapeDtypeStruct(shape, jnp.float32) for shape in outs],
        compiler_params=pltpu.CompilerParams(vmem_limit_bytes=LIMIT),
        cost_estimate=cost(
            flops=8 * rows * inner, bytes_accessed=80 * rows * inner, transcendentals=0
        ),
        name="last_rows",
    )(*flat)


def normed_grad_kernel(
    core, gate_one, inner_one, gate_two, inner_two, state, step, gate, inner, proj_state, proj_step, tokens, rstd_in, *rest
):
    out, norm_row = rest[-2:]
    tile = pl.program_id(0)
    half = gate_one.shape[1]
    states = state.shape[1]
    heads = proj_step.shape[0]
    total = dot_last(gate_one[...], gate[:, :half]) + dot_last(inner_one[...], inner[:, :half])
    total = total + dot_last(gate_two[...], gate[:, half:]) + dot_last(inner_two[...], inner[:, half:])
    chosen = jnp.where(core[0] == 0, proj_state[:, :states], proj_state[:, states:])
    total = total + dot_last(state[...], chosen) + dot(step[:, :heads], proj_step[...])
    out[...] = total
    scaled = total * tokens[...].astype(jnp.float32) * wide(rstd_in[...], TILE)
    here = pl.ds(pl.multiple_of(tile * TILE, TILE), TILE)
    norm_row[0:1, here] = jnp.sum(scaled, axis=0, keepdims=True)


def normed_grad(
    core, one, two, state, step, proj_gate, proj_inner, proj_state, proj_step, tokens, rstd_in, after
):
    rows = state.shape[0]
    width, inner = proj_gate.shape

    def whole(values):
        return pl.BlockSpec(values.shape, fixed)

    def lines(values):
        return pl.BlockSpec((TILE, values.shape[1]), lambda tile: (tile, 0))

    return pl.pallas_call(
        normed_grad_kernel,
        grid=(width // TILE,),
        in_specs=[pl.BlockSpec(memory_space=pltpu.SMEM)]
        + [whole(part) for part in (*one, *two, state, step)]
        + [lines(proj_gate), lines(proj_inner), lines(proj_state)]
        + [pl.BlockSpec((proj_step.shape[0], TILE), tile_cols)]
        + [pl.BlockSpec((rows, TILE), tile_cols), whole(rstd_in)]
        + [pl.BlockSpec(memory_space=pl.ANY)] * len(after),
        out_specs=[pl.BlockSpec((rows, TILE), tile_cols), pl.BlockSpec((1, width), fixed)],
        out_shape=[
            jax.ShapeDtypeStruct((rows, width), jnp.float32),
            jax.ShapeDtypeStruct((1, width), jnp.float32),
        ],
        compiler_params=pltpu.CompilerParams(vmem_limit_bytes=LIMIT),
        cost_estimate=cost(
            flops=4 * rows * inner * width,
            bytes_accessed=4 * inner * width + 8 * rows * width,
            transcendentals=0,
        ),
        name="normed_grad",
    )(
        core,
        *one,
        *two,
        state,
        step,
        proj_gate,
        proj_inner,
        proj_state,
        proj_step,
        tokens,
        rstd_in,
        *after,
    )


def tokens_grad_kernel(
    own, came, tokens, cotangent, gains, grad_tokens
):
    hidden = tokens[...].astype(jnp.float32)
    rstd = lax.rsqrt(jnp.mean(hidden * hidden, axis=1, keepdims=True) + EPS)
    grad_normed = own[...] + came[...]
    weighted = grad_normed * gains[2:3, :]
    back = jnp.mean(weighted * hidden, axis=1, keepdims=True)
    grad_hidden = rstd * weighted - hidden * (rstd * rstd * rstd * back)
    grad_tokens[...] = (cotangent[...].astype(jnp.float32) + grad_hidden).astype(jnp.bfloat16)


def tokens_grad(own, came, tokens, cotangent, gains):
    rows, width = tokens.shape
    lines = pl.BlockSpec((CHUNK, width), lambda step: (step, 0))

    return pl.pallas_call(
        tokens_grad_kernel,
        grid=(rows // CHUNK,),
        in_specs=[lines] * 4 + [pl.BlockSpec(gains.shape, fixed)],
        out_specs=lines,
        out_shape=jax.ShapeDtypeStruct((rows, width), jnp.bfloat16),
        compiler_params=pltpu.CompilerParams(vmem_limit_bytes=LIMIT),
        cost_estimate=cost(
            flops=12 * rows * width, bytes_accessed=14 * rows * width, transcendentals=0
        ),
        name="tokens_grad",
    )(own, came, tokens, cotangent, gains)


def block_out_kernel(
    lengths, row_sums, row_came, own, came, tokens, out, cols, *, inner_total
):
    step = pl.program_id(0)

    @pl.when(step == 0)
    def _():
        rstd, valid = scale_row(row_sums, row_came, lengths, inner_total)
        cols[...] = jnp.broadcast_to(rstd * valid, (CHUNK, rstd.shape[1])).T

    scale = cols[pl.ds(pl.multiple_of(step * CHUNK, CHUNK), CHUNK), 0:1]
    out[...] = (tokens[...].astype(jnp.float32) + scale * (own[...] + came[...])).astype(
        jnp.bfloat16
    )


def finish_block(lengths, row_sums, row_came, own, came, tokens, inner_total):
    rows, width = tokens.shape
    lines = pl.BlockSpec((CHUNK, width), lambda step: (step, 0))
    row = pl.BlockSpec((8, rows), fixed)
    return pl.pallas_call(
        functools.partial(block_out_kernel, inner_total=inner_total),
        grid=(rows // CHUNK,),
        in_specs=[pl.BlockSpec(memory_space=pltpu.SMEM), row, row, lines, lines, lines],
        out_specs=lines,
        out_shape=jax.ShapeDtypeStruct((rows, width), jnp.bfloat16),
        scratch_shapes=[pltpu.VMEM((rows, CHUNK), jnp.float32)],
        compiler_params=pltpu.CompilerParams(vmem_limit_bytes=LIMIT),
        cost_estimate=cost(
            flops=3 * rows * width, bytes_accessed=12 * rows * width, transcendentals=0
        ),
        name="block_out",
    )(lengths, row_sums, row_came, own, came, tokens)


def pass_on(part, flow, step):
    return lax.ppermute(part, ("dp", "tensor"), flow_pairs(flow, step))


def local(
    tokens,
    seq_lengths,
    norm_in,
    proj_gate,
    proj_inner,
    proj_state,
    proj_step,
    conv_inner,
    bias_inner,
    conv_state,
    bias_state,
    step_bias,
    decay_log,
    skip_gain,
    norm_out,
    proj_out,
    cotangent,
):
    width = tokens.shape[1]
    row_count = tokens.shape[0]
    heads_local = proj_step.shape[1]
    inner_local = proj_inner.shape[1]
    state_size = proj_state.shape[1] // 2
    tensor_count = lax.axis_size("tensor")
    inner_total = inner_local * tensor_count
    core = lax.axis_index("tensor").reshape(1)
    blocks = block_order()
    step_t = proj_step.T
    (
        normed,
        gate_raw,
        inner_raw,
        mixed,
        scaled_in,
        partial_value,
        row_sums,
        state_raw,
        state_pre,
        maps,
        step_pre,
        cumul,
        gains,
        rstd_in,
    ) = forward(
        seq_lengths,
        skip_gain,
        tokens,
        norm_in.reshape(-1, CHUNK),
        bias_inner.reshape(-1, CHUNK),
        norm_out.reshape(-1, CHUNK),
        proj_gate,
        proj_inner,
        proj_state,
        step_t,
        conv_inner,
        conv_state,
        bias_state[None, :],
        step_bias[None, :],
        decay_log[None, :],
        proj_out,
        cotangent,
    )
    row_came = swap_tensor(row_sums)
    arranged, *out_halves = out_grad(
        seq_lengths, blocks, row_sums, row_came, cotangent, scaled_in, normed, inner_total
    )

    def first_halving(outs):
        keeps, sends = outs[: len(outs) // 2], outs[len(outs) // 2 :]
        return [[kept, pass_on(sent, flow, 0)] for flow, (kept, sent) in enumerate(zip(keeps, sends))]

    flows_out = first_halving(out_halves)

    def run_backward(origin, after):
        return backward(
            seq_lengths,
            skip_gain,
            row_sums,
            row_came,
            cotangent,
            proj_out,
            gains,
            gate_raw,
            mixed,
            inner_raw,
            conv_inner,
            maps,
            step_pre,
            cumul,
            arranged,
            after,
            origin,
            inner_total,
        )

    one = run_backward(0, out_halves[:1])
    flows_one = first_halving(one[5:])
    two = run_backward(FLOWS, [one[5]] + [terms[1] for terms in flows_out])
    flows_two = first_halving(two[5:])
    own, other, grad_step_raw, head_sums = scan_gradients(
        seq_lengths,
        core,
        one[2:4],
        two[2:4],
        maps,
        step_pre,
        decay_log[None, :],
        [terms[1] for terms in flows_one],
    )
    grad_state_part, state_sums, *side_halves = state_gradients(
        seq_lengths,
        core,
        own,
        swap_tensor(other),
        state_raw,
        state_pre,
        conv_state,
        grad_step_raw,
        arranged,
    )
    flows_side = first_halving(side_halves[2:] + side_halves[:2])
    side_flows = len(flows_side)

    rows = width // 4
    groups = [[flows_out[flow], flows_one[flow], flows_two[flow]] for flow in range(FLOWS)]
    for flow in range(side_flows):
        groups[flow].append(flows_side[flow])
    goes = add_rows([([], group) for group in groups], rows, rows)
    came = [pass_on(go, flow, 1) for flow, go in enumerate(goes)]
    stays = add_rows([([], group) for group in groups], 0, rows, goes[0])
    grad_normed, norm_row = normed_grad(
        core,
        one[:2],
        two[:2],
        grad_state_part,
        grad_step_raw,
        proj_gate,
        proj_inner,
        proj_state,
        step_t,
        tokens,
        rstd_in,
        [goes[0]],
    )
    members = 1 << HALVINGS
    spread_sums, grad_normed, partial_late = spread(
        one[4],
        two[4],
        state_sums,
        head_sums,
        norm_row,
        swap_tensor(norm_row),
        members,
        (grad_normed, partial_value),
    )
    grad_tokens = tokens_grad(grad_normed, swap_tensor(grad_normed), tokens, cotangent, gains)
    small = lax.all_to_all(
        spread_sums,
        ("dp", "tensor"),
        0,
        0,
        axis_index_groups=cube_groups(0, HALVINGS),
    )
    rows = width // 8
    flows = [([], [[stays[flow], came[flow]]]) for flow in range(FLOWS)]
    more = add_rows(flows, rows, rows, spread_sums)
    came_more = [pass_on(go, flow, 2) for flow, go in enumerate(more)]
    stays = add_rows(flows, 0, rows, more[0])
    block_out = finish_block(
        seq_lengths,
        row_sums,
        row_came,
        partial_late,
        swap_tensor(partial_late),
        tokens,
        inner_total,
    )
    later = []
    for step in range(HALVINGS, DIMS):
        rows = width >> (step + 1)
        after = (None, block_out, grad_tokens)[step - HALVINGS]
        goes = go_rows(stays, came_more, later, small, rows, after)
        later.append([pass_on(go, flow, step) for flow, go in enumerate(goes)])
    (
        grad_proj_out,
        grad_proj_gate,
        grad_proj_inner,
        grad_proj_state,
        grad_proj_step,
        grad_norm_in,
        grad_conv_inner,
        grad_bias_inner,
        grad_conv_state,
        grad_bias_state,
        grad_step_bias,
        grad_decay_log,
        grad_skip_gain,
        grad_norm_out,
    ) = last_rows(
        stays,
        came_more,
        later,
        small,
        width // BLOCKS,
        inner_local,
        2 * state_size // tensor_count,
        heads_local,
        conv_inner.shape[0],
    )

    return (
        block_out,
        grad_tokens,
        grad_norm_in.reshape(-1),
        grad_proj_gate,
        grad_proj_inner,
        grad_proj_state,
        grad_proj_step,
        grad_conv_inner,
        grad_bias_inner.reshape(-1),
        grad_conv_state,
        grad_bias_state.reshape(-1),
        grad_step_bias.reshape(-1),
        grad_decay_log.reshape(-1),
        grad_skip_gain.reshape(-1),
        grad_norm_out.reshape(-1),
        grad_proj_out.T,
    )


def solution(mesh):
    return jax.shard_map(
        local,
        mesh=mesh,
        in_specs=(
            P("dp", None),
            P("dp", None),
            P(),
            P(None, "tensor"),
            P(None, "tensor"),
            P(),
            P(None, "tensor"),
            P(None, "tensor"),
            P("tensor"),
            P(),
            P(),
            P("tensor"),
            P("tensor"),
            P("tensor"),
            P("tensor"),
            P("tensor", None),
            P("dp", None),
        ),
        out_specs=(
            P("dp", None),
            P("dp", None),
            P(),
            P("dp", "tensor"),
            P("dp", "tensor"),
            P("dp", "tensor"),
            P("dp", "tensor"),
            P(None, "tensor"),
            P("tensor"),
            P(None, "tensor"),
            P("tensor"),
            P("tensor"),
            P("tensor"),
            P("tensor"),
            P("tensor"),
            P("tensor", "dp"),
        ),
        check_vma=False,
    )
```

```python
import functools

import jax
import jax.numpy as jnp
from jax import lax
from jax.experimental import pallas as pl
from jax.experimental.pallas import tpu as pltpu
from jax.sharding import PartitionSpec as P

EPS = 1e-05
FLOWS = 3
DIMS = 6
BLOCKS = 64
TILE = 256
WIDE = 512
CHUNK = 128
LIMIT = 65400 * 1024
HINT = 10**6


def cost(flops, bytes_accessed, transcendentals):
    return pl.CostEstimate(
        flops=flops // HINT, bytes_accessed=bytes_accessed // HINT, transcendentals=transcendentals // HINT
    )


def dot(left, right):
    return jnp.dot(left, right, preferred_element_type=jnp.float32)


def thirds(values):
    high = values.astype(jnp.bfloat16)
    rest = values - high.astype(jnp.float32)
    middle = rest.astype(jnp.bfloat16)
    return high, middle, (rest - middle.astype(jnp.float32)).astype(jnp.bfloat16)


def dot_exact(left, right, how=None):
    how = how or dot
    if left.dtype == jnp.bfloat16:
        one, two, three = [how(left, part) for part in thirds(right)]
    else:
        one, two, three = [how(part, right) for part in thirds(left)]
    return one + (two + three)


def dot_first(left, right):
    return lax.dot_general(
        left,
        right,
        (((0,), (0,)), ((), ())),
        preferred_element_type=jnp.float32,
    )


def dot_last(left, right):
    return lax.dot_general(
        left,
        right,
        (((1,), (1,)), ((), ())),
        preferred_element_type=jnp.float32,
    )


def chip_bits(index):
    bits = []
    for place in (4, 2, 0):
        coord = (index >> place) & 3
        bits += [(coord ^ (coord >> 1)) & 1, coord >> 1]
    return bits


def partner(index, dim):
    place = (4, 2, 0)[dim // 2]
    return index ^ ((3 if dim % 2 else 1) << place)


HALVINGS = 3


def flow_dim(core, flow, step):
    return 2 * ((flow + step) % HALVINGS) + (core if step < HALVINGS else 1 - core)


def cube_groups(first, stop):
    groups = []
    for core in range(2):
        lines = {}
        for index in range(BLOCKS):
            bits = chip_bits(index)
            dims = [flow_dim(core, 0, step) for step in range(DIMS)]
            inside = tuple(bits[dim] for dim in dims[first:stop])
            outside = tuple(bits[dim] for dim in dims[:first] + dims[stop:])
            lines.setdefault(outside, []).append((inside, 2 * index + core))
        groups += [[device for _, device in sorted(line)] for line in lines.values()]
    return groups


def flow_pairs(flow, step):
    return [
        (2 * index + core, 2 * partner(index, flow_dim(core, flow, step)) + core)
        for index in range(BLOCKS)
        for core in range(2)
    ]


def swap_tensor(values):
    return lax.ppermute(values, "tensor", [(0, 1), (1, 0)])


def block_order():
    index = lax.axis_index("dp")
    core = lax.axis_index("tensor")
    mine = chip_bits(index)
    place = jnp.arange(BLOCKS, dtype=jnp.int32)
    orders = []
    for flow in range(FLOWS):
        by_core = []
        for which in range(2):
            bits = [None] * DIMS
            for step in range(DIMS):
                dim = flow_dim(which, flow, step)
                bits[dim] = ((place >> (DIMS - 1 - step)) & 1) ^ mine[dim]
            block = jnp.zeros((BLOCKS,), jnp.int32)
            for first in range(0, DIMS, 2):
                high = bits[first + 1]
                block = block * 4 + 2 * high + (bits[first] ^ high)
            by_core.append(block)
        orders.append(jnp.where(core == 0, by_core[0], by_core[1]))
    return jnp.stack(orders)


def ends_of(lengths):
    ends, total = [], 0
    for slot in range(lengths.shape[1]):
        total = total + lengths[0, slot]
        ends.append(total)
    return ends


def segment_of(positions, ends):
    segment = jnp.zeros(positions.shape, jnp.int32)
    for end in ends:
        segment = segment + (positions >= end).astype(jnp.int32)
    return segment


def fill_keeps(keeps, ends):
    rows = lax.broadcasted_iota(jnp.int32, keeps.shape[1:], 0)
    here = segment_of(rows, ends)
    for lag in range(1, keeps.shape[0] + 1):
        same = (segment_of(rows - lag, ends) == here) & (rows >= lag)
        keeps[lag - 1] = same.astype(jnp.float32)


def same_sequence(rows, ends, later):
    first = lax.broadcasted_iota(jnp.int32, (rows, rows), later)
    second = lax.broadcasted_iota(jnp.int32, (rows, rows), 1 - later)
    same = segment_of(first, ends) == segment_of(second, ends)
    return (same & (first >= second)).astype(jnp.float32)


def wide(mask, cols):
    return mask if cols == CHUNK else jnp.concatenate([mask] * (cols // CHUNK), axis=1)


def lagged_rows(values, keeps):
    cols = values.shape[1]
    return [values] + [
        pltpu.roll(values, lag, 0) * wide(keeps[lag - 1], cols)
        for lag in range(1, keeps.shape[0] + 1)
    ]


def conv_forward(lines, taps, bias):
    total = bias + taps[0:1] * lines[0]
    for lag in range(1, len(lines)):
        total = total + taps[lag : lag + 1] * lines[lag]
    return total


def conv_backward(grad_pre, lines, taps, keeps):
    rows, cols = grad_pre.shape
    tap_grads = [jnp.sum(grad_pre * line, axis=0, keepdims=True) for line in lines]
    grad_values = grad_pre * taps[0:1]
    for lag in range(1, len(lines)):
        kept = grad_pre * wide(keeps[lag - 1], cols)
        grad_values = grad_values + pltpu.roll(kept, rows - lag, 0) * taps[lag : lag + 1]
    return jnp.concatenate(tap_grads, axis=0), jnp.sum(grad_pre, axis=0, keepdims=True), grad_values


def by_head(pair):
    lane = lax.broadcasted_iota(jnp.int32, pair.shape, 1)
    none = jnp.zeros_like(pair)
    return jnp.concatenate(
        [jnp.where(lane < CHUNK // 2, pair, none), jnp.where(lane < CHUNK // 2, none, pair)], axis=0
    )


def softplus(values):
    return jnp.maximum(values, 0.0) + jnp.log1p(jnp.exp(-jnp.abs(values)))


def head_row(values, first, count):
    channel = lax.broadcasted_iota(jnp.int32, (1, count), 1)
    row = jnp.zeros((1, count), jnp.float32)
    for head in range(count // 64):
        row = jnp.where(channel // 64 == head, values[first + head], row)
    return row


def forward_kernel(
    lengths,
    skip,
    tokens,
    norm_in,
    bias_inner,
    norm_out,
    proj_gate,
    proj_inner,
    proj_state,
    proj_step,
    conv_inner,
    conv_state,
    bias_state,
    step_bias,
    decay_log,
    proj_out,
    cotangent,
    normed,
    gate_raw,
    inner_raw,
    mixed,
    scaled,
    partial,
    row_sums,
    state_raw,
    state_pre,
    maps,
    step_pre,
    cumul,
    gains,
    rstd_in,
    keeps,
    scores,
    cum_rows,
    step_rows,
    reach_rows,
    reach_cols,
    square_cols,
    along_cols,
    weights,
    proj_in,
    cotangent_in,
    late_sems,
    early_in,
    early_sems,
    *,
    tiles,
):
    tile = pl.program_id(0)
    now = lax.rem(tile, 2)

    def early(which, slot):
        here = pl.ds(pl.multiple_of(which * TILE, TILE), TILE)
        return [
            pltpu.make_async_copy(source.at[:, here], early_in.at[slot, at], early_sems.at[slot, at])
            for at, source in enumerate((proj_gate, proj_inner))
        ]

    @pl.when(tile == 0)
    def _():
        for copy in early(0, 0) + early(1, 1):
            copy.start()

    @pl.when((tile > 0) & (tile + 1 < tiles))
    def _():
        for copy in early(tile + 1, 1 - now):
            copy.start()

    def late(part):
        here = pl.ds(pl.multiple_of(part * WIDE, WIDE), WIDE)
        slot = lax.rem(part, 2)
        return (
            pltpu.make_async_copy(proj_out.at[:, here], proj_in.at[slot], late_sems.at[slot, 0]),
            pltpu.make_async_copy(
                cotangent.at[:, here], cotangent_in.at[slot], late_sems.at[slot, 1]
            ),
        )

    for part in range(2):

        @pl.when(tile == tiles - 2 + part)
        def _(part=part):
            for copy in late(jnp.int32(part)):
                copy.start()

    rows = tokens.shape[0]
    heads = step_bias.shape[1]
    chunks = rows // CHUNK

    @pl.when(tile == 0)
    def _():
        ends = ends_of(lengths)
        fill_keeps(keeps, ends)
        gains[...] = jnp.zeros(gains.shape, jnp.float32)
        for row, source in enumerate((bias_inner, norm_out, norm_in)):
            for part in range(source.shape[0]):
                gains[row : row + 1, part * CHUNK : (part + 1) * CHUNK] = source[part : part + 1, :]
        for chunk in range(chunks):
            at = slice(chunk * CHUNK, (chunk + 1) * CHUNK)
            hidden = tokens[at, :].astype(jnp.float32)
            rstd = lax.rsqrt(jnp.mean(hidden * hidden, axis=1, keepdims=True) + EPS)
            normed[at, :] = (hidden * rstd * gains[2:3, :]).astype(jnp.bfloat16)
            rstd_in[at, :] = jnp.broadcast_to(rstd, (CHUNK, CHUNK))
        raw = dot(normed[...], proj_state[...])
        state_raw[...] = raw
        pre = conv_forward(lagged_rows(raw, keeps), conv_state, bias_state[...])
        state_pre[...] = pre
        maps[...] = jax.nn.silu(pre).astype(jnp.bfloat16)
        states = maps.shape[1] // 2
        scores[...] = dot_last(maps[:, states:], maps[:, :states]) * same_sequence(rows, ends, 0)
        step_pre[...] = jnp.zeros(step_pre.shape, jnp.float32)
        step_pre[:, :heads] = dot_last(normed[...], proj_step[...]) + step_bias[...]
        steps = softplus(step_pre[...])
        cumul[...] = jnp.zeros(cumul.shape, jnp.float32)
        cumul[:, :heads] = steps[:, :heads] * -jnp.exp(decay_log[...])
        earlier = lax.broadcasted_iota(jnp.int32, (rows, rows), 0) >= lax.broadcasted_iota(
            jnp.int32, (rows, rows), 1
        )
        total = dot_exact(earlier.astype(jnp.bfloat16), cumul[...])
        cumul[...] = total
        total_rows = total.T
        steps_rows = steps.T
        cum_rows[...] = total_rows
        step_rows[...] = steps_rows
        for chunk in range(1, chunks):
            start = chunk * CHUNK
            reach_rows[chunk - 1, :, :start] = (
                jnp.exp(total_rows[:, start - 1 : start] - total_rows[:, :start])
                * steps_rows[:, :start]
            )
            reach_cols[start : start + CHUNK, :] = jnp.exp(
                total[start : start + CHUNK] - total[start - 1 : start]
            )
        square_cols[...] = jnp.zeros(square_cols.shape, jnp.float32)
        along_cols[...] = jnp.zeros(along_cols.shape, jnp.float32)
        weights[...] = jnp.zeros(weights.shape, weights.dtype)

    @pl.when(tile < tiles)
    def _():
        for copy in early(tile, now):
            copy.wait()
        gate = dot(normed[...], early_in[now, 0])
        gate_raw[...] = gate
        inner = dot(normed[...], early_in[now, 1])
        inner_raw[...] = inner
        here = pl.ds(pl.multiple_of(tile * TILE, TILE), TILE)
        pre = conv_forward(lagged_rows(inner, keeps), conv_inner, gains[0:1, here])
        xconv = jax.nn.silu(pre)
        values = xconv.astype(jnp.bfloat16)
        first = tile * (TILE // 64)
        back = lax.rem(CHUNK - first, CHUNK)
        cum_cols = pltpu.roll(cumul[...], back, 1)
        near_cols = pltpu.roll(reach_cols[...], back, 1)
        skip_row = head_row(skip, first, TILE)
        for pair in range(TILE // CHUNK):
            cols = slice(pair * CHUNK, (pair + 1) * CHUNK)
            two = values[:, cols]
            for half in range(2):
                head = 2 * pair + half
                cum_row = cum_rows[pl.ds(first + head, 1), :]
                step_row = step_rows[pl.ds(first + head, 1), :]
                for chunk in range(chunks):
                    start, stop = chunk * CHUNK, (chunk + 1) * CHUNK
                    base = half * rows
                    gap = cum_cols[start:stop, head : head + 1] - cum_row[:, start:stop]
                    weights[pair, start:stop, base + start : base + stop] = (
                        scores[start:stop, start:stop]
                        * (jnp.exp(jnp.minimum(gap, 0.0)) * step_row[:, start:stop])
                    ).astype(jnp.bfloat16)
                    if chunk:
                        reach = reach_rows[chunk - 1, pl.ds(first + head, 1), :][:, :start]
                        weights[pair, start:stop, base : base + start] = (
                            scores[start:stop, :start]
                            * (near_cols[start:stop, head : head + 1] * reach)
                        ).astype(jnp.bfloat16)
            ssd = dot(weights[pair], by_head(two))
            whole = ssd + skip_row[:, cols] * xconv[:, cols]
            mixed[:, cols] = whole
            gated = whole * jax.nn.silu(gate[:, cols])
            square_cols[...] += gated * gated
            place = pl.multiple_of(tile * TILE + pair * CHUNK, CHUNK)
            scaled[:, pl.ds(place, CHUNK)] = (gated * gains[1:2, pl.ds(place, CHUNK)]).astype(jnp.bfloat16)

    @pl.when(tile >= tiles)
    def _():
        part = tile - tiles
        slot = lax.rem(part, 2)
        for copy in late(part):
            copy.wait()
        projected = dot(scaled[...], proj_in[slot])
        partial[...] = projected
        products = projected * cotangent_in[slot].astype(jnp.float32)
        for start in range(0, WIDE, CHUNK):
            along_cols[...] += products[:, start : start + CHUNK]

        @pl.when(part + 2 < proj_out.shape[1] // WIDE)
        def _():
            for copy in late(part + 2):
                copy.start()

    @pl.when(tile == pl.num_programs(0) - 1)
    def _():
        row_sums[...] = jnp.zeros(row_sums.shape, jnp.float32)
        row_sums[0:1, :] = jnp.sum(square_cols[...].T, axis=0, keepdims=True)
        row_sums[1:2, :] = jnp.sum(along_cols[...].T, axis=0, keepdims=True)


def tile_cols(tile):
    return (0, tile)


def fixed(tile):
    return (0, 0)


def forward(
    lengths,
    skip,
    tokens,
    norm_in,
    bias_inner,
    norm_out,
    proj_gate,
    proj_inner,
    proj_state,
    proj_step,
    conv_inner,
    conv_state,
    bias_state,
    step_bias,
    decay_log,
    proj_out,
    cotangent,
):
    rows, width = tokens.shape
    inner = proj_gate.shape[1]
    taps = conv_inner.shape[0]
    states = proj_state.shape[1]
    heads = proj_step.shape[0]
    f32, bf16 = jnp.float32, jnp.bfloat16
    smem = pl.BlockSpec(memory_space=pltpu.SMEM)

    def whole(*shape):
        return pl.BlockSpec(shape, fixed)

    tiles = inner // TILE

    def strip(count):
        return pl.BlockSpec((count, TILE), lambda tile: (0, jnp.minimum(tile, tiles - 1)))

    def later(count):
        return pl.BlockSpec((count, WIDE), lambda tile: (0, jnp.maximum(tile - tiles, 0)))

    return pl.pallas_call(
        functools.partial(forward_kernel, tiles=tiles),
        grid=(tiles + width // WIDE,),
        in_specs=[
            smem,
            smem,
            whole(rows, width),
            whole(*norm_in.shape),
            whole(*norm_in.shape),
            whole(*norm_in.shape),
            pl.BlockSpec(memory_space=pl.ANY),
            pl.BlockSpec(memory_space=pl.ANY),
            whole(width, states),
            whole(heads, width),
            strip(taps),
            whole(taps, states),
            whole(1, states),
            whole(1, heads),
            whole(1, heads),
            pl.BlockSpec(memory_space=pl.ANY),
            pl.BlockSpec(memory_space=pl.ANY),
        ],
        out_specs=[
            whole(rows, width),
            strip(rows),
            strip(rows),
            strip(rows),
            whole(rows, inner),
            later(rows),
            whole(8, rows),
            whole(rows, states),
            whole(rows, states),
            whole(rows, states),
            whole(rows, CHUNK),
            whole(rows, CHUNK),
            whole(8, inner),
            whole(rows, CHUNK),
        ],
        out_shape=[
            jax.ShapeDtypeStruct((rows, width), bf16),
            jax.ShapeDtypeStruct((rows, inner), f32),
            jax.ShapeDtypeStruct((rows, inner), f32),
            jax.ShapeDtypeStruct((rows, inner), f32),
            jax.ShapeDtypeStruct((rows, inner), bf16),
            jax.ShapeDtypeStruct((rows, width), f32),
            jax.ShapeDtypeStruct((8, rows), f32),
            jax.ShapeDtypeStruct((rows, states), f32),
            jax.ShapeDtypeStruct((rows, states), f32),
            jax.ShapeDtypeStruct((rows, states), bf16),
            jax.ShapeDtypeStruct((rows, CHUNK), f32),
            jax.ShapeDtypeStruct((rows, CHUNK), f32),
            jax.ShapeDtypeStruct((8, inner), f32),
            jax.ShapeDtypeStruct((rows, CHUNK), f32),
        ],
        scratch_shapes=[
            pltpu.VMEM((taps - 1, rows, CHUNK), f32),
            pltpu.VMEM((rows, rows), f32),
            pltpu.VMEM((CHUNK, rows), f32),
            pltpu.VMEM((CHUNK, rows), f32),
            pltpu.VMEM((rows // CHUNK - 1, CHUNK, rows), f32),
            pltpu.VMEM((rows, CHUNK), f32),
            pltpu.VMEM((rows, CHUNK), f32),
            pltpu.VMEM((rows, CHUNK), f32),
            pltpu.VMEM((TILE // CHUNK, rows, 2 * rows), bf16),
            pltpu.VMEM((2, inner, WIDE), bf16),
            pltpu.VMEM((2, rows, WIDE), bf16),
            pltpu.SemaphoreType.DMA((2, 2)),
            pltpu.VMEM((2, 2, width, TILE), bf16),
            pltpu.SemaphoreType.DMA((2, 2)),
        ],
        compiler_params=pltpu.CompilerParams(vmem_limit_bytes=LIMIT),
        cost_estimate=cost(
            flops=2 * rows * width * (2 * inner + states + heads) + 2 * rows * rows * inner,
            bytes_accessed=4 * width * inner + 18 * rows * inner,
            transcendentals=4 * rows * inner,
        ),
        name="layer_forward",
    )(
        lengths,
        skip,
        tokens,
        norm_in,
        bias_inner,
        norm_out,
        proj_gate,
        proj_inner,
        proj_state,
        proj_step,
        conv_inner,
        conv_state,
        bias_state,
        step_bias,
        decay_log,
        proj_out,
        cotangent,
    )


def scale_row(row_sums, came, lengths, inner_total):
    rstd = lax.rsqrt((row_sums[0:1, :] + came[0:1, :]) / inner_total + EPS)
    rows = lax.broadcasted_iota(jnp.int32, rstd.shape, 1)
    return rstd, (rows < ends_of(lengths)[-1]).astype(jnp.float32)


def turned(values):
    count = values.shape[1]
    row = lax.broadcasted_iota(jnp.int32, (count, count), 0)
    col = lax.broadcasted_iota(jnp.int32, (count, count), 1)
    return dot_last((row == col).astype(jnp.bfloat16), values)


def store_flow(held, sems, flow, count, compute, keeps, sends):
    half = held.shape[1] // 2
    slot = lax.rem(flow, 2)

    def copy_out(which_flow, which):
        to = (keeps, sends)[which][which_flow]
        at = which_flow % 2
        return pltpu.make_async_copy(
            held.at[at, pl.ds(which * half, half)], to, sems.at[at, which]
        )

    for done in range(count - 2):

        @pl.when(flow == done + 2)
        def _(done=done):
            copy_out(done, 0).wait()
            copy_out(done, 1).wait()

    for which in (1, 0):
        compute(slot, slice(which * half, (which + 1) * half))
        for each in range(count):

            @pl.when(flow == each)
            def _(each=each, which=which):
                copy_out(each, which).start()

    @pl.when(flow == count - 1)
    def _():
        for each in (count - 2, count - 1):
            copy_out(each, 0).wait()
            copy_out(each, 1).wait()


def out_grad_kernel(
    lengths,
    blocks,
    row_sums,
    came,
    cotangent,
    scaled,
    normed,
    arranged,
    keep_one,
    keep_two,
    keep_three,
    send_one,
    send_two,
    send_three,
    normed_t,
    cotangent_t,
    grad_projected,
    held,
    sems,
    *,
    inner_total,
    tiles,
):
    step = pl.program_id(0)

    @pl.when(step < tiles)
    def _():
        rstd, valid = scale_row(row_sums, came, lengths, inner_total)

        @pl.loop(0, WIDE // TILE)
        def _(part):
            at = pl.ds(pl.multiple_of(step * WIDE + part * TILE, TILE), TILE)
            here = pl.ds(pl.multiple_of(part * TILE, TILE), TILE)
            cotangent_t[at, :] = turned(cotangent[:, here]) * (rstd * valid)
            normed_t[at, :] = turned(normed[:, here])


    @pl.when(step >= tiles)
    def _():
        per = normed_t.shape[0] // BLOCKS
        flow = step - tiles
        for place in range(0, BLOCKS, 2):
            at = slice(place * per, (place + 2) * per)
            rows = [
                pl.ds(pl.multiple_of(blocks[flow, place + more] * per, 8), per) for more in range(2)
            ]
            arranged[0, at, :] = jnp.concatenate(
                [normed_t[one, :] for one in rows], axis=0
            ).astype(jnp.bfloat16)
            grad_projected[at, :] = jnp.concatenate(
                [cotangent_t[one, :] for one in rows], axis=0
            ).astype(jnp.bfloat16)

        def compute(slot, at):
            held[slot, at, :] = dot(grad_projected[at, :], scaled[...])

        store_flow(
            held,
            sems,
            flow,
            FLOWS,
            compute,
            (keep_one, keep_two, keep_three),
            (send_one, send_two, send_three),
        )


def out_grad(lengths, blocks, row_sums, came, cotangent, scaled, normed, inner_total):
    rows, width = cotangent.shape
    inner = scaled.shape[1]
    tiles = width // WIDE
    share = inner // FLOWS
    smem = pl.BlockSpec(memory_space=pltpu.SMEM)
    row = pl.BlockSpec((8, rows), fixed)
    cols = pl.BlockSpec((rows, WIDE), lambda step: (0, jnp.minimum(step, tiles - 1)))
    return pl.pallas_call(
        functools.partial(out_grad_kernel, inner_total=inner_total, tiles=tiles),
        grid=(tiles + FLOWS,),
        in_specs=[
            smem,
            smem,
            row,
            row,
            cols,
            pl.BlockSpec((rows, share), lambda step: (0, jnp.maximum(step - tiles, 0))),
            cols,
        ],
        out_specs=[
            pl.BlockSpec((1, width, rows), lambda step: (jnp.maximum(step - tiles, 0), 0, 0)),
        ]
        + [pl.BlockSpec(memory_space=pl.ANY)] * (2 * FLOWS),
        out_shape=[jax.ShapeDtypeStruct((FLOWS, width, rows), jnp.bfloat16)]
        + [jax.ShapeDtypeStruct((width // 2, share), jnp.float32)] * (2 * FLOWS),
        scratch_shapes=[
            pltpu.VMEM((width, rows), jnp.float32),
            pltpu.VMEM((width, rows), jnp.float32),
            pltpu.VMEM((width, rows), jnp.bfloat16),
            pltpu.VMEM((2, width, share), jnp.float32),
            pltpu.SemaphoreType.DMA((2, 2)),
        ],
        compiler_params=pltpu.CompilerParams(vmem_limit_bytes=LIMIT),
        cost_estimate=cost(
            flops=2 * rows * inner * width,
            bytes_accessed=4 * inner * width + 14 * rows * width,
            transcendentals=0,
        ),
        name="out_grad",
    )(lengths, blocks, row_sums, came, cotangent, scaled, normed)


def backward_kernel(
    lengths,
    skip,
    row_sums,
    came,
    cotangent,
    proj_out,
    gains,
    gate_raw,
    mixed,
    inner_raw,
    conv_inner,
    maps,
    step_pre,
    cumul,
    arranged,
    *rest,
    origin,
    inner_total,
):
    (
        grad_gate,
        grad_inner,
        grad_scores,
        flows,
        sums,
        keep_one,
        keep_two,
        keep_three,
        send_one,
        send_two,
        send_three,
        grad_projected,
        slope_cols,
        keeps,
        scores,
        cum_rows,
        near_rows,
        far_cols,
        step_cols,
        held,
        sems,
        weights,
        both,
        lines_in,
        lines_sem,
    ) = rest[-25:]
    tile = pl.program_id(0)
    fetch = pltpu.make_async_copy(arranged.at[tile], lines_in, lines_sem)
    fetch.start()
    rows = cotangent.shape[0]
    chunks = rows // CHUNK

    @pl.when(tile == 0)
    def _():
        ends = ends_of(lengths)
        fill_keeps(keeps, ends)
        rstd, valid = scale_row(row_sums, came, lengths, inner_total)
        slope = (row_sums[1:2, :] + came[1:2, :]) * valid * (rstd * rstd * rstd) / inner_total
        scale_cols = jnp.broadcast_to(rstd * valid, (CHUNK, rows)).T
        slope_cols[...] = jnp.broadcast_to(slope, (CHUNK, rows)).T
        for chunk in range(chunks):
            at = slice(chunk * CHUNK, (chunk + 1) * CHUNK)
            grad_projected[at, :] = (
                cotangent[at, :].astype(jnp.float32) * scale_cols[at, 0:1]
            ).astype(jnp.bfloat16)
        states = maps.shape[1] // 2
        scores[...] = dot_last(maps[:, :states], maps[:, states:]) * same_sequence(rows, ends, 1)
        total = cumul[...]
        total_rows = total.T
        cum_rows[...] = total_rows
        step_cols[...] = softplus(step_pre[...])
        for chunk in range(chunks - 1):
            start, stop = chunk * CHUNK, (chunk + 1) * CHUNK
            near_rows[chunk, :, stop:] = jnp.exp(
                total_rows[:, stop:] - total_rows[:, stop - 1 : stop]
            )
            far_cols[start:stop, :] = jnp.exp(total[stop - 1 : stop] - total[start:stop])
        grad_scores[...] = jnp.zeros(grad_scores.shape, jnp.float32)
        weights[...] = jnp.zeros(weights.shape, weights.dtype)
        flows[...] = jnp.zeros(flows.shape, jnp.float32)

    first = (tile + origin) * (TILE // 64)
    back = lax.rem(CHUNK - first, CHUNK)
    cum_turned = pltpu.roll(cumul[...], back, 1)
    far_turned = pltpu.roll(far_cols[...], back, 1)
    step_turned = pltpu.roll(step_cols[...], back, 1)
    skip_row = head_row(skip, first, TILE)
    lane = lax.broadcasted_iota(jnp.int32, (rows, CHUNK), 1)
    grad_scaled = dot_last(grad_projected[...], proj_out[...])
    for pair in range(TILE // CHUNK):
        cols = slice(pair * CHUNK, (pair + 1) * CHUNK)
        raw = gate_raw[:, cols]
        sigma = jax.nn.sigmoid(raw)
        act = raw * sigma
        mix = mixed[:, cols]
        gated = mix * act
        grad_wide = grad_scaled[:, cols]
        sums[0:1, cols] = jnp.sum(grad_wide * gated, axis=0, keepdims=True)
        grad_gated = grad_wide * gains[1:2, cols] - slope_cols[...] * gated
        grad_mixed = grad_gated * act
        gate_grad = (grad_gated * mix * (sigma * (1.0 + raw * (1.0 - sigma)))).astype(jnp.bfloat16)
        grad_gate[:, cols] = gate_grad
        both[:, cols] = gate_grad
        lines = lagged_rows(inner_raw[:, cols], keeps)
        pre = conv_forward(lines, conv_inner[:, cols], gains[0:1, cols])
        sigma = jax.nn.sigmoid(pre)
        xconv = pre * sigma
        sums[1:2, cols] = jnp.sum(grad_mixed * xconv, axis=0, keepdims=True)
        values = xconv.astype(jnp.bfloat16)
        grad_ssd = grad_mixed.astype(jnp.bfloat16)
        middle = rows // 2
        heads_own = by_head(values)
        stacked = jnp.concatenate(
            [
                heads_own[:middle],
                heads_own[rows : rows + middle],
                heads_own[middle:rows],
                heads_own[rows + middle :],
            ],
            axis=0,
        )
        early = dot_last(stacked[:rows], grad_ssd[:middle])
        late = dot_last(stacked, grad_ssd[middle:])
        for half in range(2):
            head = 2 * pair + half
            base = half * rows
            cum_row = cum_rows[pl.ds(first + head, 1), :]
            for chunk in range(chunks):
                start, stop = chunk * CHUNK, (chunk + 1) * CHUNK
                step_col = step_turned[start:stop, head : head + 1]
                cum_col = cum_turned[start:stop, head : head + 1]
                if chunk < chunks - 1:
                    far_step = far_turned[start:stop, head : head + 1] * step_col
                    near_row = near_rows[chunk, pl.ds(first + head, 1), :]
                line = start + half * middle if start < middle else start + (1 + half) * middle
                for other in range(chunk, chunks):
                    begin, end = other * CHUNK, (other + 1) * CHUNK
                    if begin < middle:
                        grad_mix = early[line : line + CHUNK, begin:end]
                    else:
                        grad_mix = late[line : line + CHUNK, begin - middle : end - middle]
                    if other == chunk:
                        gap = cum_row[:, begin:end] - cum_col
                        weighted = jnp.exp(jnp.minimum(gap, 0.0)) * step_col
                    else:
                        weighted = far_step * near_row[:, begin:end]
                    grad_scores[start:stop, begin:end] += grad_mix * weighted
                    weights[pair, start:stop, base + begin : base + end] = (
                        scores[start:stop, begin:end] * weighted
                    ).astype(jnp.bfloat16)
        grad_values = dot(weights[pair], by_head(grad_ssd))
        taken = values.astype(jnp.float32) * grad_values
        given = grad_ssd.astype(jnp.float32) * (mix - skip_row[:, cols] * xconv)
        channel = lax.broadcasted_iota(jnp.int32, (2 * CHUNK, CHUNK), 0)
        target = lax.broadcasted_iota(jnp.int32, (2 * CHUNK, CHUNK), 1)
        head = first + 2 * pair + lax.rem(channel // 64, 2)
        chosen = head + jnp.where(channel < CHUNK, 0, CHUNK // 2) == target
        flows[...] += dot_exact(
            jnp.concatenate([taken, given], axis=1), chosen.astype(jnp.bfloat16)
        )
        grad_xconv = grad_mixed * skip_row[:, cols] + grad_values
        grad_pre = grad_xconv * (sigma * (1.0 + pre * (1.0 - sigma)))
        tap_grads, bias_grad, grad_raw = conv_backward(
            grad_pre, lines, conv_inner[:, cols], keeps
        )
        sums[2:3, cols] = bias_grad
        sums[3:7, cols] = tap_grads
        grad_raw = grad_raw.astype(jnp.bfloat16)
        grad_inner[:, cols] = grad_raw
        both[:, TILE + pair * CHUNK : TILE + (pair + 1) * CHUNK] = grad_raw

    def compute(slot, at):
        held[slot, at, :] = dot(lines_in[at, :], both[...])

    fetch.wait()
    store_flow(
        held,
        sems,
        tile,
        FLOWS,
        compute,
        (keep_one, keep_two, keep_three),
        (send_one, send_two, send_three),
    )


def backward(
    lengths,
    skip,
    row_sums,
    came,
    cotangent,
    proj_out,
    gains,
    gate_raw,
    mixed,
    inner_raw,
    conv_inner,
    maps,
    step_pre,
    cumul,
    arranged,
    after,
    origin,
    inner_total,
):
    tiles = FLOWS
    rows, width = cotangent.shape
    taps = conv_inner.shape[0]
    states = maps.shape[1]
    f32, bf16 = jnp.float32, jnp.bfloat16
    smem = pl.BlockSpec(memory_space=pltpu.SMEM)

    def whole(*shape):
        return pl.BlockSpec(shape, fixed)

    def strip(count):
        return pl.BlockSpec((count, TILE), lambda tile: (0, tile + origin))

    return pl.pallas_call(
        functools.partial(backward_kernel, origin=origin, inner_total=inner_total),
        grid=(tiles,),
        in_specs=[
            smem,
            smem,
            whole(8, rows),
            whole(8, rows),
            whole(rows, width),
            pl.BlockSpec((TILE, width), lambda tile: (tile + origin, 0)),
            strip(8),
            strip(rows),
            strip(rows),
            strip(rows),
            strip(taps),
            whole(rows, states),
            whole(rows, CHUNK),
            whole(rows, CHUNK),
            pl.BlockSpec(memory_space=pl.ANY),
        ]
        + [pl.BlockSpec(memory_space=pl.ANY)] * len(after),
        out_specs=[
            pl.BlockSpec((rows, TILE), tile_cols),
            pl.BlockSpec((rows, TILE), tile_cols),
            whole(rows, rows),
            whole(rows, CHUNK),
            pl.BlockSpec((8, TILE), tile_cols),
        ]
        + [pl.BlockSpec(memory_space=pl.ANY)] * (2 * FLOWS),
        out_shape=[
            jax.ShapeDtypeStruct((rows, TILE * tiles), bf16),
            jax.ShapeDtypeStruct((rows, TILE * tiles), bf16),
            jax.ShapeDtypeStruct((rows, rows), f32),
            jax.ShapeDtypeStruct((rows, CHUNK), f32),
            jax.ShapeDtypeStruct((8, TILE * tiles), f32),
        ]
        + [jax.ShapeDtypeStruct((width // 2, 2 * TILE), f32)] * (2 * FLOWS),
        scratch_shapes=[
            pltpu.VMEM((rows, width), bf16),
            pltpu.VMEM((rows, CHUNK), f32),
            pltpu.VMEM((taps - 1, rows, CHUNK), f32),
            pltpu.VMEM((rows, rows), f32),
            pltpu.VMEM((CHUNK, rows), f32),
            pltpu.VMEM((rows // CHUNK - 1, CHUNK, rows), f32),
            pltpu.VMEM((rows, CHUNK), f32),
            pltpu.VMEM((rows, CHUNK), f32),
            pltpu.VMEM((2, width, 2 * TILE), f32),
            pltpu.SemaphoreType.DMA((2, 2)),
            pltpu.VMEM((TILE // CHUNK, rows, 2 * rows), bf16),
            pltpu.VMEM((rows, 2 * TILE), bf16),
            pltpu.VMEM((width, rows), bf16),
            pltpu.SemaphoreType.DMA(()),
        ],
        compiler_params=pltpu.CompilerParams(vmem_limit_bytes=LIMIT),
        cost_estimate=cost(
            flops=6 * rows * width * TILE * tiles + 4 * rows * rows * TILE * tiles,
            bytes_accessed=2 * width * TILE * tiles + 20 * rows * TILE * tiles,
            transcendentals=4 * rows * TILE * tiles,
        ),
        name="layer_backward",
    )(
        lengths,
        skip,
        row_sums,
        came,
        cotangent,
        proj_out,
        gains,
        gate_raw,
        mixed,
        inner_raw,
        conv_inner,
        maps,
        step_pre,
        cumul,
        arranged,
        *after,
    )


def scan_kernel(
    lengths,
    core,
    scores_one,
    scores_two,
    flows_one,
    flows_two,
    maps,
    step_pre,
    decay_log,
    *rest,
):
    own, other, grad_step, sums, rates = rest[-5:]
    rows = maps.shape[0]
    states = maps.shape[1] // 2
    heads = decay_log.shape[1]
    grad_scores = (scores_one[...] + scores_two[...]) * same_sequence(rows, ends_of(lengths), 1)
    grad_input = dot_exact(grad_scores, maps[:, states:])
    grad_output = dot_exact(grad_scores, maps[:, :states], dot_first)
    first = core[0] == 0
    own[...] = jnp.where(first, grad_input, grad_output)
    other[...] = jnp.where(first, grad_output, grad_input)
    pre = step_pre[...]
    steps = softplus(pre)
    rates[...] = jnp.zeros(rates.shape, jnp.float32)
    rates[0:1, :heads] = -jnp.exp(decay_log[...])
    rate = rates[0:1, :]
    flows = flows_one[...] + flows_two[...]
    lane = lax.broadcasted_iota(jnp.int32, flows.shape, 1)
    taken = jnp.where(lane < CHUNK // 2, flows, 0.0)
    grad_cum = jnp.where(lane < CHUNK // 2, pltpu.roll(flows, CHUNK // 2, 1) - flows, 0.0)
    later = lax.broadcasted_iota(jnp.int32, (rows, rows), 0) <= lax.broadcasted_iota(
        jnp.int32, (rows, rows), 1
    )
    grad_rate = dot_exact(later.astype(jnp.bfloat16), grad_cum)
    sigma = jax.nn.sigmoid(pre)
    share = jnp.where(pre < -30.0, 1.0, sigma / jnp.maximum(steps, 1e-30))
    grad_pre = taken * share + grad_rate * rate * sigma
    grad_step[...] = grad_pre.astype(jnp.bfloat16)
    sums[...] = jnp.zeros(sums.shape, jnp.float32)
    sums[0:1, :] = jnp.sum(grad_pre, axis=0, keepdims=True)
    sums[1:2, :] = jnp.sum(grad_rate * steps, axis=0, keepdims=True) * rate


def scan_gradients(lengths, core, one, two, maps, step_pre, decay_log, after):
    rows = maps.shape[0]
    states = maps.shape[1] // 2
    vmem = pl.BlockSpec(memory_space=pltpu.VMEM)
    smem = pl.BlockSpec(memory_space=pltpu.SMEM)
    return pl.pallas_call(
        scan_kernel,
        in_specs=[smem, smem] + [vmem] * 7 + [pl.BlockSpec(memory_space=pl.ANY)] * len(after),
        out_specs=[vmem] * 4,
        out_shape=[
            jax.ShapeDtypeStruct((rows, states), jnp.float32),
            jax.ShapeDtypeStruct((rows, states), jnp.float32),
            jax.ShapeDtypeStruct((rows, CHUNK), jnp.bfloat16),
            jax.ShapeDtypeStruct((8, CHUNK), jnp.float32),
        ],
        scratch_shapes=[pltpu.VMEM((8, CHUNK), jnp.float32)],
        compiler_params=pltpu.CompilerParams(vmem_limit_bytes=LIMIT),
        cost_estimate=cost(
            flops=36 * rows * rows * states, bytes_accessed=16 * rows * rows, transcendentals=0
        ),
        name="scan_gradients",
    )(lengths, core, one[0], two[0], one[1], two[1], maps, step_pre, decay_log, *after)


def state_kernel(
    lengths,
    core,
    own,
    came,
    state_raw,
    state_pre,
    conv_state,
    grad_step,
    arranged,
    grad_state,
    sums,
    send_state,
    send_step,
    keep_state,
    keep_step,
    keeps,
):
    flow = pl.program_id(0)
    half = arranged.shape[1] // 2

    @pl.when(flow == 0)
    def _():
        fill_keeps(keeps, ends_of(lengths))
        cols = own.shape[1]
        first = core[0] == 0
        pre = jnp.where(first, state_pre[:, :cols], state_pre[:, cols:])
        raw = jnp.where(first, state_raw[:, :cols], state_raw[:, cols:])
        taps = jnp.where(first, conv_state[:, :cols], conv_state[:, cols:])
        sigma = jax.nn.sigmoid(pre)
        grad_pre = (own[...] + came[...]) * (sigma * (1.0 + pre * (1.0 - sigma)))
        tap_grads, bias_grad, grad_raw = conv_backward(
            grad_pre, lagged_rows(raw, keeps), taps, keeps
        )
        grad_state[...] = grad_raw.astype(jnp.bfloat16)
        sums[...] = jnp.zeros(sums.shape, jnp.float32)
        sums[0:1, :] = bias_grad
        sums[1:5, :] = tap_grads
        send_state[...] = dot(arranged[0, half:], grad_state[...])
        keep_state[...] = dot(arranged[0, :half], grad_state[...])

    @pl.when(flow == 1)
    def _():
        send_step[...] = dot(arranged[0, half:], grad_step[...])
        keep_step[...] = dot(arranged[0, :half], grad_step[...])


def state_gradients(lengths, core, own, came, state_raw, state_pre, conv_state, grad_step, arranged):
    rows, cols = own.shape
    _, width, _ = arranged.shape
    smem = pl.BlockSpec(memory_space=pltpu.SMEM)

    def whole(values):
        return pl.BlockSpec(values.shape, lambda flow: (0, 0))

    half = jax.ShapeDtypeStruct((width // 2, CHUNK), jnp.float32)
    outs = [
        jax.ShapeDtypeStruct((rows, cols), jnp.bfloat16),
        jax.ShapeDtypeStruct((8, cols), jnp.float32),
        half,
        half,
        half,
        half,
    ]
    return pl.pallas_call(
        state_kernel,
        grid=(2,),
        in_specs=[smem, smem]
        + [whole(part) for part in (own, came, state_raw, state_pre, conv_state, grad_step)]
        + [pl.BlockSpec((1, width, rows), lambda flow: (flow, 0, 0))],
        out_specs=[whole(part) for part in outs],
        out_shape=outs,
        scratch_shapes=[pltpu.VMEM((conv_state.shape[0] - 1, rows, CHUNK), jnp.float32)],
        compiler_params=pltpu.CompilerParams(vmem_limit_bytes=LIMIT),
        cost_estimate=cost(
            flops=40 * rows * cols, bytes_accessed=24 * rows * cols, transcendentals=rows * cols
        ),
        name="state_gradients",
    )(lengths, core, own, came, state_raw, state_pre, conv_state, grad_step, arranged)


def add_rows_kernel(*refs, shapes, outs):
    at = 0
    for flow, (joined, counts) in enumerate(shapes):
        wides = refs[at : at + joined]
        at += joined
        out = refs[len(refs) - outs + (flow if outs > 1 else 0)]
        base = sum(cols for before in shapes[:flow] for _, cols in before[1]) if outs == 1 else 0
        start = 0
        for count, cols in counts:
            total = refs[at][...]
            for more in range(1, count):
                total = total + refs[at + more][...]
            for wide_ref in wides:
                if start + cols <= wide_ref.shape[1]:
                    total = total + wide_ref[:, start : start + cols]
            out[:, base + start : base + start + cols] = total
            at += count
            start += cols


def add_rows(flows, start, rows, after=None, together=False):
    parts = 4 if rows >= 192 else 1
    block = rows // parts
    shapes, flat = [], []
    for joined, groups in flows:
        shapes.append((len(joined), tuple((len(group), group[0].shape[1]) for group in groups)))
        flat += list(joined) + [part for group in groups for part in group]
    in_specs = [
        pl.BlockSpec((block, part.shape[1]), lambda part: (start // block + part, 0))
        for part in flat
    ]
    widths = [sum(cols for _, cols in counts) for _, counts in shapes]
    if together:
        widths = [sum(widths)]
    if after is not None:
        flat.append(after)
        in_specs.append(pl.BlockSpec(memory_space=pl.ANY))
    return pl.pallas_call(
        functools.partial(add_rows_kernel, shapes=tuple(shapes), outs=len(widths)),
        grid=(parts,),
        in_specs=in_specs,
        out_specs=[pl.BlockSpec((block, cols), lambda part: (part, 0)) for cols in widths],
        out_shape=[jax.ShapeDtypeStruct((rows, cols), jnp.float32) for cols in widths],
        compiler_params=pltpu.CompilerParams(vmem_limit_bytes=LIMIT),
        cost_estimate=cost(
            flops=rows * sum(widths), bytes_accessed=16 * rows * sum(widths), transcendentals=0
        ),
        name="add_rows",
    )(*flat)


def spread_kernel(one, two, state, head, own, came, *rest):
    out = rest[len(rest) // 2]
    half = one.shape[1]
    width = 2 * half
    for member in range(out.shape[0]):
        out[member, :, :half] = one[...]
        out[member, :, half:width] = two[...]
        out[member, :, width : width + CHUNK] = state[...]
        out[member, :, width + CHUNK :] = head[...]
        out[member, 7:8, :width] = own[...] + came[...]


def spread(one, two, state, head, own, came, members, held_back):
    vmem = pl.BlockSpec(memory_space=pltpu.VMEM)
    shape = (members, 8, 2 * one.shape[1] + 2 * CHUNK)
    return pl.pallas_call(
        spread_kernel,
        in_specs=[vmem] * 6 + [pl.BlockSpec(memory_space=pl.ANY)] * len(held_back),
        out_specs=[vmem] + [pl.BlockSpec(memory_space=pl.ANY)] * len(held_back),
        out_shape=[
            jax.ShapeDtypeStruct(shape, jnp.float32),
        ]
        + [jax.ShapeDtypeStruct(part.shape, part.dtype) for part in held_back],
        input_output_aliases={6 + at: 1 + at for at in range(len(held_back))},
        compiler_params=pltpu.CompilerParams(vmem_limit_bytes=LIMIT),
        cost_estimate=cost(flops=8 * shape[2], bytes_accessed=4 * 64 * shape[2], transcendentals=0),
        name="spread",
    )(one, two, state, head, own, came, *held_back)


def late_sums(refs, count, more):
    flows = [refs[flow * (2 + more) : (flow + 1) * (2 + more)] for flow in range(FLOWS)]
    totals = []
    for terms in flows:
        total = terms[0][...]
        for term in terms[1:]:
            total = total + term[...]
        totals.append(total)
    small, lines = refs[count], refs[count + 1 : count + 1 + 2 * more]
    total = small[0]
    for member in range(1, small.shape[0]):
        total = total + small[member]
    for upper, lower in zip(lines[::2], lines[1::2]):
        cols = upper.shape[1]
        total = total + jnp.concatenate([upper[...], lower[:, : total.shape[1] - cols]], axis=1)
    return totals, total


def late_specs(stays, came, later, small, rows, index, after=None):
    flat = []
    for flow in range(FLOWS):
        flat += [stays[flow], came[flow]] + [parts[flow] for parts in later]
    specs = [pl.BlockSpec((rows, part.shape[1]), lambda _: (index, 0)) for part in flat]
    specs.append(pl.BlockSpec(small.shape, lambda _: (0, 0, 0)))
    for parts in later:
        last = parts[0].shape[0] // 8
        for place in (last - 2, last - 1):
            specs.append(pl.BlockSpec((8, parts[0].shape[1]), lambda _, place=place: (place, 0)))
    flat += [small] + [parts[0] for parts in later for _ in range(2)]
    if after is not None:
        flat.append(after)
        specs.append(pl.BlockSpec(memory_space=pl.ANY))
    return flat, specs


def go_kernel(*refs, count, more):
    outs = refs[-FLOWS:]
    totals, small = late_sums(refs, count, more)
    for flow, total in enumerate(totals):
        rows, cols = total.shape
        outs[flow][:rows, :] = total
        if flow == 0:
            outs[0][rows : rows + 8, :] = small[:, :cols]
            outs[0][rows + 8 :, : small.shape[1] - cols] = small[:, cols:]
            outs[0][rows + 8 :, small.shape[1] - cols :] = jnp.zeros(
                (8, 2 * cols - small.shape[1]), jnp.float32
            )


def go_rows(stays, came, later, small, rows, after):
    flat, specs = late_specs(stays, came, later, small, rows, 1, after)
    shapes = [
        (rows + (16 if flow == 0 else 0), stays[flow].shape[1]) for flow in range(FLOWS)
    ]
    return pl.pallas_call(
        functools.partial(go_kernel, count=FLOWS * (2 + len(later)), more=len(later)),
        grid=(1,),
        in_specs=specs,
        out_specs=[pl.BlockSpec(shape, fixed) for shape in shapes],
        out_shape=[jax.ShapeDtypeStruct(shape, jnp.float32) for shape in shapes],
        compiler_params=pltpu.CompilerParams(vmem_limit_bytes=LIMIT),
        cost_estimate=cost(flops=rows, bytes_accessed=rows, transcendentals=0),
        name="go_rows",
    )(*flat)


def last_rows_kernel(*refs, count, more):
    totals, sums = late_sums(refs, count, more)
    (
        out_grad_out,
        out_gate,
        out_inner,
        out_state,
        out_step,
        out_norm_in,
        out_conv_inner,
        out_bias_inner,
        out_conv_state,
        out_bias_state,
        out_step_bias,
        out_decay,
        out_skip,
        out_norm_out,
    ) = refs[-14:]
    share = out_grad_out.shape[1] // FLOWS
    for flow, total in enumerate(totals):
        out_grad_out[:, flow * share : (flow + 1) * share] = total[:, :share]
        start = share
        for group in range(2):
            first = (group * FLOWS + flow) * TILE
            out_gate[:, first : first + TILE] = total[:, start : start + TILE]
            out_inner[:, first : first + TILE] = total[:, start + TILE : start + 2 * TILE]
            start += 2 * TILE
        if flow < 2:
            side = (out_state, out_step)[flow]
            side[...] = total[:, start : start + side.shape[1]]
    inner = out_gate.shape[1]
    for out, row in ((out_norm_out, 0), (out_bias_inner, 2), (out_norm_in, 7)):
        for part in range(out.shape[0]):
            out[part : part + 1, :] = sums[row : row + 1, part * CHUNK : (part + 1) * CHUNK]
    out_conv_inner[...] = sums[3:7, :inner]
    out_bias_state[...] = sums[0:1, inner : inner + CHUNK]
    out_conv_state[...] = sums[1:5, inner : inner + CHUNK]
    heads = out_skip.shape[1]
    out_step_bias[...] = sums[0:1, inner + CHUNK : inner + CHUNK + heads]
    out_decay[...] = sums[1:2, inner + CHUNK : inner + CHUNK + heads]
    channel = lax.broadcasted_iota(jnp.int32, (inner, CHUNK), 0)
    target = lax.broadcasted_iota(jnp.int32, (inner, CHUNK), 1)
    by_head_sums = dot_exact(sums[:, :inner], (channel // 64 == target).astype(jnp.bfloat16))
    out_skip[...] = by_head_sums[1:2, :heads]


def last_rows(stays, came, later, small, rows, inner, states, heads, taps):
    flat, specs = late_specs(stays, came, later, small, rows, 0)
    vector = (inner // CHUNK, CHUNK)
    outs = [(rows, inner), (rows, inner), (rows, inner), (rows, states), (rows, heads)]
    outs += [vector, (taps, inner), vector, (taps, states), (1, states)]
    outs += [(1, heads), (1, heads), (1, heads), vector]
    return pl.pallas_call(
        functools.partial(last_rows_kernel, count=FLOWS * (2 + len(later)), more=len(later)),
        grid=(1,),
        in_specs=specs,
        out_specs=[pl.BlockSpec(shape, fixed) for shape in outs],
        out_shape=[jax.ShapeDtypeStruct(shape, jnp.float32) for shape in outs],
        compiler_params=pltpu.CompilerParams(vmem_limit_bytes=LIMIT),
        cost_estimate=cost(
            flops=8 * rows * inner, bytes_accessed=80 * rows * inner, transcendentals=0
        ),
        name="last_rows",
    )(*flat)


def normed_grad_kernel(
    core, gate_one, inner_one, gate_two, inner_two, state, step, gate, inner, proj_state, proj_step, tokens, rstd_in, *rest
):
    out, norm_row = rest[-2:]
    tile = pl.program_id(0)
    half = gate_one.shape[1]
    states = state.shape[1]
    heads = proj_step.shape[0]
    total = dot_last(gate_one[...], gate[:, :half]) + dot_last(inner_one[...], inner[:, :half])
    total = total + dot_last(gate_two[...], gate[:, half:]) + dot_last(inner_two[...], inner[:, half:])
    chosen = jnp.where(core[0] == 0, proj_state[:, :states], proj_state[:, states:])
    total = total + dot_last(state[...], chosen) + dot(step[:, :heads], proj_step[...])
    out[...] = total
    scaled = total * tokens[...].astype(jnp.float32) * wide(rstd_in[...], TILE)
    here = pl.ds(pl.multiple_of(tile * TILE, TILE), TILE)
    norm_row[0:1, here] = jnp.sum(scaled, axis=0, keepdims=True)


def normed_grad(
    core, one, two, state, step, proj_gate, proj_inner, proj_state, proj_step, tokens, rstd_in, after
):
    rows = state.shape[0]
    width, inner = proj_gate.shape

    def whole(values):
        return pl.BlockSpec(values.shape, fixed)

    def lines(values):
        return pl.BlockSpec((TILE, values.shape[1]), lambda tile: (tile, 0))

    return pl.pallas_call(
        normed_grad_kernel,
        grid=(width // TILE,),
        in_specs=[pl.BlockSpec(memory_space=pltpu.SMEM)]
        + [whole(part) for part in (*one, *two, state, step)]
        + [lines(proj_gate), lines(proj_inner), lines(proj_state)]
        + [pl.BlockSpec((proj_step.shape[0], TILE), tile_cols)]
        + [pl.BlockSpec((rows, TILE), tile_cols), whole(rstd_in)]
        + [pl.BlockSpec(memory_space=pl.ANY)] * len(after),
        out_specs=[pl.BlockSpec((rows, TILE), tile_cols), pl.BlockSpec((1, width), fixed)],
        out_shape=[
            jax.ShapeDtypeStruct((rows, width), jnp.float32),
            jax.ShapeDtypeStruct((1, width), jnp.float32),
        ],
        compiler_params=pltpu.CompilerParams(vmem_limit_bytes=LIMIT),
        cost_estimate=cost(
            flops=4 * rows * inner * width,
            bytes_accessed=4 * inner * width + 8 * rows * width,
            transcendentals=0,
        ),
        name="normed_grad",
    )(
        core,
        *one,
        *two,
        state,
        step,
        proj_gate,
        proj_inner,
        proj_state,
        proj_step,
        tokens,
        rstd_in,
        *after,
    )


def tokens_grad_kernel(
    own, came, tokens, cotangent, gains, grad_tokens
):
    hidden = tokens[...].astype(jnp.float32)
    rstd = lax.rsqrt(jnp.mean(hidden * hidden, axis=1, keepdims=True) + EPS)
    grad_normed = own[...] + came[...]
    weighted = grad_normed * gains[2:3, :]
    back = jnp.mean(weighted * hidden, axis=1, keepdims=True)
    grad_hidden = rstd * weighted - hidden * (rstd * rstd * rstd * back)
    grad_tokens[...] = (cotangent[...].astype(jnp.float32) + grad_hidden).astype(jnp.bfloat16)


def tokens_grad(own, came, tokens, cotangent, gains):
    rows, width = tokens.shape
    lines = pl.BlockSpec((CHUNK, width), lambda step: (step, 0))

    return pl.pallas_call(
        tokens_grad_kernel,
        grid=(rows // CHUNK,),
        in_specs=[lines] * 4 + [pl.BlockSpec(gains.shape, fixed)],
        out_specs=lines,
        out_shape=jax.ShapeDtypeStruct((rows, width), jnp.bfloat16),
        compiler_params=pltpu.CompilerParams(vmem_limit_bytes=LIMIT),
        cost_estimate=cost(
            flops=12 * rows * width, bytes_accessed=14 * rows * width, transcendentals=0
        ),
        name="tokens_grad",
    )(own, came, tokens, cotangent, gains)


def block_out_kernel(
    lengths, row_sums, row_came, own, came, tokens, out, cols, *, inner_total
):
    step = pl.program_id(0)

    @pl.when(step == 0)
    def _():
        rstd, valid = scale_row(row_sums, row_came, lengths, inner_total)
        cols[...] = jnp.broadcast_to(rstd * valid, (CHUNK, rstd.shape[1])).T

    scale = cols[pl.ds(pl.multiple_of(step * CHUNK, CHUNK), CHUNK), 0:1]
    out[...] = (tokens[...].astype(jnp.float32) + scale * (own[...] + came[...])).astype(
        jnp.bfloat16
    )


def finish_block(lengths, row_sums, row_came, own, came, tokens, inner_total):
    rows, width = tokens.shape
    lines = pl.BlockSpec((CHUNK, width), lambda step: (step, 0))
    row = pl.BlockSpec((8, rows), fixed)
    return pl.pallas_call(
        functools.partial(block_out_kernel, inner_total=inner_total),
        grid=(rows // CHUNK,),
        in_specs=[pl.BlockSpec(memory_space=pltpu.SMEM), row, row, lines, lines, lines],
        out_specs=lines,
        out_shape=jax.ShapeDtypeStruct((rows, width), jnp.bfloat16),
        scratch_shapes=[pltpu.VMEM((rows, CHUNK), jnp.float32)],
        compiler_params=pltpu.CompilerParams(vmem_limit_bytes=LIMIT),
        cost_estimate=cost(
            flops=3 * rows * width, bytes_accessed=12 * rows * width, transcendentals=0
        ),
        name="block_out",
    )(lengths, row_sums, row_came, own, came, tokens)


def pass_on(part, flow, step):
    return lax.ppermute(part, ("dp", "tensor"), flow_pairs(flow, step))


def local(
    tokens,
    seq_lengths,
    norm_in,
    proj_gate,
    proj_inner,
    proj_state,
    proj_step,
    conv_inner,
    bias_inner,
    conv_state,
    bias_state,
    step_bias,
    decay_log,
    skip_gain,
    norm_out,
    proj_out,
    cotangent,
):
    width = tokens.shape[1]
    row_count = tokens.shape[0]
    heads_local = proj_step.shape[1]
    inner_local = proj_inner.shape[1]
    state_size = proj_state.shape[1] // 2
    tensor_count = lax.axis_size("tensor")
    inner_total = inner_local * tensor_count
    core = lax.axis_index("tensor").reshape(1)
    blocks = block_order()
    step_t = proj_step.T
    (
        normed,
        gate_raw,
        inner_raw,
        mixed,
        scaled_in,
        partial_value,
        row_sums,
        state_raw,
        state_pre,
        maps,
        step_pre,
        cumul,
        gains,
        rstd_in,
    ) = forward(
        seq_lengths,
        skip_gain,
        tokens,
        norm_in.reshape(-1, CHUNK),
        bias_inner.reshape(-1, CHUNK),
        norm_out.reshape(-1, CHUNK),
        proj_gate,
        proj_inner,
        proj_state,
        step_t,
        conv_inner,
        conv_state,
        bias_state[None, :],
        step_bias[None, :],
        decay_log[None, :],
        proj_out,
        cotangent,
    )
    row_came = swap_tensor(row_sums)
    arranged, *out_halves = out_grad(
        seq_lengths, blocks, row_sums, row_came, cotangent, scaled_in, normed, inner_total
    )

    def first_halving(outs):
        keeps, sends = outs[: len(outs) // 2], outs[len(outs) // 2 :]
        return [[kept, pass_on(sent, flow, 0)] for flow, (kept, sent) in enumerate(zip(keeps, sends))]

    flows_out = first_halving(out_halves)

    def run_backward(origin, after):
        return backward(
            seq_lengths,
            skip_gain,
            row_sums,
            row_came,
            cotangent,
            proj_out,
            gains,
            gate_raw,
            mixed,
            inner_raw,
            conv_inner,
            maps,
            step_pre,
            cumul,
            arranged,
            after,
            origin,
            inner_total,
        )

    one = run_backward(0, out_halves[:1])
    flows_one = first_halving(one[5:])
    two = run_backward(FLOWS, [one[5]] + [terms[1] for terms in flows_out])
    flows_two = first_halving(two[5:])
    own, other, grad_step_raw, head_sums = scan_gradients(
        seq_lengths,
        core,
        one[2:4],
        two[2:4],
        maps,
        step_pre,
        decay_log[None, :],
        [terms[1] for terms in flows_one],
    )
    grad_state_part, state_sums, *side_halves = state_gradients(
        seq_lengths,
        core,
        own,
        swap_tensor(other),
        state_raw,
        state_pre,
        conv_state,
        grad_step_raw,
        arranged,
    )
    flows_side = first_halving(side_halves[2:] + side_halves[:2])
    side_flows = len(flows_side)

    rows = width // 4
    groups = [[flows_out[flow], flows_one[flow], flows_two[flow]] for flow in range(FLOWS)]
    for flow in range(side_flows):
        groups[flow].append(flows_side[flow])
    goes = add_rows([([], group) for group in groups], rows, rows)
    came = [pass_on(go, flow, 1) for flow, go in enumerate(goes)]
    stays = add_rows([([], group) for group in groups], 0, rows, goes[0])
    grad_normed, norm_row = normed_grad(
        core,
        one[:2],
        two[:2],
        grad_state_part,
        grad_step_raw,
        proj_gate,
        proj_inner,
        proj_state,
        step_t,
        tokens,
        rstd_in,
        [goes[0]],
    )
    members = 1 << HALVINGS
    spread_sums, grad_normed, partial_late = spread(
        one[4],
        two[4],
        state_sums,
        head_sums,
        norm_row,
        swap_tensor(norm_row),
        members,
        (grad_normed, partial_value),
    )
    grad_tokens = tokens_grad(grad_normed, swap_tensor(grad_normed), tokens, cotangent, gains)
    small = lax.all_to_all(
        spread_sums,
        ("dp", "tensor"),
        0,
        0,
        axis_index_groups=cube_groups(0, HALVINGS),
    )
    rows = width // 8
    flows = [([], [[stays[flow], came[flow]]]) for flow in range(FLOWS)]
    more = add_rows(flows, rows, rows, spread_sums)
    came_more = [pass_on(go, flow, 2) for flow, go in enumerate(more)]
    stays = add_rows(flows, 0, rows, more[0])
    block_out = finish_block(
        seq_lengths,
        row_sums,
        row_came,
        partial_late,
        swap_tensor(partial_late),
        tokens,
        inner_total,
    )
    later = []
    for step in range(HALVINGS, DIMS):
        rows = width >> (step + 1)
        after = (None, block_out, grad_tokens)[step - HALVINGS]
        goes = go_rows(stays, came_more, later, small, rows, after)
        later.append([pass_on(go, flow, step) for flow, go in enumerate(goes)])
    (
        grad_proj_out,
        grad_proj_gate,
        grad_proj_inner,
        grad_proj_state,
        grad_proj_step,
        grad_norm_in,
        grad_conv_inner,
        grad_bias_inner,
        grad_conv_state,
        grad_bias_state,
        grad_step_bias,
        grad_decay_log,
        grad_skip_gain,
        grad_norm_out,
    ) = last_rows(
        stays,
        came_more,
        later,
        small,
        width // BLOCKS,
        inner_local,
        2 * state_size // tensor_count,
        heads_local,
        conv_inner.shape[0],
    )

    return (
        block_out,
        grad_tokens,
        grad_norm_in.reshape(-1),
        grad_proj_gate,
        grad_proj_inner,
        grad_proj_state,
        grad_proj_step,
        grad_conv_inner,
        grad_bias_inner.reshape(-1),
        grad_conv_state,
        grad_bias_state.reshape(-1),
        grad_step_bias.reshape(-1),
        grad_decay_log.reshape(-1),
        grad_skip_gain.reshape(-1),
        grad_norm_out.reshape(-1),
        grad_proj_out.T,
    )


def solution(mesh):
    return jax.shard_map(
        local,
        mesh=mesh,
        in_specs=(
            P("dp", None),
            P("dp", None),
            P(),
            P(None, "tensor"),
            P(None, "tensor"),
            P(),
            P(None, "tensor"),
            P(None, "tensor"),
            P("tensor"),
            P(),
            P(),
            P("tensor"),
            P("tensor"),
            P("tensor"),
            P("tensor"),
            P("tensor", None),
            P("dp", None),
        ),
        out_specs=(
            P("dp", None),
            P("dp", None),
            P(),
            P("dp", "tensor"),
            P("dp", "tensor"),
            P("dp", "tensor"),
            P("dp", "tensor"),
            P(None, "tensor"),
            P("tensor"),
            P(None, "tensor"),
            P("tensor"),
            P("tensor"),
            P("tensor"),
            P("tensor"),
            P("tensor"),
            P("tensor", "dp"),
        ),
        check_vma=False,
    )
```
